512 devices in a mesh: img: 64 (over x, z_lo, core), blk: 8 (over z_hi, y).
Axes of the slice: x: 4, y: 4, z: 16 (z_hi: 2, z_lo: 8; z = z_hi * 8 + z_lo), core: 2. Of those that a mesh axis runs over, the one named last changes fastest.
Arguments:
- image_embeds: bfloat16 [6144, 1152], P(('img', 'blk')), may hold values from -48 to 48
- text_embeds: bfloat16 [6144, 1152], P(('img', 'blk')), may hold values from -48 to 48
- log_temp: float32 [1], replicated, may hold values from 1 to 2.3
- bias: float32 [1], replicated, may hold values from -3 to -1
Outputs:
- image_grads: float32 [6144, 1152], P(('img', 'blk'))
- text_grads: float32 [6144, 1152], P(('img', 'blk'))
The draws below stay inside these ranges and needn't reach their ends.
All inputs are finite; a program needn't handle non-finite values.
Results may differ from the reference program's by a relative error of at most 0.00145.
Values may be sent and summed in bfloat16 or wider, within the bound.
No kernel may reach another device: no remote copies, remote signals or barrier semaphores. Data moves between devices by JAX's collectives and lax.ppermute only.
A program may use at most 64 MiB of HBM per device.

```python
import math
import jax
import jax.numpy as jnp
from jax import lax

D = 1152
PAIRS = 6144


def common_part(key, strength_low):
    key_topic, key_assign, key_strength, key_shared, key_column = jax.random.split(key, 5)
    topics = 24
    topic_vectors = jax.random.truncated_normal(key_topic, -4.0, 4.0, (topics, D), jnp.float32)
    assigned = jax.random.randint(key_assign, (PAIRS,), 0, topics)
    strength = jax.random.uniform(key_strength, (PAIRS, 1), jnp.float32, strength_low, 1.0)
    shared = jax.random.truncated_normal(key_shared, -4.0, 4.0, (PAIRS, D), jnp.float32)
    column_scale = jnp.exp(jax.random.uniform(key_column, (1, D), jnp.float32, 0.0, math.log(10.0))) / 4.64
    mixed = strength * topic_vectors[assigned] + 0.5 * shared
    return (mixed, column_scale)


def draw_image_embeds(key, part):
    mixed, column_scale = common_part(key, 0.4)
    key = jax.random.fold_in(key, 3)
    key_noise, key_row = jax.random.split(key)
    noise = jax.random.truncated_normal(key_noise, -4.0, 4.0, (PAIRS, D), jnp.float32)
    row_scale = jnp.exp(jax.random.uniform(key_row, (PAIRS, 1), jnp.float32, math.log(0.3), math.log(3.0)))
    values = (mixed + 0.45 * noise) * column_scale * row_scale * 0.6
    return values.astype(jnp.bfloat16)


def draw_text_embeds(key, part):
    mixed, column_scale = common_part(key, 0.4)
    key = jax.random.fold_in(key, 5)
    key_noise, key_row = jax.random.split(key)
    noise = jax.random.truncated_normal(key_noise, -4.0, 4.0, (PAIRS, D), jnp.float32)
    row_scale = jnp.exp(jax.random.uniform(key_row, (PAIRS, 1), jnp.float32, math.log(0.3), math.log(3.0)))
    values = (mixed + 0.45 * noise) * column_scale * row_scale * 0.6
    return values.astype(jnp.bfloat16)


def setup_inputs(seed: int = 0) -> dict:
    splits = jax.random.split(jax.random.key(seed), 5)
    image_embeds = draw_image_embeds(jax.random.fold_in(splits[4], 71), 0)
    text_embeds = draw_text_embeds(jax.random.fold_in(splits[4], 71), 0)
    log_temp = jnp.clip(jax.random.uniform(splits[2], (1,), jnp.float32, 1.0, 2.3), 1.0, 2.3)
    bias = jnp.clip(jax.random.uniform(splits[3], (1,), jnp.float32, -3.0, -1.0), -3.0, -1.0)
    return {"image_embeds": image_embeds, "text_embeds": text_embeds, "log_temp": log_temp, "bias": bias}


EPS = 1e-06

def unit_rows(emb):
    wide = emb.astype(jnp.float32)
    inverse = lax.rsqrt(lax.optimization_barrier(jnp.sum(wide * wide, axis=1, keepdims=True)) + EPS)
    return (wide * inverse, inverse)

def reference(image_embeds, text_embeds, log_temp, bias):
    img_unit, img_inv = unit_rows(image_embeds)
    txt_unit, txt_inv = unit_rows(text_embeds)
    img_half = img_unit.astype(jnp.bfloat16)
    txt_half = txt_unit.astype(jnp.bfloat16)
    scale = jnp.exp(log_temp[0])
    logits = scale * lax.dot_general(img_half, txt_half, (((1,), (1,)), ((), ())), preferred_element_type=jnp.float32) + bias[0]
    count = image_embeds.shape[0]
    same = jnp.arange(count)[:, None] == jnp.arange(count)[None, :]
    coeff = (jnp.where(same, -jax.nn.sigmoid(-logits), jax.nn.sigmoid(logits)) * scale).astype(jnp.bfloat16)
    img_dir = jnp.dot(coeff, txt_half, preferred_element_type=jnp.float32)
    txt_dir = lax.dot_general(coeff, img_half, (((0,), (0,)), ((), ())), preferred_element_type=jnp.float32)
    image_grads = (img_dir - img_unit * lax.optimization_barrier(jnp.sum(img_unit * img_dir, axis=1, keepdims=True))) * img_inv
    text_grads = (txt_dir - txt_unit * lax.optimization_barrier(jnp.sum(txt_unit * txt_dir, axis=1, keepdims=True))) * txt_inv
    return (image_grads, text_grads)
```

```python
import jax
import jax.numpy as jnp
from jax import lax
from jax.sharding import Mesh, PartitionSpec as P

EPS = 1e-06
PAD = 16


def unit_rows(emb):
    wide = emb.astype(jnp.float32)
    inverse = lax.rsqrt(jnp.sum(wide * wide, axis=1, keepdims=True) + EPS)
    return (wide * inverse, inverse)


def finish(direction, unit, inverse):
    return (direction - unit * jnp.sum(unit * direction, axis=1, keepdims=True)) * inverse


def on_device(image_embeds, text_embeds, log_temp, bias):
    rows = image_embeds.shape[0]
    width = image_embeds.shape[1]
    scale = jnp.exp(log_temp[0])
    img_unit, img_inv = unit_rows(image_embeds)
    txt_unit, txt_inv = unit_rows(text_embeds)
    fill = ((0, PAD - rows), (0, 0))
    img_half = jnp.pad(img_unit.astype(jnp.bfloat16), fill)
    txt_half = jnp.pad(txt_unit.astype(jnp.bfloat16), fill)
    plane = ("x", "core", "y")
    n_plane = lax.axis_size(plane)
    here = lax.axis_index(plane)

    steps = (("zh", 1), ("zl", 4), ("zl", 2), ("zl", 1))
    n_line = lax.axis_size("zh") * lax.axis_size("zl")

    def exchange(value, step):
        axis, by = step
        return lax.ppermute(value, axis, [(i, i ^ by) for i in range(lax.axis_size(axis))])

    images = lax.all_gather(img_half, plane, axis=0, tiled=False).reshape(n_plane * PAD, width)
    texts = txt_half
    for step in steps:
        texts = jnp.concatenate([texts, exchange(texts, step)], axis=0)

    logits = (
        scale
        * lax.dot_general(
            images, texts, (((1,), (1,)), ((), ())), preferred_element_type=jnp.float32
        )
        + bias[0]
    )
    row = lax.broadcasted_iota(jnp.int32, logits.shape, 0)
    col = lax.broadcasted_iota(jnp.int32, logits.shape, 1)
    same = row == col + here * PAD
    same = same & (col < PAD)
    coeff = (jnp.where(same, -jax.nn.sigmoid(-logits), jax.nn.sigmoid(logits)) * scale).astype(
        jnp.bfloat16
    )
    img_part = jnp.dot(coeff, texts, preferred_element_type=jnp.float32)
    txt_part = lax.dot_general(
        coeff, images, (((0,), (0,)), ((), ())), preferred_element_type=jnp.float32
    )

    back = lax.all_to_all(
        img_part.astype(jnp.bfloat16).reshape(n_plane, PAD, width), plane, 0, 0, tiled=False
    )
    img_dir = jnp.sum(back.astype(jnp.float32), axis=0)[:rows]

    part = txt_part.reshape(n_line, PAD, width)
    kind = jnp.bfloat16
    for step in reversed(steps):
        half = part.shape[0] // 2
        part = part[:half] + exchange(part[half:].astype(kind), step).astype(jnp.float32)
        kind = jnp.float32
    txt_dir = part[0, :rows]
    return (finish(img_dir, img_unit, img_inv), finish(txt_dir, txt_unit, txt_inv))


def solution(mesh):
    fine = Mesh(mesh.devices.reshape(4, 8, 2, 2, 4), ("x", "zl", "core", "zh", "y"))
    split = P(("x", "zl", "core", "zh", "y"), None)
    return jax.shard_map(
        on_device,
        mesh=fine,
        in_specs=(split, split, P(), P()),
        out_specs=(split, split),
        check_vma=False,
    )
```

```python
import jax
import jax.numpy as jnp
from jax import lax
from jax.sharding import Mesh, PartitionSpec as P

EPS = 1e-06
PAD = 16


def unit_rows(emb):
    wide = emb.astype(jnp.float32)
    inverse = lax.rsqrt(jnp.sum(wide * wide, axis=1, keepdims=True) + EPS)
    return (wide * inverse, inverse)


def finish(direction, unit, inverse):
    return (direction - unit * jnp.sum(unit * direction, axis=1, keepdims=True)) * inverse


def on_device(image_embeds, text_embeds, log_temp, bias):
    rows = image_embeds.shape[0]
    width = image_embeds.shape[1]
    scale = jnp.exp(log_temp[0])
    img_unit, img_inv = unit_rows(image_embeds)
    txt_unit, txt_inv = unit_rows(text_embeds)
    fill = ((0, PAD - rows), (0, 0))
    img_half = jnp.pad(img_unit.astype(jnp.bfloat16), fill)
    txt_half = jnp.pad(txt_unit.astype(jnp.bfloat16), fill)
    plane = ("x", "core", "y")
    here = lax.axis_index(plane)

    line = ("zl", "zh")
    spot = lax.axis_index(line)

    def to_all(block, axes):
        sent = jnp.broadcast_to(block[None], (lax.axis_size(axes),) + block.shape)
        return lax.all_to_all(sent, axes, 0, 0).reshape(-1, width)

    texts = to_all(txt_half, line)
    images = to_all(img_half, plane)

    logits = (
        scale
        * lax.dot_general(
            images, texts, (((1,), (1,)), ((), ())), preferred_element_type=jnp.float32
        )
        + bias[0]
    )
    row = lax.broadcasted_iota(jnp.int32, logits.shape, 0)
    col = lax.broadcasted_iota(jnp.int32, logits.shape, 1)
    same = (row - here * PAD == col - spot * PAD) & (row // PAD == here)
    coeff = (jnp.where(same, -jax.nn.sigmoid(-logits), jax.nn.sigmoid(logits)) * scale).astype(
        jnp.bfloat16
    )
    img_part = jnp.dot(coeff, texts, preferred_element_type=jnp.float32)
    txt_part = lax.dot_general(
        coeff, images, (((0,), (0,)), ((), ())), preferred_element_type=jnp.float32
    )

    def to_owners(part, axes):
        sent = part.astype(jnp.bfloat16).reshape(-1, PAD, width)
        back = lax.all_to_all(sent, axes, 0, 0)
        return jnp.sum(back.astype(jnp.float32), axis=0)[:rows]

    txt_dir = to_owners(txt_part, line)
    img_dir = to_owners(img_part, plane)
    return (finish(img_dir, img_unit, img_inv), finish(txt_dir, txt_unit, txt_inv))


def solution(mesh):
    fine = Mesh(mesh.devices.reshape(4, 8, 2, 2, 4), ("x", "zl", "core", "zh", "y"))
    split = P(("x", "zl", "core", "zh", "y"), None)
    return jax.shard_map(
        on_device,
        mesh=fine,
        in_specs=(split, split, P(), P()),
        out_specs=(split, split),
        check_vma=False,
    )
```

```python
import jax
import jax.numpy as jnp
from jax import lax
from jax.sharding import Mesh, PartitionSpec as P

EPS = 1e-06
PAD = 16
LINE = ("zl", "zh")
PLANE = ("x", "core", "y")
FAR = (4, 8, 12)
NEAR = (1, 2, 15)


def unit_rows(emb):
    wide = emb.astype(jnp.float32)
    inverse = lax.rsqrt(jnp.sum(wide * wide, axis=1, keepdims=True) + EPS)
    return (wide * inverse, inverse)


def finish(direction, unit, inverse):
    return (direction - unit * jnp.sum(unit * direction, axis=1, keepdims=True)) * inverse


def along_z(value, by):
    def place(z):
        return (z % 8) * 2 + z // 8

    return lax.ppermute(value, LINE, [(place(z), place((z + by) % 16)) for z in range(16)])


def on_device(image_embeds, text_embeds, log_temp, bias):
    rows = image_embeds.shape[0]
    width = image_embeds.shape[1]
    scale = jnp.exp(log_temp[0])
    fill = ((0, PAD - rows), (0, 0))
    txt_unit, txt_inv = unit_rows(text_embeds)
    txt_half = jnp.pad(txt_unit.astype(jnp.bfloat16), fill)[None]
    img_unit, img_inv = unit_rows(image_embeds)
    img_half = jnp.pad(img_unit.astype(jnp.bfloat16), fill)
    here = lax.axis_index(PLANE)
    peers = lax.axis_size(PLANE)

    column = jnp.concatenate([txt_half] + [along_z(txt_half, by) for by in FAR], axis=0)
    images = lax.all_to_all(
        jnp.broadcast_to(img_half[None], (peers,) + img_half.shape), PLANE, 0, 0
    ).reshape(-1, width)
    texts = jnp.concatenate([column] + [along_z(column, by) for by in NEAR], axis=0).reshape(
        -1, width
    )

    logits = (
        scale
        * lax.dot_general(
            images, texts, (((1,), (1,)), ((), ())), preferred_element_type=jnp.float32
        )
        + bias[0]
    )
    row = lax.broadcasted_iota(jnp.int32, logits.shape, 0)
    col = lax.broadcasted_iota(jnp.int32, logits.shape, 1)
    same = (row - here * PAD == col) & (col < PAD)
    coeff = (jnp.where(same, -jax.nn.sigmoid(-logits), jax.nn.sigmoid(logits)) * scale).astype(
        jnp.bfloat16
    )
    txt_part = lax.dot_general(
        coeff, images, (((0,), (0,)), ((), ())), preferred_element_type=jnp.float32
    ).reshape(4, 4, PAD, width)
    img_part = jnp.dot(coeff, texts, preferred_element_type=jnp.float32)

    column = txt_part[0]
    for slot, by in enumerate(NEAR):
        column = column + along_z(txt_part[slot + 1].astype(jnp.bfloat16), 16 - by).astype(
            jnp.float32
        )
    sent = img_part.astype(jnp.bfloat16).reshape(peers, PAD, width)
    back = lax.all_to_all(sent, PLANE, 0, 0)
    txt_dir = column[0]
    for slot, by in enumerate(FAR):
        txt_dir = txt_dir + along_z(column[slot + 1], 16 - by)
    img_dir = jnp.sum(back.astype(jnp.float32), axis=0)
    return (
        finish(img_dir[:rows], img_unit, img_inv),
        finish(txt_dir[:rows], txt_unit, txt_inv),
    )


def solution(mesh):
    fine = Mesh(mesh.devices.reshape(4, 8, 2, 2, 4), ("x", "zl", "core", "zh", "y"))
    split = P(("x", "zl", "core", "zh", "y"), None)
    return jax.shard_map(
        on_device,
        mesh=fine,
        in_specs=(split, split, P(), P()),
        out_specs=(split, split),
        check_vma=False,
    )
```

```python
import functools

import jax
import jax.numpy as jnp
from jax import lax
from jax.experimental import pallas as pl
from jax.experimental.pallas import tpu as pltpu
from jax.sharding import Mesh, PartitionSpec as P

EPS = 1e-06
AXES = ("x", "zm", "zn", "core", "zh", "y")
SIZES = (4, 2, 4, 2, 2, 4)
PLANE = ("x", "core", "y")
FAR = ("zm", "zh")
LINE = ("zm", "zn", "zh")
VMEM = 48 * 1024 * 1024

ROWS = 12
WIDTH = 1152
TALL = 16
MAIN = 896
REST = WIDTH - MAIN
STEP = TALL - ROWS
PIECES = [
    (
        slice(m * STEP, (m + 1) * STEP),
        slice(g * 128, (g + 1) * 128),
        slice((3 * g + m) * 128, (3 * g + m + 1) * 128),
    )
    for g in range(REST // 128)
    for m in range(ROWS // STEP)
]


def unit_rows(emb):
    wide = emb.astype(jnp.float32)
    inverse = lax.rsqrt(jnp.sum(wide * wide, axis=1, keepdims=True) + EPS)
    return (wide * inverse, inverse)


def spread_kernel(emb_ref, out_ref, block):
    unit, _ = unit_rows(emb_ref[...])
    block[:ROWS, :] = unit[:, :MAIN]
    block[ROWS:, :] = jnp.zeros((STEP, MAIN), jnp.float32)
    for rows, cols, place in PIECES:
        block[ROWS:, place] = unit[rows, MAIN + cols.start : MAIN + cols.stop]
    out_ref[...] = jnp.broadcast_to(block[...].astype(jnp.bfloat16)[None], out_ref.shape)


def spread(emb, peers):
    return pl.pallas_call(
        spread_kernel,
        out_shape=jax.ShapeDtypeStruct((peers, TALL, MAIN), jnp.bfloat16),
        scratch_shapes=[pltpu.VMEM((TALL, MAIN), jnp.float32)],
        compiler_params=pltpu.CompilerParams(vmem_limit_bytes=VMEM),
        cost_estimate=pl.CostEstimate(flops=100_000, bytes_accessed=1_000_000, transcendentals=0),
    )(emb)


def pair_kernel(
    temp_ref,
    bias_ref,
    place_ref,
    images_ref,
    own_ref,
    *refs,
):
    near_refs = refs[:3]
    image_out, own_out = refs[3:5]
    near_outs = refs[5:8]
    images, texts, rest, main = refs[8:]
    n_images = images_ref.shape[0]
    n_texts = own_ref.shape[0]
    groups = [(images, 0, images_ref)]
    groups += [(texts, i * n_texts, ref) for i, ref in enumerate((own_ref,) + near_refs)]
    rest[:, ROWS:, :] = jnp.zeros((n_images, STEP, REST), jnp.float32)
    for whole, first, ref in groups:
        n = ref.shape[0]
        span = pl.ds(first * TALL, n * TALL)
        whole[span, :MAIN] = ref[...].reshape(n * TALL, MAIN)
        for rows, cols, place in PIECES:
            rest[:n, rows, cols] = ref[:, ROWS:, place].astype(jnp.float32)
        whole[span, MAIN:] = rest[:n].reshape(n * TALL, REST).astype(jnp.bfloat16)

    scale = jnp.exp(jnp.full((1, 1), temp_ref[0], jnp.float32))
    logits = (
        scale
        * lax.dot_general(
            images[...], texts[...], (((1,), (1,)), ((), ())), preferred_element_type=jnp.float32
        )
        + bias_ref[0]
    )
    row = lax.broadcasted_iota(jnp.int32, logits.shape, 0)
    col = lax.broadcasted_iota(jnp.int32, logits.shape, 1)
    row_in, col_in = row % TALL, col % TALL
    real = (row_in < ROWS) & (col_in < ROWS)
    same = (row - place_ref[0] * TALL == row_in) & (col - place_ref[1] * TALL == col_in)
    same = same & (row_in == col_in)
    sig = jax.nn.sigmoid(jnp.where(same, -logits, logits))
    coeff = jnp.where(real, jnp.where(same, -sig, sig) * scale, 0.0).astype(jnp.bfloat16)

    def packed(n):
        for rows, cols, place in PIECES:
            main[:n, ROWS:, place] = rest[:n, rows, cols]
        return main[:n]

    main[...] = jnp.dot(
        coeff, texts[:, :MAIN], preferred_element_type=jnp.float32
    ).reshape(n_images, TALL, MAIN)
    rest[...] = jnp.dot(
        coeff, texts[:, MAIN:], preferred_element_type=jnp.float32
    ).reshape(n_images, TALL, REST)
    image_out[...] = packed(n_images).astype(jnp.bfloat16)

    n = 4 * n_texts
    flip = (((0,), (0,)), ((), ()))
    main[:n] = lax.dot_general(
        coeff, images[:, :MAIN], flip, preferred_element_type=jnp.float32
    ).reshape(n, TALL, MAIN)
    rest[:n] = lax.dot_general(
        coeff, images[:, MAIN:], flip, preferred_element_type=jnp.float32
    ).reshape(n, TALL, REST)
    part = packed(n)
    own_out[...] = part[:n_texts]
    for i, out in enumerate(near_outs):
        out[...] = part[(i + 1) * n_texts : (i + 2) * n_texts].astype(jnp.bfloat16)


def pair_terms(log_temp, bias, place, images, own, near):
    small = jax.ShapeDtypeStruct(own.shape, jnp.bfloat16)
    n_images, n_texts = images.shape[0], 4 * own.shape[0]
    return pl.pallas_call(
        pair_kernel,
        in_specs=[pl.BlockSpec(memory_space=pltpu.SMEM)] * 3
        + [pl.BlockSpec(memory_space=pltpu.VMEM)] * 5,
        out_shape=[
            jax.ShapeDtypeStruct(images.shape, jnp.bfloat16),
            jax.ShapeDtypeStruct(own.shape, jnp.float32),
        ]
        + [small] * 3,
        scratch_shapes=[
            pltpu.VMEM((n_images * TALL, WIDTH), jnp.bfloat16),
            pltpu.VMEM((n_texts * TALL, WIDTH), jnp.bfloat16),
            pltpu.VMEM((n_images, TALL, REST), jnp.float32),
            pltpu.VMEM((n_images, TALL, MAIN), jnp.float32),
        ],
        compiler_params=pltpu.CompilerParams(vmem_limit_bytes=VMEM),
        cost_estimate=pl.CostEstimate(
            flops=900_000_000, bytes_accessed=4_000_000, transcendentals=131_072
        ),
    )(log_temp, bias, place, images, own, *near)


def finish_kernel(emb_ref, back_ref, out_ref, block):
    total = jnp.sum(back_ref[...].astype(jnp.float32), axis=0)
    block[:, :MAIN] = total[:ROWS]
    for rows, cols, place in PIECES:
        block[rows, MAIN + cols.start : MAIN + cols.stop] = total[ROWS:, place]
    unit, inverse = unit_rows(emb_ref[...])
    direction = block[...]
    along = jnp.sum(unit * direction, axis=1, keepdims=True)
    out_ref[...] = (direction - unit * along) * inverse


def finish(emb, back):
    return pl.pallas_call(
        finish_kernel,
        out_shape=jax.ShapeDtypeStruct(emb.shape, jnp.float32),
        scratch_shapes=[pltpu.VMEM((ROWS, WIDTH), jnp.float32)],
        compiler_params=pltpu.CompilerParams(vmem_limit_bytes=VMEM),
        cost_estimate=pl.CostEstimate(flops=500_000, bytes_accessed=1_000_000, transcendentals=0),
    )(emb, back)


def along_z(value, move):
    def place(z):
        return (z // 4 % 2) * 8 + (z % 4) * 2 + z // 8

    return lax.ppermute(value, LINE, [(place(z), place(move(z) % 16)) for z in range(16)])


NEAR = (
    (lambda z: z + 1, lambda z: z - 1),
    (lambda z: z - 1, lambda z: z + 1),
    (lambda z: z + 2 - 4 * (z % 2), lambda z: z + 2 - 4 * (z % 2)),
)


def on_device(image_embeds, text_embeds, log_temp, bias):
    place = jnp.stack([lax.axis_index(PLANE), lax.axis_index(FAR)]).astype(jnp.int32)

    own = lax.all_to_all(spread(text_embeds, lax.axis_size(FAR)), FAR, 0, 0)
    sent = spread(image_embeds, lax.axis_size(PLANE))
    sent, own = lax.optimization_barrier((sent, own))
    images = lax.all_to_all(sent, PLANE, 0, 0)
    near = [along_z(own, there) for there, _ in NEAR]

    image_part, own_part, *near_parts = pair_terms(log_temp, bias, place, images, own, near)

    image_back = lax.all_to_all(image_part, PLANE, 0, 0)
    for part, (_, home) in zip(near_parts, NEAR):
        own_part = own_part + along_z(part, home).astype(jnp.float32)
    own_part, image_back = lax.optimization_barrier((own_part, image_back))
    text_back = lax.all_to_all(own_part, FAR, 0, 0)
    return (finish(image_embeds, image_back), finish(text_embeds, text_back))


def solution(mesh):
    fine = Mesh(mesh.devices.reshape(SIZES), AXES)
    split = P(AXES, None)
    return jax.shard_map(
        on_device,
        mesh=fine,
        in_specs=(split, split, P(), P()),
        out_specs=(split, split),
        check_vma=False,
    )
```

```python
import jax
import jax.numpy as jnp
from jax import lax
from jax.experimental import pallas as pl
from jax.experimental.pallas import tpu as pltpu
from jax.sharding import Mesh, PartitionSpec as P

EPS = 1e-06
AXES = ("x", "zm", "zn", "core", "zh", "y")
SIZES = (4, 2, 4, 2, 2, 4)
PLANE = ("x", "core", "y")
LINE = ("zm", "zn", "zh")
FAR = (0, 4, 12, 8)
VMEM = 48 * 1024 * 1024

ROWS = 12
WIDTH = 1152
TALL = 16
MAIN = 896
REST = WIDTH - MAIN
STEP = TALL - ROWS
PIECES = [
    (
        slice(m * STEP, (m + 1) * STEP),
        slice(g * 128, (g + 1) * 128),
        slice((3 * g + m) * 128, (3 * g + m + 1) * 128),
    )
    for g in range(REST // 128)
    for m in range(ROWS // STEP)
]


def unit_rows(emb):
    wide = emb.astype(jnp.float32)
    inverse = lax.rsqrt(jnp.sum(wide * wide, axis=1, keepdims=True) + EPS)
    return (wide * inverse, inverse)


def spread_kernel(emb_ref, out_ref, block):
    unit, _ = unit_rows(emb_ref[...])
    block[:ROWS, :] = unit[:, :MAIN]
    block[ROWS:, :] = jnp.zeros((STEP, MAIN), jnp.float32)
    for rows, cols, place in PIECES:
        block[ROWS:, place] = unit[rows, MAIN + cols.start : MAIN + cols.stop]
    out_ref[...] = jnp.broadcast_to(block[...].astype(jnp.bfloat16)[None], out_ref.shape)


def spread(emb, peers):
    return pl.pallas_call(
        spread_kernel,
        out_shape=jax.ShapeDtypeStruct((peers, TALL, MAIN), jnp.bfloat16),
        scratch_shapes=[pltpu.VMEM((TALL, MAIN), jnp.float32)],
        compiler_params=pltpu.CompilerParams(vmem_limit_bytes=VMEM),
        cost_estimate=pl.CostEstimate(flops=100_000, bytes_accessed=1_000_000, transcendentals=0),
    )(emb)


def pair_kernel(temp_ref, bias_ref, place_ref, images_ref, *refs):
    text_refs = refs[:4]
    core_out, image_out, text_out = refs[4:7]
    images, texts, rest, main = refs[7:]
    n_images = images_ref.shape[0]
    far = text_refs[0].shape[0]
    groups = [(images, 0, images_ref)]
    groups += [(texts, i * far, ref) for i, ref in enumerate(text_refs)]
    rest[:, ROWS:, :] = jnp.zeros((n_images, STEP, REST), jnp.float32)
    for whole, first, ref in groups:
        n = ref.shape[0]
        span = pl.ds(first * TALL, n * TALL)
        whole[span, :MAIN] = ref[...].reshape(n * TALL, MAIN)
        for rows, cols, place in PIECES:
            rest[:n, rows, cols] = ref[:, ROWS:, place].astype(jnp.float32)
        whole[span, MAIN:] = rest[:n].reshape(n * TALL, REST).astype(jnp.bfloat16)

    scale = jnp.exp(jnp.full((1, 1), temp_ref[0], jnp.float32))
    logits = (
        scale
        * lax.dot_general(
            images[...], texts[...], (((1,), (1,)), ((), ())), preferred_element_type=jnp.float32
        )
        + bias_ref[0]
    )
    x, core, y, z = (place_ref[i] for i in range(4))
    row = lax.broadcasted_iota(jnp.int32, logits.shape, 0)
    col = lax.broadcasted_iota(jnp.int32, logits.shape, 1)
    row_in, col_in = row % TALL, col % TALL
    real = (row_in < ROWS) & (col_in < ROWS)
    same = (row == col + (x * 8 + core * 4 + y) * TALL) & (col < TALL)
    sig = jax.nn.sigmoid(jnp.where(same, -logits, logits))
    coeff = jnp.where(real, jnp.where(same, -sig, sig) * scale, 0.0).astype(jnp.bfloat16)

    def pack(n):
        for rows, cols, place in PIECES:
            main[:n, ROWS:, place] = rest[:n, rows, cols]

    main[...] = jnp.dot(
        coeff, texts[:, :MAIN], preferred_element_type=jnp.float32
    ).reshape(n_images, TALL, MAIN)
    rest[...] = jnp.dot(
        coeff, texts[:, MAIN:], preferred_element_type=jnp.float32
    ).reshape(n_images, TALL, REST)
    pack(n_images)
    for dy in range(4):
        for dx in range(4):
            spot = (x + dx) % 4 * 8 + (y + dy) % 4
            core_out[dy * 4 + dx] = main[spot + (1 - core) * 4].astype(jnp.bfloat16)
            image_out[dy * 4 + dx] = main[spot + core * 4]

    n = 4 * far
    flip = (((0,), (0,)), ((), ()))
    main[:n] = lax.dot_general(
        coeff, images[:, :MAIN], flip, preferred_element_type=jnp.float32
    ).reshape(n, TALL, MAIN)
    rest[:n] = lax.dot_general(
        coeff, images[:, MAIN:], flip, preferred_element_type=jnp.float32
    ).reshape(n, TALL, REST)
    pack(n)
    for i, near in enumerate(near_moves(z)):
        for j, by in enumerate(FAR):
            source = (z - near - by + 32) % 16
            text_out[line_place(source)] = main[i * far + j].astype(jnp.bfloat16)


def pair_terms(log_temp, bias, place, images, texts):
    n_images, n_texts = images.shape[0], 4 * texts[0].shape[0]
    return pl.pallas_call(
        pair_kernel,
        in_specs=[pl.BlockSpec(memory_space=pltpu.SMEM)] * 3
        + [pl.BlockSpec(memory_space=pltpu.VMEM)] * 5,
        out_shape=[
            jax.ShapeDtypeStruct((n_images // 2, TALL, MAIN), jnp.bfloat16),
            jax.ShapeDtypeStruct((n_images // 2, TALL, MAIN), jnp.float32),
            jax.ShapeDtypeStruct((n_texts, TALL, MAIN), jnp.bfloat16),
        ],
        scratch_shapes=[
            pltpu.VMEM((n_images * TALL, WIDTH), jnp.bfloat16),
            pltpu.VMEM((n_texts * TALL, WIDTH), jnp.bfloat16),
            pltpu.VMEM((n_images, TALL, REST), jnp.float32),
            pltpu.VMEM((n_images, TALL, MAIN), jnp.float32),
        ],
        compiler_params=pltpu.CompilerParams(vmem_limit_bytes=VMEM),
        cost_estimate=pl.CostEstimate(
            flops=900_000_000, bytes_accessed=4_000_000, transcendentals=131_072
        ),
    )(log_temp, bias, place, images, *texts)


def finish_kernel(emb_ref, back_ref, out_ref, block):
    total = jnp.sum(back_ref[...].astype(jnp.float32), axis=0)
    block[:, :MAIN] = total[:ROWS]
    for rows, cols, place in PIECES:
        block[rows, MAIN + cols.start : MAIN + cols.stop] = total[ROWS:, place]
    unit, inverse = unit_rows(emb_ref[...])
    direction = block[...]
    along = jnp.sum(unit * direction, axis=1, keepdims=True)
    out_ref[...] = (direction - unit * along) * inverse


def finish(emb, back):
    return pl.pallas_call(
        finish_kernel,
        out_shape=jax.ShapeDtypeStruct(emb.shape, jnp.float32),
        scratch_shapes=[pltpu.VMEM((ROWS, WIDTH), jnp.float32)],
        compiler_params=pltpu.CompilerParams(vmem_limit_bytes=VMEM),
        cost_estimate=pl.CostEstimate(flops=500_000, bytes_accessed=1_000_000, transcendentals=0),
    )(emb, back)


def line_place(z):
    return (z // 4 % 2) * 8 + (z % 4) * 2 + z // 8


def near_moves(z):
    return (0, 1, -1, 2 - 4 * (z % 2))


def along_z(value, move):
    pairs = [(line_place(z), line_place((z + move(z)) % 16)) for z in range(16)]
    return lax.ppermute(value, LINE, pairs)


def around(value, axis, by):
    n = lax.axis_size(axis)
    return lax.ppermute(value, axis, [(i, (i + by) % n) for i in range(n)])


def on_device(image_embeds, text_embeds, log_temp, bias):
    z = lax.axis_index("zh") * 8 + lax.axis_index("zm") * 4 + lax.axis_index("zn")
    place = jnp.stack([lax.axis_index(axis) for axis in PLANE] + [z]).astype(jnp.int32)

    images = lax.all_to_all(spread(image_embeds, lax.axis_size(PLANE)), PLANE, 0, 0)
    own = spread(text_embeds, 1)
    own = jnp.concatenate([own] + [along_z(own, lambda z, by=by: by) for by in FAR[1:]], axis=0)
    texts = [own] + [along_z(own, lambda z, i=i: near_moves(z)[i]) for i in (1, 2, 3)]

    core_part, part, text_part = pair_terms(log_temp, bias, place, images, texts)

    text_back = lax.all_to_all(text_part, LINE, 0, 0)
    part = part + around(core_part, "core", 1).astype(jnp.float32)
    part = part.reshape((4, 4) + part.shape[1:])
    part = part[0] + sum(
        around(part[by].astype(jnp.bfloat16), "y", by).astype(jnp.float32) for by in (1, 3, 2)
    )
    image_back = jnp.stack([part[0]] + [around(part[by], "x", by) for by in (1, 3, 2)], axis=0)
    return (finish(image_embeds, image_back), finish(text_embeds, text_back))


def solution(mesh):
    fine = Mesh(mesh.devices.reshape(SIZES), AXES)
    split = P(AXES, None)
    return jax.shard_map(
        on_device,
        mesh=fine,
        in_specs=(split, split, P(), P()),
        out_specs=(split, split),
        check_vma=False,
    )
```

```python
import jax
import jax.numpy as jnp
from jax import lax
from jax.experimental import pallas as pl
from jax.experimental.pallas import tpu as pltpu
from jax.sharding import Mesh, PartitionSpec as P

EPS = 1e-06
AXES = ("x", "zm", "zn", "core", "zh", "y")
SIZES = (4, 2, 4, 2, 2, 4)
PLANE = ("x", "core", "y")
LINE = ("zm", "zn", "zh")
FAR = (0, 5, -5)
NEAR = (1, -1, 2, -2)
VMEM = 48 * 1024 * 1024

ROWS = 12
WIDTH = 1152
TALL = 16
MAIN = 896
REST = WIDTH - MAIN
STEP = TALL - ROWS
PIECES = [
    (
        slice(m * STEP, (m + 1) * STEP),
        slice(g * 128, (g + 1) * 128),
        slice((3 * g + m) * 128, (3 * g + m + 1) * 128),
    )
    for g in range(REST // 128)
    for m in range(ROWS // STEP)
]


def spread_kernel(emb_ref, out_ref, unit_ref, inverse_ref, block):
    wide = emb_ref[...].astype(jnp.float32)
    inverse = lax.rsqrt(jnp.sum(wide * wide, axis=1, keepdims=True) + EPS)
    unit_ref[...] = wide * inverse
    inverse_ref[...] = inverse
    block[:ROWS, :] = unit_ref[:, :MAIN]
    block[ROWS:, :] = jnp.zeros((STEP, MAIN), jnp.float32)
    for rows, cols, place in PIECES:
        block[ROWS:, place] = unit_ref[rows, MAIN + cols.start : MAIN + cols.stop]
    out_ref[...] = jnp.broadcast_to(block[...].astype(jnp.bfloat16)[None], out_ref.shape)


def spread(emb, peers):
    return pl.pallas_call(
        spread_kernel,
        out_shape=[
            jax.ShapeDtypeStruct((peers, TALL, MAIN), jnp.bfloat16),
            jax.ShapeDtypeStruct(emb.shape, jnp.float32),
            jax.ShapeDtypeStruct((ROWS, 1), jnp.float32),
        ],
        scratch_shapes=[pltpu.VMEM((TALL, MAIN), jnp.float32)],
        compiler_params=pltpu.CompilerParams(vmem_limit_bytes=VMEM),
        cost_estimate=pl.CostEstimate(flops=100_000, bytes_accessed=1_000_000, transcendentals=0),
    )(emb)


def packed(main, rest, n):
    for rows, cols, place in PIECES:
        main[:n, ROWS:, place] = rest[:n, rows, cols]
    return main[:n]


def text_kernel(temp_ref, bias_ref, place_ref, images_ref, *refs):
    text_refs = refs[:6]
    coeff_ref, texts = refs[6:8]
    outs = refs[8:14]
    images, rest, main = refs[14:]
    rest[:, ROWS:, :] = jnp.zeros((rest.shape[0], STEP, REST), jnp.float32)
    first = [0]
    for ref in text_refs:
        first.append(first[-1] + ref.shape[0])
    groups = [(images, 0, images_ref)] + [(texts, i, ref) for i, ref in zip(first, text_refs)]
    for whole, start, ref in groups:
        n = ref.shape[0]
        span = pl.ds(start * TALL, n * TALL)
        whole[span, :MAIN] = ref[...].reshape(n * TALL, MAIN)
        for rows, cols, place in PIECES:
            rest[:n, rows, cols] = ref[:, ROWS:, place].astype(jnp.float32)
        whole[span, MAIN:] = rest[:n].reshape(n * TALL, REST).astype(jnp.bfloat16)

    scale = jnp.exp(jnp.full((1, 1), temp_ref[0], jnp.float32))
    logits = (
        scale
        * lax.dot_general(
            images[...], texts[...], (((1,), (1,)), ((), ())), preferred_element_type=jnp.float32
        )
        + bias_ref[0]
    )
    row = lax.broadcasted_iota(jnp.int32, logits.shape, 0)
    col = lax.broadcasted_iota(jnp.int32, logits.shape, 1)
    real = (row % TALL < ROWS) & (col % TALL < ROWS)
    same = (row == col + place_ref[0] * TALL) & (col < TALL)
    sig = jax.nn.sigmoid(jnp.where(same, -logits, logits))
    coeff = jnp.where(real, jnp.where(same, -sig, sig) * scale, 0.0).astype(jnp.bfloat16)
    coeff_ref[...] = coeff

    n = first[-1]
    flip = (((0,), (0,)), ((), ()))
    main[...] = lax.dot_general(
        coeff, images[:, :MAIN], flip, preferred_element_type=jnp.float32
    ).reshape(n, TALL, MAIN)
    rest[:n] = lax.dot_general(
        coeff, images[:, MAIN:], flip, preferred_element_type=jnp.float32
    ).reshape(n, TALL, REST)
    packed(main, rest, n)
    for start, out in zip(first, outs):
        out[...] = main[start : start + out.shape[0]].astype(out.dtype)


def text_terms(log_temp, bias, place, images, texts):
    n_images, n_texts = images.shape[0], sum(text.shape[0] for text in texts)
    return pl.pallas_call(
        text_kernel,
        in_specs=[pl.BlockSpec(memory_space=pltpu.SMEM)] * 3
        + [pl.BlockSpec(memory_space=pltpu.VMEM)] * (1 + len(texts)),
        out_shape=[
            jax.ShapeDtypeStruct((n_images * TALL, n_texts * TALL), jnp.bfloat16),
            jax.ShapeDtypeStruct((n_texts * TALL, WIDTH), jnp.bfloat16),
            jax.ShapeDtypeStruct(texts[0].shape, jnp.float32),
        ]
        + [jax.ShapeDtypeStruct(text.shape, jnp.bfloat16) for text in texts[1:]],
        scratch_shapes=[
            pltpu.VMEM((n_images * TALL, WIDTH), jnp.bfloat16),
            pltpu.VMEM((n_images, TALL, REST), jnp.float32),
            pltpu.VMEM((n_texts, TALL, MAIN), jnp.float32),
        ],
        compiler_params=pltpu.CompilerParams(vmem_limit_bytes=VMEM),
        cost_estimate=pl.CostEstimate(
            flops=600_000_000, bytes_accessed=4_000_000, transcendentals=131_072
        ),
    )(log_temp, bias, place, images, *texts)


def image_kernel(coeff_ref, texts_ref, out_ref, rest, main):
    n = out_ref.shape[0]
    coeff = coeff_ref[...]
    main[...] = jnp.dot(
        coeff, texts_ref[:, :MAIN], preferred_element_type=jnp.float32
    ).reshape(n, TALL, MAIN)
    rest[...] = jnp.dot(
        coeff, texts_ref[:, MAIN:], preferred_element_type=jnp.float32
    ).reshape(n, TALL, REST)
    out_ref[...] = packed(main, rest, n).astype(jnp.bfloat16)


def image_terms(coeff, texts):
    n = coeff.shape[0] // TALL
    return pl.pallas_call(
        image_kernel,
        out_shape=jax.ShapeDtypeStruct((n, TALL, MAIN), jnp.bfloat16),
        scratch_shapes=[
            pltpu.VMEM((n, TALL, REST), jnp.float32),
            pltpu.VMEM((n, TALL, MAIN), jnp.float32),
        ],
        compiler_params=pltpu.CompilerParams(vmem_limit_bytes=VMEM),
        cost_estimate=pl.CostEstimate(
            flops=300_000_000, bytes_accessed=2_000_000, transcendentals=0
        ),
    )(coeff, texts)


def finish_kernel(unit_ref, inverse_ref, *refs):
    back_refs, (out_ref, block) = refs[:-2], refs[-2:]
    total = sum(jnp.sum(ref[...].astype(jnp.float32), axis=0) for ref in back_refs)
    block[:, :MAIN] = total[:ROWS]
    for rows, cols, place in PIECES:
        block[rows, MAIN + cols.start : MAIN + cols.stop] = total[ROWS:, place]
    unit = unit_ref[...]
    direction = block[...]
    along = jnp.sum(unit * direction, axis=1, keepdims=True)
    out_ref[...] = (direction - unit * along) * inverse_ref[...]


def finish(unit, inverse, *back):
    return pl.pallas_call(
        finish_kernel,
        out_shape=jax.ShapeDtypeStruct(unit.shape, jnp.float32),
        scratch_shapes=[pltpu.VMEM((ROWS, WIDTH), jnp.float32)],
        compiler_params=pltpu.CompilerParams(vmem_limit_bytes=VMEM),
        cost_estimate=pl.CostEstimate(flops=500_000, bytes_accessed=1_000_000, transcendentals=0),
    )(unit, inverse, *back)


def along_z(value, by):
    def spot(z):
        return (z // 4 % 2) * 8 + (z % 4) * 2 + z // 8

    return lax.ppermute(value, LINE, [(spot(z), spot((z + by) % 16)) for z in range(16)])


def on_device(image_embeds, text_embeds, log_temp, bias):
    place = lax.axis_index(PLANE).astype(jnp.int32).reshape(1)
    sent, img_unit, img_inv = spread(image_embeds, lax.axis_size(PLANE))
    own, txt_unit, txt_inv = spread(text_embeds, 1)

    images = lax.all_to_all(sent, PLANE, 0, 0)
    own = jnp.concatenate([own] + [along_z(own, by) for by in FAR[1:]], axis=0)
    texts = [own] + [along_z(own, by) for by in NEAR] + [along_z(own[1:2], 8 - FAR[1])]

    coeff, whole, part, *near_parts, last_part = text_terms(log_temp, bias, place, images, texts)
    home = [along_z(near_part, -by) for near_part, by in zip(near_parts, NEAR)]
    last = along_z(last_part, FAR[1] - 8)
    image_back = lax.all_to_all(image_terms(coeff, whole), PLANE, 0, 0)
    part = part + sum(value.astype(jnp.float32) for value in home)
    far = [along_z(part[1:2] + last.astype(jnp.float32), -FAR[1]), along_z(part[2:3], -FAR[2])]
    return (
        finish(img_unit, img_inv, image_back),
        finish(txt_unit, txt_inv, part[:1], *far),
    )


def solution(mesh):
    fine = Mesh(mesh.devices.reshape(SIZES), AXES)
    split = P(AXES, None)
    return jax.shard_map(
        on_device,
        mesh=fine,
        in_specs=(split, split, P(), P()),
        out_specs=(split, split),
        check_vma=False,
    )
```

```python
import jax
import jax.numpy as jnp
from jax import lax
from jax.experimental import pallas as pl
from jax.experimental.pallas import tpu as pltpu
from jax.sharding import Mesh, PartitionSpec as P

EPS = 1e-06
AXES = ("x", "zm", "zn", "core", "zh", "y")
SIZES = (4, 2, 4, 2, 2, 4)
PLANE = ("x", "core", "y")
LINE = ("zm", "zn", "zh")
FAR = ("zm", "zh")
VMEM = 48 * 1024 * 1024

ROWS = 12
WIDTH = 1152
TALL = 16
MAIN = 896
REST = WIDTH - MAIN
STEP = TALL - ROWS
PIECES = [
    (
        slice(m * STEP, (m + 1) * STEP),
        slice(g * 128, (g + 1) * 128),
        slice((3 * g + m) * 128, (3 * g + m + 1) * 128),
    )
    for g in range(REST // 128)
    for m in range(ROWS // STEP)
]


def spread_kernel(emb_ref, out_ref, unit_ref, inverse_ref, block):
    wide = emb_ref[...].astype(jnp.float32)
    inverse = lax.rsqrt(jnp.sum(wide * wide, axis=1, keepdims=True) + EPS)
    unit_ref[...] = wide * inverse
    inverse_ref[...] = inverse
    block[:ROWS, :] = unit_ref[:, :MAIN]
    block[ROWS:, :] = jnp.zeros((STEP, MAIN), jnp.float32)
    for rows, cols, place in PIECES:
        block[ROWS:, place] = unit_ref[rows, MAIN + cols.start : MAIN + cols.stop]
    out_ref[...] = jnp.broadcast_to(block[...].astype(jnp.bfloat16)[None], out_ref.shape)


def spread(emb, peers):
    return pl.pallas_call(
        spread_kernel,
        out_shape=[
            jax.ShapeDtypeStruct((peers, TALL, MAIN), jnp.bfloat16),
            jax.ShapeDtypeStruct(emb.shape, jnp.float32),
            jax.ShapeDtypeStruct((ROWS, 1), jnp.float32),
        ],
        scratch_shapes=[pltpu.VMEM((TALL, MAIN), jnp.float32)],
        compiler_params=pltpu.CompilerParams(vmem_limit_bytes=VMEM),
        cost_estimate=pl.CostEstimate(flops=100_000, bytes_accessed=1_000_000, transcendentals=0),
    )(emb)


def packed(main, rest, n):
    for rows, cols, place in PIECES:
        main[:n, ROWS:, place] = rest[:n, rows, cols]
    return main[:n]


def text_kernel(temp_ref, bias_ref, place_ref, images_ref, texts_ref, coeff_ref, texts, *refs):
    own_out, near_outs = refs[0], refs[1:4]
    images, rest, main = refs[4:]
    n = texts_ref.shape[0]
    rest[:, ROWS:, :] = jnp.zeros((rest.shape[0], STEP, REST), jnp.float32)
    for whole, ref in ((images, images_ref), (texts, texts_ref)):
        count = ref.shape[0]
        whole[:, :MAIN] = ref[...].reshape(count * TALL, MAIN)
        for rows, cols, place in PIECES:
            rest[:count, rows, cols] = ref[:, ROWS:, place].astype(jnp.float32)
        whole[:, MAIN:] = rest[:count].reshape(count * TALL, REST).astype(jnp.bfloat16)

    scale = jnp.exp(jnp.full((1, 1), temp_ref[0], jnp.float32))
    logits = (
        scale
        * lax.dot_general(
            images[...], texts[...], (((1,), (1,)), ((), ())), preferred_element_type=jnp.float32
        )
        + bias_ref[0]
    )
    row = lax.broadcasted_iota(jnp.int32, logits.shape, 0)
    col = lax.broadcasted_iota(jnp.int32, logits.shape, 1)
    row_in, col_in = row % TALL, col % TALL
    real = (row_in < ROWS) & (col_in < ROWS)
    zm, zn, zh = (place_ref[i] for i in (1, 2, 3))
    mine = zm * 8 + zn * 2 + zh
    same = (row - place_ref[0] * TALL == row_in) & (col - mine * TALL == col_in)
    same = same & (row_in == col_in)
    sig = jax.nn.sigmoid(jnp.where(same, -logits, logits))
    coeff = jnp.where(real, jnp.where(same, -sig, sig) * scale, 0.0).astype(jnp.bfloat16)
    coeff_ref[...] = coeff

    flip = (((0,), (0,)), ((), ()))
    main[...] = lax.dot_general(
        coeff, images[:, :MAIN], flip, preferred_element_type=jnp.float32
    ).reshape(n, TALL, MAIN)
    rest[:n] = lax.dot_general(
        coeff, images[:, MAIN:], flip, preferred_element_type=jnp.float32
    ).reshape(n, TALL, REST)
    packed(main, rest, n)
    for out, by in zip((own_out,) + near_outs, (0, 1, 3, 2)):
        for far in range(4):
            part = main[far // 2 * 8 + (zn + by) % 4 * 2 + far % 2]
            out[far] = part.astype(out.dtype)


def text_terms(log_temp, bias, place, images, texts):
    n_images, n_texts = images.shape[0], texts.shape[0]
    return pl.pallas_call(
        text_kernel,
        in_specs=[pl.BlockSpec(memory_space=pltpu.SMEM)] * 3
        + [pl.BlockSpec(memory_space=pltpu.VMEM)] * 2,
        out_shape=[
            jax.ShapeDtypeStruct((n_images * TALL, n_texts * TALL), jnp.bfloat16),
            jax.ShapeDtypeStruct((n_texts * TALL, WIDTH), jnp.bfloat16),
            jax.ShapeDtypeStruct((n_texts // 4, TALL, MAIN), jnp.float32),
        ]
        + [jax.ShapeDtypeStruct((n_texts // 4, TALL, MAIN), jnp.bfloat16)] * 3,
        scratch_shapes=[
            pltpu.VMEM((n_images * TALL, WIDTH), jnp.bfloat16),
            pltpu.VMEM((n_images, TALL, REST), jnp.float32),
            pltpu.VMEM((n_texts, TALL, MAIN), jnp.float32),
        ],
        compiler_params=pltpu.CompilerParams(vmem_limit_bytes=VMEM),
        cost_estimate=pl.CostEstimate(
            flops=600_000_000, bytes_accessed=4_000_000, transcendentals=131_072
        ),
    )(log_temp, bias, place, images, texts)


def image_kernel(coeff_ref, texts_ref, out_ref, rest, main):
    n = out_ref.shape[0]
    coeff = coeff_ref[...]
    main[...] = jnp.dot(
        coeff, texts_ref[:, :MAIN], preferred_element_type=jnp.float32
    ).reshape(n, TALL, MAIN)
    rest[...] = jnp.dot(
        coeff, texts_ref[:, MAIN:], preferred_element_type=jnp.float32
    ).reshape(n, TALL, REST)
    out_ref[...] = packed(main, rest, n).astype(jnp.bfloat16)


def image_terms(coeff, texts):
    n = coeff.shape[0] // TALL
    return pl.pallas_call(
        image_kernel,
        out_shape=jax.ShapeDtypeStruct((n, TALL, MAIN), jnp.bfloat16),
        scratch_shapes=[
            pltpu.VMEM((n, TALL, REST), jnp.float32),
            pltpu.VMEM((n, TALL, MAIN), jnp.float32),
        ],
        compiler_params=pltpu.CompilerParams(vmem_limit_bytes=VMEM),
        cost_estimate=pl.CostEstimate(
            flops=300_000_000, bytes_accessed=2_000_000, transcendentals=0
        ),
    )(coeff, texts)


def finish_kernel(unit_ref, inverse_ref, *refs):
    back_refs, (out_ref, block) = refs[:-2], refs[-2:]
    total = sum(jnp.sum(ref[...].astype(jnp.float32), axis=0) for ref in back_refs)
    block[:, :MAIN] = total[:ROWS]
    for rows, cols, place in PIECES:
        block[rows, MAIN + cols.start : MAIN + cols.stop] = total[ROWS:, place]
    unit = unit_ref[...]
    direction = block[...]
    along = jnp.sum(unit * direction, axis=1, keepdims=True)
    out_ref[...] = (direction - unit * along) * inverse_ref[...]


def finish(unit, inverse, *back):
    return pl.pallas_call(
        finish_kernel,
        out_shape=jax.ShapeDtypeStruct(unit.shape, jnp.float32),
        scratch_shapes=[pltpu.VMEM((ROWS, WIDTH), jnp.float32)],
        compiler_params=pltpu.CompilerParams(vmem_limit_bytes=VMEM),
        cost_estimate=pl.CostEstimate(flops=500_000, bytes_accessed=1_000_000, transcendentals=0),
    )(unit, inverse, *back)


def along_z(value, move):
    def spot(z):
        return (z // 4 % 2) * 8 + (z % 4) * 2 + z // 8

    return lax.ppermute(value, LINE, [(spot(z), spot(move(z) % 16)) for z in range(16)])


HOME = (lambda z: z + 1, lambda z: z - 1, lambda z: z + 2 - 4 * (z % 2))


def on_device(image_embeds, text_embeds, log_temp, bias):
    place = [lax.axis_index(PLANE)] + [lax.axis_index(axis) for axis in LINE]
    place = jnp.stack(place).astype(jnp.int32)
    own, txt_unit, txt_inv = spread(text_embeds, 1)
    sent, img_unit, img_inv = spread(image_embeds, lax.axis_size(PLANE))

    texts = lax.all_gather(own, LINE, axis=0, tiled=True)
    images = lax.all_to_all(sent, PLANE, 0, 0)

    coeff, whole, part, *near_parts = text_terms(log_temp, bias, place, images, texts)
    image_back = lax.all_to_all(image_terms(coeff, whole), PLANE, 0, 0)
    for near_part, move in zip(near_parts, HOME):
        part = part + along_z(near_part, move).astype(jnp.float32)
    part, image_back = lax.optimization_barrier((part, image_back))
    text_back = lax.all_to_all(part, FAR, 0, 0)
    return (
        finish(img_unit, img_inv, image_back),
        finish(txt_unit, txt_inv, text_back),
    )


def solution(mesh):
    fine = Mesh(mesh.devices.reshape(SIZES), AXES)
    split = P(AXES, None)
    return jax.shard_map(
        on_device,
        mesh=fine,
        in_specs=(split, split, P(), P()),
        out_specs=(split, split),
        check_vma=False,
    )
```

```python
import jax
import jax.numpy as jnp
from jax import lax
from jax.experimental import pallas as pl
from jax.experimental.pallas import tpu as pltpu
from jax.sharding import Mesh, PartitionSpec as P

EPS = 1e-06
AXES = ("x", "zm", "zn", "core", "zh", "y")
SIZES = (4, 2, 4, 2, 2, 4)
PLANE = ("x", "core", "y")
LINE = ("zm", "zn", "zh")
FAR = ("zm", "zh")
VMEM = 48 * 1024 * 1024

ROWS = 12
WIDTH = 1152
TALL = 16
MAIN = 896
REST = WIDTH - MAIN
STEP = TALL - ROWS
PIECES = [
    (
        slice(m * STEP, (m + 1) * STEP),
        slice(g * 128, (g + 1) * 128),
        slice((3 * g + m) * 128, (3 * g + m + 1) * 128),
    )
    for g in range(REST // 128)
    for m in range(ROWS // STEP)
]

WIDE = 1024


def spread_kernel(emb_ref, out_ref, unit_ref, inverse_ref, half_ref, block):
    wide = emb_ref[...].astype(jnp.float32)
    inverse = lax.rsqrt(jnp.sum(wide * wide, axis=1, keepdims=True) + EPS)
    unit_ref[...] = wide * inverse
    inverse_ref[...] = inverse
    half_ref[...] = unit_ref[...].astype(jnp.bfloat16)
    block[:ROWS, :] = unit_ref[:, :MAIN]
    block[ROWS:, :] = jnp.zeros((STEP, MAIN), jnp.float32)
    for rows, cols, place in PIECES:
        block[ROWS:, place] = unit_ref[rows, MAIN + cols.start : MAIN + cols.stop]
    out_ref[...] = jnp.broadcast_to(block[...].astype(jnp.bfloat16)[None], out_ref.shape)


def spread(emb, peers):
    return pl.pallas_call(
        spread_kernel,
        out_shape=[
            jax.ShapeDtypeStruct((peers, TALL, MAIN), jnp.bfloat16),
            jax.ShapeDtypeStruct(emb.shape, jnp.float32),
            jax.ShapeDtypeStruct((ROWS, 1), jnp.float32),
            jax.ShapeDtypeStruct(emb.shape, jnp.bfloat16),
        ],
        scratch_shapes=[pltpu.VMEM((TALL, MAIN), jnp.float32)],
        compiler_params=pltpu.CompilerParams(vmem_limit_bytes=VMEM),
        cost_estimate=pl.CostEstimate(flops=100_000, bytes_accessed=1_000_000, transcendentals=0),
    )(emb)


def packed(main, rest, n):
    for rows, cols, place in PIECES:
        main[:n, ROWS:, place] = rest[:n, rows, cols]
    return main[:n]


def text_kernel(temp_ref, bias_ref, place_ref, images_ref, *refs):
    text_refs = refs[:4]
    coeff_ref, texts = refs[4:6]
    outs = refs[6:10]
    images, rest, main = refs[10:]
    rest[:, ROWS:, :] = jnp.zeros((rest.shape[0], STEP, REST), jnp.float32)
    first = [0]
    for ref in text_refs:
        first.append(first[-1] + ref.shape[0])
    groups = [(images, 0, images_ref)] + [(texts, i, ref) for i, ref in zip(first, text_refs)]
    for whole, start, ref in groups:
        n = ref.shape[0]
        span = pl.ds(start * TALL, n * TALL)
        whole[span, :MAIN] = ref[...].reshape(n * TALL, MAIN)
        for rows, cols, place in PIECES:
            rest[:n, rows, cols] = ref[:, ROWS:, place].astype(jnp.float32)
        whole[span, MAIN:] = rest[:n].reshape(n * TALL, REST).astype(jnp.bfloat16)

    scale = jnp.exp(jnp.full((1, 1), temp_ref[0], jnp.float32))
    logits = (
        scale
        * lax.dot_general(
            images[...], texts[...], (((1,), (1,)), ((), ())), preferred_element_type=jnp.float32
        )
        + bias_ref[0]
    )
    row = lax.broadcasted_iota(jnp.int32, logits.shape, 0)
    col = lax.broadcasted_iota(jnp.int32, logits.shape, 1)
    row_in, col_in = row % TALL, col % TALL
    real = (row_in < ROWS) & (col_in < ROWS)
    same = (row - place_ref[0] * TALL == row_in) & (col - place_ref[1] * TALL == col_in)
    same = same & (row_in == col_in)
    sig = jax.nn.sigmoid(jnp.where(same, -logits, logits))
    coeff = jnp.where(real, jnp.where(same, -sig, sig) * scale, 0.0).astype(jnp.bfloat16)
    coeff_ref[...] = coeff

    n = first[-1]
    flip = (((0,), (0,)), ((), ()))
    main[...] = lax.dot_general(
        coeff, images[:, :MAIN], flip, preferred_element_type=jnp.float32
    ).reshape(n, TALL, MAIN)
    rest[:n] = lax.dot_general(
        coeff, images[:, MAIN:], flip, preferred_element_type=jnp.float32
    ).reshape(n, TALL, REST)
    packed(main, rest, n)
    for start, out in zip(first, outs):
        out[...] = main[start : start + out.shape[0]].astype(out.dtype)


def text_terms(log_temp, bias, place, images, texts):
    n_images, n_texts = images.shape[0], sum(text.shape[0] for text in texts)
    return pl.pallas_call(
        text_kernel,
        in_specs=[pl.BlockSpec(memory_space=pltpu.SMEM)] * 3
        + [pl.BlockSpec(memory_space=pltpu.VMEM)] * (1 + len(texts)),
        out_shape=[
            jax.ShapeDtypeStruct((n_images * TALL, n_texts * TALL), jnp.bfloat16),
            jax.ShapeDtypeStruct((n_texts * TALL, WIDTH), jnp.bfloat16),
            jax.ShapeDtypeStruct(texts[0].shape, jnp.float32),
        ]
        + [jax.ShapeDtypeStruct(text.shape, jnp.bfloat16) for text in texts[1:]],
        scratch_shapes=[
            pltpu.VMEM((n_images * TALL, WIDTH), jnp.bfloat16),
            pltpu.VMEM((n_images, TALL, REST), jnp.float32),
            pltpu.VMEM((n_texts, TALL, MAIN), jnp.float32),
        ],
        compiler_params=pltpu.CompilerParams(vmem_limit_bytes=VMEM),
        cost_estimate=pl.CostEstimate(
            flops=600_000_000, bytes_accessed=4_000_000, transcendentals=131_072
        ),
    )(log_temp, bias, place, images, *texts)


def image_kernel(coeff_ref, texts_ref, out_ref, rest, main):
    n = out_ref.shape[0]
    coeff = coeff_ref[...]
    main[...] = jnp.dot(
        coeff, texts_ref[:, :MAIN], preferred_element_type=jnp.float32
    ).reshape(n, TALL, MAIN)
    rest[...] = jnp.dot(
        coeff, texts_ref[:, MAIN:], preferred_element_type=jnp.float32
    ).reshape(n, TALL, REST)
    out_ref[...] = packed(main, rest, n).astype(jnp.bfloat16)


def image_terms(coeff, texts):
    n = coeff.shape[0] // TALL
    return pl.pallas_call(
        image_kernel,
        out_shape=jax.ShapeDtypeStruct((n, TALL, MAIN), jnp.bfloat16),
        scratch_shapes=[
            pltpu.VMEM((n, TALL, REST), jnp.float32),
            pltpu.VMEM((n, TALL, MAIN), jnp.float32),
        ],
        compiler_params=pltpu.CompilerParams(vmem_limit_bytes=VMEM),
        cost_estimate=pl.CostEstimate(
            flops=300_000_000, bytes_accessed=2_000_000, transcendentals=0
        ),
    )(coeff, texts)


def rounded(value):
    return value.astype(jnp.bfloat16)


def far_kernel(own_ref, near_a, near_b, near_c, half_ref, out_ref, block):
    n = own_ref.shape[0]
    part = own_ref[...] + sum(ref[...].astype(jnp.float32) for ref in (near_a, near_b, near_c))
    block[:, :ROWS, :MAIN] = part[:, :ROWS]
    block[:, ROWS:, :] = jnp.zeros((n, STEP, WIDTH), jnp.float32)
    for rows, cols, place in PIECES:
        block[:, rows, MAIN + cols.start : MAIN + cols.stop] = part[:, ROWS:, place]
    half = half_ref[: n * TALL, :].astype(jnp.float32).reshape(n, TALL, WIDTH)

    along = jnp.sum(block[...] * half, axis=2, keepdims=True)
    lane = lax.broadcasted_iota(jnp.int32, (n, STEP, 128), 2)
    spare = slice(6 * 128, 7 * 128)

    def store(factor, first):
        held = out_ref[:, ROWS:, spare]
        for m in range(ROWS // STEP):
            piece = rounded(jnp.broadcast_to(factor[:, m * STEP : (m + 1) * STEP], lane.shape))
            held = jnp.where(lane == first + m, piece, held)
        out_ref[:, ROWS:, spare] = held

    def load(first):
        held = out_ref[:, ROWS:, spare].astype(jnp.float32)
        return [
            jnp.sum(jnp.where(lane == first + m, held, 0.0), axis=2, keepdims=True)
            for m in range(ROWS // STEP)
        ]

    out_ref[:, ROWS:, :] = jnp.zeros((n, STEP, WIDE), jnp.bfloat16)
    store(along, 0)
    for m, factor in enumerate(load(0)):
        rows = slice(m * STEP, (m + 1) * STEP)
        block[:, rows, :] = block[:, rows, :] - factor * half[:, rows]
    mean = jnp.sum(block[...], axis=1, keepdims=True) * (1.0 / ROWS)
    mean = rounded(mean).astype(jnp.float32)
    size = jnp.sum(mean * mean, axis=2, keepdims=True)
    along = jnp.sum(block[...] * mean, axis=2, keepdims=True)
    store(jnp.where(size > 0.0, along / jnp.where(size > 0.0, size, 1.0), 0.0), 4)
    for j in range(WIDTH // 128):
        row = ROWS + j % STEP
        cols = slice((3 + j // STEP) * 128, (4 + j // STEP) * 128)
        out_ref[:, row : row + 1, cols] = rounded(mean[:, :, j * 128 : (j + 1) * 128])
    for m, factor in enumerate(load(4)):
        rows = slice(m * STEP, (m + 1) * STEP)
        left = block[:, rows, :] - factor * mean
        block[:, rows, :] = left
    out_ref[:, :ROWS, :] = rounded(block[:, :ROWS, :WIDE])
    for m in range(ROWS // STEP):
        rows = slice(m * STEP, (m + 1) * STEP)
        out_ref[:, ROWS:, m * 128 : (m + 1) * 128] = rounded(block[:, rows, WIDE:])


def far_message(own, near, half):
    n = own.shape[0]
    return pl.pallas_call(
        far_kernel,
        out_shape=jax.ShapeDtypeStruct((n, TALL, WIDE), jnp.bfloat16),
        scratch_shapes=[pltpu.VMEM((n, TALL, WIDTH), jnp.float32)],
        compiler_params=pltpu.CompilerParams(vmem_limit_bytes=VMEM),
        cost_estimate=pl.CostEstimate(flops=500_000, bytes_accessed=1_000_000, transcendentals=0),
    )(own, *near, half)


def project(direction, unit, inverse):
    along = jnp.sum(unit * direction, axis=1, keepdims=True)
    return (direction - unit * along) * inverse


def finish_images_kernel(unit_ref, inverse_ref, back_ref, out_ref, block):
    total = jnp.sum(back_ref[...].astype(jnp.float32), axis=0)
    block[:, :MAIN] = total[:ROWS]
    for rows, cols, place in PIECES:
        block[rows, MAIN + cols.start : MAIN + cols.stop] = total[ROWS:, place]
    out_ref[...] = project(block[...], unit_ref[...], inverse_ref[...])


def finish_texts_kernel(unit_ref, inverse_ref, half_ref, back_ref, out_ref, block):
    back = back_ref[...].astype(jnp.float32)
    total = jnp.sum(back, axis=0)
    block[:, :WIDE] = total[:ROWS]
    spare = back[:, ROWS:, 6 * 128 : 7 * 128]
    lane = lax.broadcasted_iota(jnp.int32, spare.shape, 2)
    means = [
        back[:, ROWS + j % STEP : ROWS + j % STEP + 1, (3 + j // STEP) * 128 : (4 + j // STEP) * 128]
        for j in range(WIDTH // 128)
    ]
    for m in range(ROWS // STEP):
        rows = slice(m * STEP, (m + 1) * STEP)
        block[rows, WIDE:] = total[ROWS:, m * 128 : (m + 1) * 128]
        own = jnp.sum(jnp.where(lane == m, spare, 0.0), axis=2, keepdims=True)
        mean = jnp.sum(jnp.where(lane == 4 + m, spare, 0.0), axis=2, keepdims=True)
        block[rows, :] += jnp.sum(own, axis=0) * half_ref[rows, :].astype(jnp.float32)
        for j, piece in enumerate(means):
            block[rows, j * 128 : (j + 1) * 128] += jnp.sum(mean * piece, axis=0)
    out_ref[...] = project(block[...], unit_ref[...], inverse_ref[...])


def finish(kernel, unit, *operands):
    return pl.pallas_call(
        kernel,
        out_shape=jax.ShapeDtypeStruct(unit.shape, jnp.float32),
        scratch_shapes=[pltpu.VMEM((ROWS, WIDTH), jnp.float32)],
        compiler_params=pltpu.CompilerParams(vmem_limit_bytes=VMEM),
        cost_estimate=pl.CostEstimate(flops=500_000, bytes_accessed=1_000_000, transcendentals=0),
    )(unit, *operands)


def along_z(value, move):
    def spot(z):
        return (z // 4 % 2) * 8 + (z % 4) * 2 + z // 8

    return lax.ppermute(value, LINE, [(spot(z), spot(move(z) % 16)) for z in range(16)])


NEAR = (
    (lambda z: z + 1, lambda z: z - 1),
    (lambda z: z - 1, lambda z: z + 1),
    (lambda z: z + 2 - 4 * (z % 2), lambda z: z + 2 - 4 * (z % 2)),
)


def on_device(image_embeds, text_embeds, log_temp, bias):
    place = jnp.stack([lax.axis_index(PLANE), lax.axis_index(FAR)]).astype(jnp.int32)

    own, txt_unit, txt_inv, txt_half = spread(text_embeds, lax.axis_size(FAR))
    own = lax.all_to_all(own, FAR, 0, 0)
    sent, img_unit, img_inv, _ = spread(image_embeds, lax.axis_size(PLANE))
    sent, own = lax.optimization_barrier((sent, own))
    images = lax.all_to_all(sent, PLANE, 0, 0)
    texts = [own] + [along_z(own, there) for there, _ in NEAR]

    coeff, whole, part, *near_parts = text_terms(log_temp, bias, place, images, texts)
    image_back = lax.all_to_all(image_terms(coeff, whole), PLANE, 0, 0)
    near = [along_z(near_part, home) for near_part, (_, home) in zip(near_parts, NEAR)]
    message, image_back = lax.optimization_barrier((far_message(part, near, whole), image_back))
    text_back = lax.all_to_all(message, FAR, 0, 0)
    return (
        finish(finish_images_kernel, img_unit, img_inv, image_back),
        finish(finish_texts_kernel, txt_unit, txt_inv, txt_half, text_back),
    )


def solution(mesh):
    fine = Mesh(mesh.devices.reshape(SIZES), AXES)
    split = P(AXES, None)
    return jax.shard_map(
        on_device,
        mesh=fine,
        in_specs=(split, split, P(), P()),
        out_specs=(split, split),
        check_vma=False,
    )
```

```python
import jax
import jax.numpy as jnp
from jax import lax
from jax.experimental import pallas as pl
from jax.experimental.pallas import tpu as pltpu
from jax.sharding import Mesh, PartitionSpec as P

EPS = 1e-06
AXES = ("x", "zm", "zn", "core", "zh", "y")
SIZES = (4, 2, 4, 2, 2, 4)
PLANE = ("x", "core", "y")
LINE = ("zm", "zn", "zh")
FAR = (0, 4, 12, 8)
VMEM = 48 * 1024 * 1024

ROWS = 12
WIDTH = 1152
TALL = 16
MAIN = 896
REST = WIDTH - MAIN
STEP = TALL - ROWS
PIECES = [
    (
        slice(m * STEP, (m + 1) * STEP),
        slice(g * 128, (g + 1) * 128),
        slice((3 * g + m) * 128, (3 * g + m + 1) * 128),
    )
    for g in range(REST // 128)
    for m in range(ROWS // STEP)
]


def spread_kernel(emb_ref, out_ref, unit_ref, inverse_ref, block):
    wide = emb_ref[...].astype(jnp.float32)
    inverse = lax.rsqrt(jnp.sum(wide * wide, axis=1, keepdims=True) + EPS)
    unit_ref[...] = wide * inverse
    inverse_ref[...] = inverse
    block[:ROWS, :] = unit_ref[:, :MAIN]
    block[ROWS:, :] = jnp.zeros((STEP, MAIN), jnp.float32)
    for rows, cols, place in PIECES:
        block[ROWS:, place] = unit_ref[rows, MAIN + cols.start : MAIN + cols.stop]
    out_ref[...] = jnp.broadcast_to(block[...].astype(jnp.bfloat16)[None], out_ref.shape)


def spread(emb, peers):
    return pl.pallas_call(
        spread_kernel,
        out_shape=[
            jax.ShapeDtypeStruct((peers, TALL, MAIN), jnp.bfloat16),
            jax.ShapeDtypeStruct(emb.shape, jnp.float32),
            jax.ShapeDtypeStruct((ROWS, 1), jnp.float32),
        ],
        scratch_shapes=[pltpu.VMEM((TALL, MAIN), jnp.float32)],
        compiler_params=pltpu.CompilerParams(vmem_limit_bytes=VMEM),
        cost_estimate=pl.CostEstimate(flops=100_000, bytes_accessed=1_000_000, transcendentals=0),
    )(emb)


def packed(main, rest, n):
    for rows, cols, place in PIECES:
        main[:n, ROWS:, place] = rest[:n, rows, cols]
    return main[:n]


def text_kernel(temp_ref, bias_ref, place_ref, images_ref, *refs):
    text_refs = refs[:4]
    coeff_ref, texts, out_ref = refs[4:7]
    images, rest, main = refs[7:]
    rest[:, ROWS:, :] = jnp.zeros((rest.shape[0], STEP, REST), jnp.float32)
    first = [0]
    for ref in text_refs:
        first.append(first[-1] + ref.shape[0])
    groups = [(images, 0, images_ref)] + [(texts, i, ref) for i, ref in zip(first, text_refs)]
    for whole, start, ref in groups:
        n = ref.shape[0]
        span = pl.ds(start * TALL, n * TALL)
        whole[span, :MAIN] = ref[...].reshape(n * TALL, MAIN)
        for rows, cols, place in PIECES:
            rest[:n, rows, cols] = ref[:, ROWS:, place].astype(jnp.float32)
        whole[span, MAIN:] = rest[:n].reshape(n * TALL, REST).astype(jnp.bfloat16)

    scale = jnp.exp(jnp.full((1, 1), temp_ref[0], jnp.float32))
    logits = (
        scale
        * lax.dot_general(
            images[...], texts[...], (((1,), (1,)), ((), ())), preferred_element_type=jnp.float32
        )
        + bias_ref[0]
    )
    row = lax.broadcasted_iota(jnp.int32, logits.shape, 0)
    col = lax.broadcasted_iota(jnp.int32, logits.shape, 1)
    real = (row % TALL < ROWS) & (col % TALL < ROWS)
    same = (row == col + place_ref[0] * TALL) & (col < TALL)
    sig = jax.nn.sigmoid(jnp.where(same, -logits, logits))
    coeff = jnp.where(real, jnp.where(same, -sig, sig) * scale, 0.0).astype(jnp.bfloat16)
    coeff_ref[...] = coeff

    n = first[-1]
    flip = (((0,), (0,)), ((), ()))
    main[...] = lax.dot_general(
        coeff, images[:, :MAIN], flip, preferred_element_type=jnp.float32
    ).reshape(n, TALL, MAIN)
    rest[:n] = lax.dot_general(
        coeff, images[:, MAIN:], flip, preferred_element_type=jnp.float32
    ).reshape(n, TALL, REST)
    packed(main, rest, n)
    z = place_ref[1]
    for start, near in zip(first, near_moves(z)):
        for slot, far in enumerate(FAR):
            out_ref[line_place((z - near - far + 32) % 16)] = main[start + slot].astype(jnp.bfloat16)


def text_terms(log_temp, bias, place, images, texts):
    n_images, n_texts = images.shape[0], sum(text.shape[0] for text in texts)
    return pl.pallas_call(
        text_kernel,
        in_specs=[pl.BlockSpec(memory_space=pltpu.SMEM)] * 3
        + [pl.BlockSpec(memory_space=pltpu.VMEM)] * (1 + len(texts)),
        out_shape=[
            jax.ShapeDtypeStruct((n_images * TALL, n_texts * TALL), jnp.bfloat16),
            jax.ShapeDtypeStruct((n_texts * TALL, WIDTH), jnp.bfloat16),
            jax.ShapeDtypeStruct((n_texts, TALL, MAIN), jnp.bfloat16),
        ],
        scratch_shapes=[
            pltpu.VMEM((n_images * TALL, WIDTH), jnp.bfloat16),
            pltpu.VMEM((n_images, TALL, REST), jnp.float32),
            pltpu.VMEM((n_texts, TALL, MAIN), jnp.float32),
        ],
        compiler_params=pltpu.CompilerParams(vmem_limit_bytes=VMEM),
        cost_estimate=pl.CostEstimate(
            flops=600_000_000, bytes_accessed=4_000_000, transcendentals=131_072
        ),
    )(log_temp, bias, place, images, *texts)


def image_kernel(place_ref, coeff_ref, texts_ref, core_out, own_out, rest, main):
    n = main.shape[0]
    coeff = coeff_ref[...]
    main[...] = jnp.dot(
        coeff, texts_ref[:, :MAIN], preferred_element_type=jnp.float32
    ).reshape(n, TALL, MAIN)
    rest[...] = jnp.dot(
        coeff, texts_ref[:, MAIN:], preferred_element_type=jnp.float32
    ).reshape(n, TALL, REST)
    packed(main, rest, n)
    x, core, y = place_ref[0] // 8, place_ref[0] // 4 % 2, place_ref[0] % 4
    for dy in range(4):
        for dx in range(4):
            spot = (x + dx) % 4 * 8 + (y + dy) % 4
            core_out[dy * 4 + dx] = main[spot + (1 - core) * 4].astype(jnp.bfloat16)
            own_out[dy * 4 + dx] = main[spot + core * 4]


def image_terms(place, coeff, texts):
    n = coeff.shape[0] // TALL
    return pl.pallas_call(
        image_kernel,
        in_specs=[pl.BlockSpec(memory_space=pltpu.SMEM)]
        + [pl.BlockSpec(memory_space=pltpu.VMEM)] * 2,
        out_shape=[
            jax.ShapeDtypeStruct((n // 2, TALL, MAIN), jnp.bfloat16),
            jax.ShapeDtypeStruct((n // 2, TALL, MAIN), jnp.float32),
        ],
        scratch_shapes=[
            pltpu.VMEM((n, TALL, REST), jnp.float32),
            pltpu.VMEM((n, TALL, MAIN), jnp.float32),
        ],
        compiler_params=pltpu.CompilerParams(vmem_limit_bytes=VMEM),
        cost_estimate=pl.CostEstimate(
            flops=300_000_000, bytes_accessed=2_000_000, transcendentals=0
        ),
    )(place, coeff, texts)


def finish_kernel(unit_ref, inverse_ref, *refs):
    back_refs, (out_ref, block) = refs[:-2], refs[-2:]
    total = sum(jnp.sum(ref[...].astype(jnp.float32), axis=0) for ref in back_refs)
    block[:, :MAIN] = total[:ROWS]
    for rows, cols, place in PIECES:
        block[rows, MAIN + cols.start : MAIN + cols.stop] = total[ROWS:, place]
    unit = unit_ref[...]
    direction = block[...]
    along = jnp.sum(unit * direction, axis=1, keepdims=True)
    out_ref[...] = (direction - unit * along) * inverse_ref[...]


def finish(unit, inverse, *back):
    return pl.pallas_call(
        finish_kernel,
        out_shape=jax.ShapeDtypeStruct(unit.shape, jnp.float32),
        scratch_shapes=[pltpu.VMEM((ROWS, WIDTH), jnp.float32)],
        compiler_params=pltpu.CompilerParams(vmem_limit_bytes=VMEM),
        cost_estimate=pl.CostEstimate(flops=500_000, bytes_accessed=1_000_000, transcendentals=0),
    )(unit, inverse, *back)


def line_place(z):
    return (z // 4 % 2) * 8 + (z % 4) * 2 + z // 8


def near_moves(z):
    return (0, 1, -1, 2 - 4 * (z % 2))


def along_z(value, move):
    pairs = [(line_place(z), line_place((z + move(z)) % 16)) for z in range(16)]
    return lax.ppermute(value, LINE, pairs)


def around(value, axis, by):
    n = lax.axis_size(axis)
    return lax.ppermute(value, axis, [(i, (i + by) % n) for i in range(n)])


def on_device(image_embeds, text_embeds, log_temp, bias):
    z = lax.axis_index("zh") * 8 + lax.axis_index("zm") * 4 + lax.axis_index("zn")
    place = jnp.stack([lax.axis_index(PLANE), z]).astype(jnp.int32)
    sent, img_unit, img_inv = spread(image_embeds, lax.axis_size(PLANE))
    own, txt_unit, txt_inv = spread(text_embeds, 1)

    images = lax.all_to_all(sent, PLANE, 0, 0)
    own = jnp.concatenate([own] + [along_z(own, lambda z, by=by: by) for by in FAR[1:]], axis=0)
    texts = [own] + [along_z(own, lambda z, i=i: near_moves(z)[i]) for i in (1, 2, 3)]

    coeff, whole, text_part = text_terms(log_temp, bias, place, images, texts)
    text_back = lax.all_to_all(text_part, LINE, 0, 0)
    core_part, part = image_terms(place, coeff, whole)
    part = part + around(core_part, "core", 1).astype(jnp.float32)
    part = part.reshape((4, 4) + part.shape[1:])
    part = part[0] + sum(
        around(part[by].astype(jnp.bfloat16), "y", by).astype(jnp.float32) for by in (1, 3, 2)
    )
    image_back = [part[:1]] + [around(part[by : by + 1], "x", by) for by in (1, 3, 2)]
    return (
        finish(img_unit, img_inv, *image_back),
        finish(txt_unit, txt_inv, text_back),
    )


def solution(mesh):
    fine = Mesh(mesh.devices.reshape(SIZES), AXES)
    split = P(AXES, None)
    return jax.shard_map(
        on_device,
        mesh=fine,
        in_specs=(split, split, P(), P()),
        out_specs=(split, split),
        check_vma=False,
    )
```

```python
import jax
import jax.numpy as jnp
from jax import lax
from jax.experimental import pallas as pl
from jax.experimental.pallas import tpu as pltpu
from jax.sharding import Mesh, PartitionSpec as P

EPS = 1e-06
AXES = ("x", "zm", "zn", "core", "zh", "y")
SIZES = (4, 2, 4, 2, 2, 4)
PLANE = ("x", "y")
LINE = ("zm", "zn", "zh")
FAR = ("zm", "zh")
VMEM = 48 * 1024 * 1024

ROWS = 12
WIDTH = 1152
TALL = 16
MAIN = 896
REST = WIDTH - MAIN
STEP = TALL - ROWS
PIECES = [
    (
        slice(m * STEP, (m + 1) * STEP),
        slice(g * 128, (g + 1) * 128),
        slice((3 * g + m) * 128, (3 * g + m + 1) * 128),
    )
    for g in range(REST // 128)
    for m in range(ROWS // STEP)
]

WIDE = 1024


def spread_kernel(emb_ref, out_ref, unit_ref, inverse_ref, half_ref, block):
    wide = emb_ref[...].astype(jnp.float32)
    inverse = lax.rsqrt(jnp.sum(wide * wide, axis=1, keepdims=True) + EPS)
    unit_ref[...] = wide * inverse
    inverse_ref[...] = inverse
    half_ref[...] = unit_ref[...].astype(jnp.bfloat16)
    block[:ROWS, :] = unit_ref[:, :MAIN]
    block[ROWS:, :] = jnp.zeros((STEP, MAIN), jnp.float32)
    for rows, cols, place in PIECES:
        block[ROWS:, place] = unit_ref[rows, MAIN + cols.start : MAIN + cols.stop]
    out_ref[...] = jnp.broadcast_to(block[...].astype(jnp.bfloat16)[None], out_ref.shape)


def spread(emb, peers):
    return pl.pallas_call(
        spread_kernel,
        out_shape=[
            jax.ShapeDtypeStruct((peers, TALL, MAIN), jnp.bfloat16),
            jax.ShapeDtypeStruct(emb.shape, jnp.float32),
            jax.ShapeDtypeStruct((ROWS, 1), jnp.float32),
            jax.ShapeDtypeStruct(emb.shape, jnp.bfloat16),
        ],
        scratch_shapes=[pltpu.VMEM((TALL, MAIN), jnp.float32)],
        compiler_params=pltpu.CompilerParams(vmem_limit_bytes=VMEM),
        cost_estimate=pl.CostEstimate(flops=100_000, bytes_accessed=1_000_000, transcendentals=0),
    )(emb)


def packed(main, rest, n):
    for rows, cols, place in PIECES:
        main[:n, ROWS:, place] = rest[:n, rows, cols]
    return main[:n]


def image_kernel(temp_ref, bias_ref, place_ref, *refs):
    image_refs, text_refs = refs[:2], refs[2:6]
    coeff_ref, images, half_ref, own_out, core_out = refs[6:11]
    texts, rest, main = refs[11:]
    rest[:, ROWS:, :] = jnp.zeros((rest.shape[0], STEP, REST), jnp.float32)
    for whole, group in ((images, image_refs), (texts, text_refs)):
        start = 0
        for ref in group:
            n = ref.shape[0]
            span = pl.ds(start * TALL, n * TALL)
            whole[span, :MAIN] = ref[...].reshape(n * TALL, MAIN)
            for rows, cols, place in PIECES:
                rest[:n, rows, cols] = ref[:, ROWS:, place].astype(jnp.float32)
            whole[span, MAIN:] = rest[:n].reshape(n * TALL, REST).astype(jnp.bfloat16)
            start += n
    half_ref[...] = texts[: half_ref.shape[0], :]

    scale = jnp.exp(jnp.full((1, 1), temp_ref[0], jnp.float32))
    logits = (
        scale
        * lax.dot_general(
            images[...], texts[...], (((1,), (1,)), ((), ())), preferred_element_type=jnp.float32
        )
        + bias_ref[0]
    )
    row = lax.broadcasted_iota(jnp.int32, logits.shape, 0)
    col = lax.broadcasted_iota(jnp.int32, logits.shape, 1)
    row_in, col_in = row % TALL, col % TALL
    real = (row_in < ROWS) & (col_in < ROWS)
    same = (row - place_ref[0] * TALL == row_in) & (col - place_ref[1] * TALL == col_in)
    same = same & (row_in == col_in)
    sig = jax.nn.sigmoid(jnp.where(same, -logits, logits))
    coeff = jnp.where(real, jnp.where(same, -sig, sig) * scale, 0.0).astype(jnp.bfloat16)
    coeff_ref[...] = coeff

    n = main.shape[0]
    main[...] = jnp.dot(
        coeff, texts[:, :MAIN], preferred_element_type=jnp.float32
    ).reshape(n, TALL, MAIN)
    rest[...] = jnp.dot(
        coeff, texts[:, MAIN:], preferred_element_type=jnp.float32
    ).reshape(n, TALL, REST)
    packed(main, rest, n)
    own_out[...] = main[: n // 2]
    core_out[...] = main[n // 2 :].astype(jnp.bfloat16)


def image_terms(log_temp, bias, place, images, texts):
    n_images, n_texts = 2 * images[0].shape[0], 4 * texts[0].shape[0]
    return pl.pallas_call(
        image_kernel,
        in_specs=[pl.BlockSpec(memory_space=pltpu.SMEM)] * 3
        + [pl.BlockSpec(memory_space=pltpu.VMEM)] * 6,
        out_shape=[
            jax.ShapeDtypeStruct((n_images * TALL, n_texts * TALL), jnp.bfloat16),
            jax.ShapeDtypeStruct((n_images * TALL, WIDTH), jnp.bfloat16),
            jax.ShapeDtypeStruct((n_texts // 4 * TALL, WIDTH), jnp.bfloat16),
            jax.ShapeDtypeStruct(images[0].shape, jnp.float32),
            jax.ShapeDtypeStruct(images[0].shape, jnp.bfloat16),
        ],
        scratch_shapes=[
            pltpu.VMEM((n_texts * TALL, WIDTH), jnp.bfloat16),
            pltpu.VMEM((n_images, TALL, REST), jnp.float32),
            pltpu.VMEM((n_images, TALL, MAIN), jnp.float32),
        ],
        compiler_params=pltpu.CompilerParams(vmem_limit_bytes=VMEM),
        cost_estimate=pl.CostEstimate(
            flops=600_000_000, bytes_accessed=4_000_000, transcendentals=131_072
        ),
    )(log_temp, bias, place, *images, *texts)


def text_kernel(coeff_ref, images_ref, *refs):
    outs, (rest, main) = refs[:4], refs[4:]
    n = main.shape[0]
    coeff = coeff_ref[...]
    flip = (((0,), (0,)), ((), ()))
    main[...] = lax.dot_general(
        coeff, images_ref[:, :MAIN], flip, preferred_element_type=jnp.float32
    ).reshape(n, TALL, MAIN)
    rest[...] = lax.dot_general(
        coeff, images_ref[:, MAIN:], flip, preferred_element_type=jnp.float32
    ).reshape(n, TALL, REST)
    packed(main, rest, n)
    for i, out in enumerate(outs):
        out[...] = main[i * (n // 4) : (i + 1) * (n // 4)].astype(out.dtype)


def text_terms(coeff, images):
    n = coeff.shape[1] // TALL
    return pl.pallas_call(
        text_kernel,
        out_shape=[jax.ShapeDtypeStruct((n // 4, TALL, MAIN), jnp.float32)]
        + [jax.ShapeDtypeStruct((n // 4, TALL, MAIN), jnp.bfloat16)] * 3,
        scratch_shapes=[
            pltpu.VMEM((n, TALL, REST), jnp.float32),
            pltpu.VMEM((n, TALL, MAIN), jnp.float32),
        ],
        compiler_params=pltpu.CompilerParams(vmem_limit_bytes=VMEM),
        cost_estimate=pl.CostEstimate(
            flops=300_000_000, bytes_accessed=2_000_000, transcendentals=0
        ),
    )(coeff, images)


def rounded(value):
    return value.astype(jnp.bfloat16)


def far_kernel(own_ref, near_a, near_b, near_c, half_ref, out_ref, block):
    n = own_ref.shape[0]
    part = own_ref[...] + sum(ref[...].astype(jnp.float32) for ref in (near_a, near_b, near_c))
    block[:, :ROWS, :MAIN] = part[:, :ROWS]
    block[:, ROWS:, :] = jnp.zeros((n, STEP, WIDTH), jnp.float32)
    for rows, cols, place in PIECES:
        block[:, rows, MAIN + cols.start : MAIN + cols.stop] = part[:, ROWS:, place]
    half = half_ref[...].astype(jnp.float32).reshape(n, TALL, WIDTH)

    along = jnp.sum(block[...] * half, axis=2, keepdims=True)
    lane = lax.broadcasted_iota(jnp.int32, (n, STEP, 128), 2)
    spare = slice(6 * 128, 7 * 128)

    def store(factor, first):
        held = out_ref[:, ROWS:, spare]
        for m in range(ROWS // STEP):
            piece = rounded(jnp.broadcast_to(factor[:, m * STEP : (m + 1) * STEP], lane.shape))
            held = jnp.where(lane == first + m, piece, held)
        out_ref[:, ROWS:, spare] = held

    def load(first):
        held = out_ref[:, ROWS:, spare].astype(jnp.float32)
        return [
            jnp.sum(jnp.where(lane == first + m, held, 0.0), axis=2, keepdims=True)
            for m in range(ROWS // STEP)
        ]

    out_ref[:, ROWS:, :] = jnp.zeros((n, STEP, WIDE), jnp.bfloat16)
    store(along, 0)
    for m, factor in enumerate(load(0)):
        rows = slice(m * STEP, (m + 1) * STEP)
        block[:, rows, :] = block[:, rows, :] - factor * half[:, rows]
    mean = jnp.sum(block[...], axis=1, keepdims=True) * (1.0 / ROWS)
    mean = rounded(mean).astype(jnp.float32)
    size = jnp.sum(mean * mean, axis=2, keepdims=True)
    along = jnp.sum(block[...] * mean, axis=2, keepdims=True)
    store(jnp.where(size > 0.0, along / jnp.where(size > 0.0, size, 1.0), 0.0), 4)
    for j in range(WIDTH // 128):
        row = ROWS + j % STEP
        cols = slice((3 + j // STEP) * 128, (4 + j // STEP) * 128)
        out_ref[:, row : row + 1, cols] = rounded(mean[:, :, j * 128 : (j + 1) * 128])
    for m, factor in enumerate(load(4)):
        rows = slice(m * STEP, (m + 1) * STEP)
        left = block[:, rows, :] - factor * mean
        block[:, rows, :] = left
    out_ref[:, :ROWS, :] = rounded(block[:, :ROWS, :WIDE])
    for m in range(ROWS // STEP):
        rows = slice(m * STEP, (m + 1) * STEP)
        out_ref[:, ROWS:, m * 128 : (m + 1) * 128] = rounded(block[:, rows, WIDE:])


def far_message(own, near, half):
    n = own.shape[0]
    return pl.pallas_call(
        far_kernel,
        out_shape=jax.ShapeDtypeStruct((n, TALL, WIDE), jnp.bfloat16),
        scratch_shapes=[pltpu.VMEM((n, TALL, WIDTH), jnp.float32)],
        compiler_params=pltpu.CompilerParams(vmem_limit_bytes=VMEM),
        cost_estimate=pl.CostEstimate(flops=500_000, bytes_accessed=1_000_000, transcendentals=0),
    )(own, *near, half)


def project(direction, unit, inverse):
    along = jnp.sum(unit * direction, axis=1, keepdims=True)
    return (direction - unit * along) * inverse


def finish_images_kernel(unit_ref, inverse_ref, back_ref, out_ref, block):
    total = jnp.sum(back_ref[...].astype(jnp.float32), axis=0)
    block[:, :MAIN] = total[:ROWS]
    for rows, cols, place in PIECES:
        block[rows, MAIN + cols.start : MAIN + cols.stop] = total[ROWS:, place]
    out_ref[...] = project(block[...], unit_ref[...], inverse_ref[...])


def finish_texts_kernel(unit_ref, inverse_ref, half_ref, back_ref, out_ref, block):
    back = back_ref[...].astype(jnp.float32)
    total = jnp.sum(back, axis=0)
    block[:, :WIDE] = total[:ROWS]
    spare = back[:, ROWS:, 6 * 128 : 7 * 128]
    lane = lax.broadcasted_iota(jnp.int32, spare.shape, 2)
    means = [
        back[:, ROWS + j % STEP : ROWS + j % STEP + 1, (3 + j // STEP) * 128 : (4 + j // STEP) * 128]
        for j in range(WIDTH // 128)
    ]
    for m in range(ROWS // STEP):
        rows = slice(m * STEP, (m + 1) * STEP)
        block[rows, WIDE:] = total[ROWS:, m * 128 : (m + 1) * 128]
        own = jnp.sum(jnp.where(lane == m, spare, 0.0), axis=2, keepdims=True)
        mean = jnp.sum(jnp.where(lane == 4 + m, spare, 0.0), axis=2, keepdims=True)
        block[rows, :] += jnp.sum(own, axis=0) * half_ref[rows, :].astype(jnp.float32)
        for j, piece in enumerate(means):
            block[rows, j * 128 : (j + 1) * 128] += jnp.sum(mean * piece, axis=0)
    out_ref[...] = project(block[...], unit_ref[...], inverse_ref[...])


def finish(kernel, unit, *operands):
    return pl.pallas_call(
        kernel,
        out_shape=jax.ShapeDtypeStruct(unit.shape, jnp.float32),
        scratch_shapes=[pltpu.VMEM((ROWS, WIDTH), jnp.float32)],
        compiler_params=pltpu.CompilerParams(vmem_limit_bytes=VMEM),
        cost_estimate=pl.CostEstimate(flops=500_000, bytes_accessed=1_000_000, transcendentals=0),
    )(unit, *operands)


def along_z(value, move):
    def spot(z):
        return (z // 4 % 2) * 8 + (z % 4) * 2 + z // 8

    return lax.ppermute(value, LINE, [(spot(z), spot(move(z) % 16)) for z in range(16)])


def across(value):
    return lax.ppermute(value, "core", [(0, 1), (1, 0)])


NEAR = (
    (lambda z: z + 1, lambda z: z - 1),
    (lambda z: z - 1, lambda z: z + 1),
    (lambda z: z + 2 - 4 * (z % 2), lambda z: z + 2 - 4 * (z % 2)),
)


def on_device(image_embeds, text_embeds, log_temp, bias):
    place = jnp.stack([lax.axis_index(PLANE), lax.axis_index(FAR)]).astype(jnp.int32)

    own, txt_unit, txt_inv, txt_half = spread(text_embeds, lax.axis_size(FAR))
    own = lax.all_to_all(own, FAR, 0, 0)
    sent, img_unit, img_inv, _ = spread(image_embeds, lax.axis_size(PLANE))
    sent, own = lax.optimization_barrier((sent, own))
    images = lax.all_to_all(sent, PLANE, 0, 0)
    images = [images, across(images)]
    texts = [own] + [along_z(own, there) for there, _ in NEAR]

    coeff, whole, half, image_part, core_part = image_terms(log_temp, bias, place, images, texts)
    image_part = (image_part + across(core_part).astype(jnp.float32)).astype(jnp.bfloat16)
    image_back = lax.all_to_all(image_part, PLANE, 0, 0)
    part, *near_parts = text_terms(coeff, whole)
    near = [along_z(near_part, home) for near_part, (_, home) in zip(near_parts, NEAR)]
    message, image_back = lax.optimization_barrier((far_message(part, near, half), image_back))
    text_back = lax.all_to_all(message, FAR, 0, 0)
    return (
        finish(finish_images_kernel, img_unit, img_inv, image_back),
        finish(finish_texts_kernel, txt_unit, txt_inv, txt_half, text_back),
    )


def solution(mesh):
    fine = Mesh(mesh.devices.reshape(SIZES), AXES)
    split = P(AXES, None)
    return jax.shard_map(
        on_device,
        mesh=fine,
        in_specs=(split, split, P(), P()),
        out_specs=(split, split),
        check_vma=False,
    )
```

```python
import jax
import jax.numpy as jnp
from jax import lax
from jax.experimental import pallas as pl
from jax.experimental.pallas import tpu as pltpu
from jax.sharding import Mesh, PartitionSpec as P

EPS = 1e-06
AXES = ("x", "zm", "zn", "core", "zh", "y")
SIZES = (4, 2, 4, 2, 2, 4)
PLANE = ("x", "y")
LINE = ("zm", "zn", "zh")
FAR = ("zm", "zh")
VMEM = 48 * 1024 * 1024

ROWS = 12
WIDTH = 1152
TALL = 16
MAIN = 896
REST = WIDTH - MAIN
STEP = TALL - ROWS
PIECES = [
    (
        slice(m * STEP, (m + 1) * STEP),
        slice(g * 128, (g + 1) * 128),
        slice((3 * g + m) * 128, (3 * g + m + 1) * 128),
    )
    for g in range(REST // 128)
    for m in range(ROWS // STEP)
]

WIDE = 1024


def spread_kernel(emb_ref, out_ref, unit_ref, inverse_ref, half_ref, block):
    wide = emb_ref[...].astype(jnp.float32)
    inverse = lax.rsqrt(jnp.sum(wide * wide, axis=1, keepdims=True) + EPS)
    unit_ref[...] = wide * inverse
    inverse_ref[...] = inverse
    half_ref[...] = unit_ref[...].astype(jnp.bfloat16)
    block[:ROWS, :] = unit_ref[:, :MAIN]
    block[ROWS:, :] = jnp.zeros((STEP, MAIN), jnp.float32)
    for rows, cols, place in PIECES:
        block[ROWS:, place] = unit_ref[rows, MAIN + cols.start : MAIN + cols.stop]
    out_ref[...] = jnp.broadcast_to(block[...].astype(jnp.bfloat16)[None], out_ref.shape)


def spread(emb, peers):
    return pl.pallas_call(
        spread_kernel,
        out_shape=[
            jax.ShapeDtypeStruct((peers, TALL, MAIN), jnp.bfloat16),
            jax.ShapeDtypeStruct(emb.shape, jnp.float32),
            jax.ShapeDtypeStruct((ROWS, 1), jnp.float32),
            jax.ShapeDtypeStruct(emb.shape, jnp.bfloat16),
        ],
        scratch_shapes=[pltpu.VMEM((TALL, MAIN), jnp.float32)],
        compiler_params=pltpu.CompilerParams(vmem_limit_bytes=VMEM),
        cost_estimate=pl.CostEstimate(flops=100_000, bytes_accessed=1_000_000, transcendentals=0),
    )(emb)


def packed(main, rest, n):
    for rows, cols, place in PIECES:
        main[:n, ROWS:, place] = rest[:n, rows, cols]
    return main[:n]


def text_kernel(temp_ref, bias_ref, place_ref, images_ref, *refs):
    text_refs = refs[:4]
    coeff_ref, texts = refs[4:6]
    outs = refs[6:10]
    images, rest, main = refs[10:]
    rest[:, ROWS:, :] = jnp.zeros((rest.shape[0], STEP, REST), jnp.float32)
    first = [0]
    for ref in text_refs:
        first.append(first[-1] + ref.shape[0])
    groups = [(images, 0, images_ref)] + [(texts, i, ref) for i, ref in zip(first, text_refs)]
    for whole, start, ref in groups:
        n = ref.shape[0]
        span = pl.ds(start * TALL, n * TALL)
        whole[span, :MAIN] = ref[...].reshape(n * TALL, MAIN)
        for rows, cols, place in PIECES:
            rest[:n, rows, cols] = ref[:, ROWS:, place].astype(jnp.float32)
        whole[span, MAIN:] = rest[:n].reshape(n * TALL, REST).astype(jnp.bfloat16)

    scale = jnp.exp(jnp.full((1, 1), temp_ref[0], jnp.float32))
    logits = (
        scale
        * lax.dot_general(
            images[...], texts[...], (((1,), (1,)), ((), ())), preferred_element_type=jnp.float32
        )
        + bias_ref[0]
    )
    row = lax.broadcasted_iota(jnp.int32, logits.shape, 0)
    col = lax.broadcasted_iota(jnp.int32, logits.shape, 1)
    row_in, col_in = row % TALL, col % TALL
    real = (row_in < ROWS) & (col_in < ROWS)
    same = (row - place_ref[0] * TALL == row_in) & (col - place_ref[1] * TALL == col_in)
    same = same & (row_in == col_in)
    sig = jax.nn.sigmoid(jnp.where(same, -logits, logits))
    coeff = jnp.where(real, jnp.where(same, -sig, sig) * scale, 0.0).astype(jnp.bfloat16)
    coeff_ref[...] = coeff

    n = first[-1]
    flip = (((0,), (0,)), ((), ()))
    main[...] = lax.dot_general(
        coeff, images[:, :MAIN], flip, preferred_element_type=jnp.float32
    ).reshape(n, TALL, MAIN)
    rest[:n] = lax.dot_general(
        coeff, images[:, MAIN:], flip, preferred_element_type=jnp.float32
    ).reshape(n, TALL, REST)
    packed(main, rest, n)
    for start, out in zip(first, outs):
        out[...] = main[start : start + out.shape[0]].astype(out.dtype)


def text_terms(log_temp, bias, place, images, texts):
    n_images, n_texts = images.shape[0], sum(text.shape[0] for text in texts)
    return pl.pallas_call(
        text_kernel,
        in_specs=[pl.BlockSpec(memory_space=pltpu.SMEM)] * 3
        + [pl.BlockSpec(memory_space=pltpu.VMEM)] * (1 + len(texts)),
        out_shape=[
            jax.ShapeDtypeStruct((n_images * TALL, n_texts * TALL), jnp.bfloat16),
            jax.ShapeDtypeStruct((n_texts * TALL, WIDTH), jnp.bfloat16),
            jax.ShapeDtypeStruct(texts[0].shape, jnp.float32),
        ]
        + [jax.ShapeDtypeStruct(text.shape, jnp.bfloat16) for text in texts[1:]],
        scratch_shapes=[
            pltpu.VMEM((n_images * TALL, WIDTH), jnp.bfloat16),
            pltpu.VMEM((n_images, TALL, REST), jnp.float32),
            pltpu.VMEM((n_texts, TALL, MAIN), jnp.float32),
        ],
        compiler_params=pltpu.CompilerParams(vmem_limit_bytes=VMEM),
        cost_estimate=pl.CostEstimate(
            flops=600_000_000, bytes_accessed=4_000_000, transcendentals=131_072
        ),
    )(log_temp, bias, place, images, *texts)


def image_kernel(coeff_ref, texts_ref, out_ref, rest, main):
    n = out_ref.shape[0]
    coeff = coeff_ref[...]
    main[...] = jnp.dot(
        coeff, texts_ref[:, :MAIN], preferred_element_type=jnp.float32
    ).reshape(n, TALL, MAIN)
    rest[...] = jnp.dot(
        coeff, texts_ref[:, MAIN:], preferred_element_type=jnp.float32
    ).reshape(n, TALL, REST)
    out_ref[...] = packed(main, rest, n).astype(jnp.bfloat16)


def image_terms(coeff, texts):
    n = coeff.shape[0] // TALL
    return pl.pallas_call(
        image_kernel,
        out_shape=jax.ShapeDtypeStruct((n, TALL, MAIN), jnp.bfloat16),
        scratch_shapes=[
            pltpu.VMEM((n, TALL, REST), jnp.float32),
            pltpu.VMEM((n, TALL, MAIN), jnp.float32),
        ],
        compiler_params=pltpu.CompilerParams(vmem_limit_bytes=VMEM),
        cost_estimate=pl.CostEstimate(
            flops=300_000_000, bytes_accessed=2_000_000, transcendentals=0
        ),
    )(coeff, texts)


def rounded(value):
    return value.astype(jnp.bfloat16)


def far_kernel(own_ref, near_a, near_b, near_c, half_ref, out_ref, block):
    n = own_ref.shape[0]
    part = own_ref[...] + sum(ref[...].astype(jnp.float32) for ref in (near_a, near_b, near_c))
    block[:, :ROWS, :MAIN] = part[:, :ROWS]
    block[:, ROWS:, :] = jnp.zeros((n, STEP, WIDTH), jnp.float32)
    for rows, cols, place in PIECES:
        block[:, rows, MAIN + cols.start : MAIN + cols.stop] = part[:, ROWS:, place]
    half = half_ref[: n * TALL, :].astype(jnp.float32).reshape(n, TALL, WIDTH)

    along = jnp.sum(block[...] * half, axis=2, keepdims=True)
    lane = lax.broadcasted_iota(jnp.int32, (n, STEP, 128), 2)
    spare = slice(6 * 128, 7 * 128)

    def store(factor, first):
        held = out_ref[:, ROWS:, spare]
        for m in range(ROWS // STEP):
            piece = rounded(jnp.broadcast_to(factor[:, m * STEP : (m + 1) * STEP], lane.shape))
            held = jnp.where(lane == first + m, piece, held)
        out_ref[:, ROWS:, spare] = held

    def load(first):
        held = out_ref[:, ROWS:, spare].astype(jnp.float32)
        return [
            jnp.sum(jnp.where(lane == first + m, held, 0.0), axis=2, keepdims=True)
            for m in range(ROWS // STEP)
        ]

    out_ref[:, ROWS:, :] = jnp.zeros((n, STEP, WIDE), jnp.bfloat16)
    store(along, 0)
    for m, factor in enumerate(load(0)):
        rows = slice(m * STEP, (m + 1) * STEP)
        block[:, rows, :] = block[:, rows, :] - factor * half[:, rows]
    mean = jnp.sum(block[...], axis=1, keepdims=True) * (1.0 / ROWS)
    mean = rounded(mean).astype(jnp.float32)
    size = jnp.sum(mean * mean, axis=2, keepdims=True)
    along = jnp.sum(block[...] * mean, axis=2, keepdims=True)
    store(jnp.where(size > 0.0, along / jnp.where(size > 0.0, size, 1.0), 0.0), 4)
    for j in range(WIDTH // 128):
        row = ROWS + j % STEP
        cols = slice((3 + j // STEP) * 128, (4 + j // STEP) * 128)
        out_ref[:, row : row + 1, cols] = rounded(mean[:, :, j * 128 : (j + 1) * 128])
    for m, factor in enumerate(load(4)):
        rows = slice(m * STEP, (m + 1) * STEP)
        left = block[:, rows, :] - factor * mean
        block[:, rows, :] = left
    out_ref[:, :ROWS, :] = rounded(block[:, :ROWS, :WIDE])
    for m in range(ROWS // STEP):
        rows = slice(m * STEP, (m + 1) * STEP)
        out_ref[:, ROWS:, m * 128 : (m + 1) * 128] = rounded(block[:, rows, WIDE:])


def far_message(own, near, half):
    n = own.shape[0]
    return pl.pallas_call(
        far_kernel,
        out_shape=jax.ShapeDtypeStruct((n, TALL, WIDE), jnp.bfloat16),
        scratch_shapes=[pltpu.VMEM((n, TALL, WIDTH), jnp.float32)],
        compiler_params=pltpu.CompilerParams(vmem_limit_bytes=VMEM),
        cost_estimate=pl.CostEstimate(flops=500_000, bytes_accessed=1_000_000, transcendentals=0),
    )(own, *near, half)


def project(direction, unit, inverse):
    along = jnp.sum(unit * direction, axis=1, keepdims=True)
    return (direction - unit * along) * inverse


def finish_images_kernel(unit_ref, inverse_ref, back_ref, out_ref, block):
    total = jnp.sum(back_ref[...].astype(jnp.float32), axis=0)
    block[:, :MAIN] = total[:ROWS]
    for rows, cols, place in PIECES:
        block[rows, MAIN + cols.start : MAIN + cols.stop] = total[ROWS:, place]
    out_ref[...] = project(block[...], unit_ref[...], inverse_ref[...])


def finish_texts_kernel(unit_ref, inverse_ref, half_ref, back_ref, out_ref, block):
    back = back_ref[...].astype(jnp.float32)
    total = jnp.sum(back, axis=0)
    block[:, :WIDE] = total[:ROWS]
    spare = back[:, ROWS:, 6 * 128 : 7 * 128]
    lane = lax.broadcasted_iota(jnp.int32, spare.shape, 2)
    means = [
        back[:, ROWS + j % STEP : ROWS + j % STEP + 1, (3 + j // STEP) * 128 : (4 + j // STEP) * 128]
        for j in range(WIDTH // 128)
    ]
    for m in range(ROWS // STEP):
        rows = slice(m * STEP, (m + 1) * STEP)
        block[rows, WIDE:] = total[ROWS:, m * 128 : (m + 1) * 128]
        own = jnp.sum(jnp.where(lane == m, spare, 0.0), axis=2, keepdims=True)
        mean = jnp.sum(jnp.where(lane == 4 + m, spare, 0.0), axis=2, keepdims=True)
        block[rows, :] += jnp.sum(own, axis=0) * half_ref[rows, :].astype(jnp.float32)
        for j, piece in enumerate(means):
            block[rows, j * 128 : (j + 1) * 128] += jnp.sum(mean * piece, axis=0)
    out_ref[...] = project(block[...], unit_ref[...], inverse_ref[...])


def finish(kernel, unit, *operands):
    return pl.pallas_call(
        kernel,
        out_shape=jax.ShapeDtypeStruct(unit.shape, jnp.float32),
        scratch_shapes=[pltpu.VMEM((ROWS, WIDTH), jnp.float32)],
        compiler_params=pltpu.CompilerParams(vmem_limit_bytes=VMEM),
        cost_estimate=pl.CostEstimate(flops=500_000, bytes_accessed=1_000_000, transcendentals=0),
    )(unit, *operands)


def along_z(value, move):
    def spot(z):
        return (z // 4 % 2) * 8 + (z % 4) * 2 + z // 8

    return lax.ppermute(value, LINE, [(spot(z), spot(move(z) % 16)) for z in range(16)])


NEAR = (
    (lambda z: z + 1, lambda z: z - 1),
    (lambda z: z - 1, lambda z: z + 1),
    (lambda z: z + 2 - 4 * (z % 2), lambda z: z + 2 - 4 * (z % 2)),
)


def across(value):
    return lax.ppermute(value, "core", [(0, 1), (1, 0)])


def on_device(image_embeds, text_embeds, log_temp, bias):
    place = jnp.stack([2 * lax.axis_index(PLANE), lax.axis_index(FAR)]).astype(jnp.int32)
    chips = lax.axis_size(PLANE)

    own, txt_unit, txt_inv, txt_half = spread(text_embeds, lax.axis_size(FAR))
    own = lax.all_to_all(own, FAR, 0, 0)
    sent, img_unit, img_inv, _ = spread(image_embeds, 1)
    sent = jnp.concatenate([sent, across(sent)], axis=0)
    sent = jnp.broadcast_to(sent[None], (chips,) + sent.shape)
    sent, own = lax.optimization_barrier((sent, own))
    images = lax.all_to_all(sent, PLANE, 0, 0).reshape((2 * chips,) + sent.shape[2:])
    texts = [own] + [along_z(own, there) for there, _ in NEAR]

    coeff, whole, part, *near_parts = text_terms(log_temp, bias, place, images, texts)
    image_part = image_terms(coeff, whole)
    image_back = lax.all_to_all(
        image_part.reshape((chips, 2) + image_part.shape[1:]), PLANE, 0, 0
    )
    near = [along_z(near_part, home) for near_part, (_, home) in zip(near_parts, NEAR)]
    message, image_back = lax.optimization_barrier((far_message(part, near, whole), image_back))
    text_back = lax.all_to_all(message, FAR, 0, 0)
    image_sum = jnp.sum(image_back.astype(jnp.float32), axis=0)
    image_sum = jnp.stack([image_sum[0], across(image_sum[1])], axis=0)
    return (
        finish(finish_images_kernel, img_unit, img_inv, image_sum),
        finish(finish_texts_kernel, txt_unit, txt_inv, txt_half, text_back),
    )


def solution(mesh):
    fine = Mesh(mesh.devices.reshape(SIZES), AXES)
    split = P(AXES, None)
    return jax.shard_map(
        on_device,
        mesh=fine,
        in_specs=(split, split, P(), P()),
        out_specs=(split, split),
        check_vma=False,
    )
```

```python
import jax
import jax.numpy as jnp
from jax import lax
from jax.experimental import pallas as pl
from jax.experimental.pallas import tpu as pltpu
from jax.sharding import Mesh, PartitionSpec as P

EPS = 1e-06
AXES = ("x", "zm", "zn", "core", "zh", "y")
SIZES = (4, 2, 4, 2, 2, 4)
PLANE = ("x", "y")
LINE = ("zm", "zn", "zh")
FAR_AXES = ("zm", "zh")
FAR = (0, 4, 12, 8)
VMEM = 48 * 1024 * 1024

ROWS = 12
WIDTH = 1152
TALL = 16
MAIN = 896
REST = WIDTH - MAIN
STEP = TALL - ROWS
PIECES = [
    (
        slice(m * STEP, (m + 1) * STEP),
        slice(g * 128, (g + 1) * 128),
        slice((3 * g + m) * 128, (3 * g + m + 1) * 128),
    )
    for g in range(REST // 128)
    for m in range(ROWS // STEP)
]

WIDE = 1024


def spread_kernel(emb_ref, out_ref, unit_ref, inverse_ref, half_ref, block):
    wide = emb_ref[...].astype(jnp.float32)
    inverse = lax.rsqrt(jnp.sum(wide * wide, axis=1, keepdims=True) + EPS)
    unit_ref[...] = wide * inverse
    inverse_ref[...] = inverse
    half_ref[...] = unit_ref[...].astype(jnp.bfloat16)
    block[:ROWS, :] = unit_ref[:, :MAIN]
    block[ROWS:, :] = jnp.zeros((STEP, MAIN), jnp.float32)
    for rows, cols, place in PIECES:
        block[ROWS:, place] = unit_ref[rows, MAIN + cols.start : MAIN + cols.stop]
    out_ref[...] = jnp.broadcast_to(block[...].astype(jnp.bfloat16)[None], out_ref.shape)


def spread(emb, peers):
    return pl.pallas_call(
        spread_kernel,
        out_shape=[
            jax.ShapeDtypeStruct((peers, TALL, MAIN), jnp.bfloat16),
            jax.ShapeDtypeStruct(emb.shape, jnp.float32),
            jax.ShapeDtypeStruct((ROWS, 1), jnp.float32),
            jax.ShapeDtypeStruct(emb.shape, jnp.bfloat16),
        ],
        scratch_shapes=[pltpu.VMEM((TALL, MAIN), jnp.float32)],
        compiler_params=pltpu.CompilerParams(vmem_limit_bytes=VMEM),
        cost_estimate=pl.CostEstimate(flops=100_000, bytes_accessed=1_000_000, transcendentals=0),
    )(emb)


def packed(main, rest, n):
    for rows, cols, place in PIECES:
        main[:n, ROWS:, place] = rest[:n, rows, cols]
    return main[:n]


def line_place(z):
    return (z // 4 % 2) * 8 + (z % 4) * 2 + z // 8


def near_moves(z):
    return (0, 1, -1, 2 - 4 * (z % 2))


def text_kernel(temp_ref, bias_ref, place_ref, *refs):
    image_refs, text_refs = refs[:2], refs[2:6]
    coeff_ref, texts, half_out = refs[6:9]
    outs = refs[9:13]
    image_rest, rest, main = refs[13:]
    chips, far = image_refs[0].shape[0], text_refs[0].shape[0]
    rest[:, ROWS:, :] = jnp.zeros((rest.shape[0], STEP, REST), jnp.float32)

    def gather_rest(ref, out, start):
        n = ref.shape[0]
        for rows, cols, place in PIECES:
            rest[:n, rows, cols] = ref[:, ROWS:, place].astype(jnp.float32)
        out[pl.ds(start * TALL, n * TALL), -REST:] = rounded(rest[:n].reshape(n * TALL, REST))

    for i, ref in enumerate(text_refs):
        texts[pl.ds(i * far * TALL, far * TALL), :MAIN] = ref[...].reshape(far * TALL, MAIN)
        gather_rest(ref, texts, i * far)
    for i, ref in enumerate(image_refs):
        gather_rest(ref, image_rest, i * chips)

    def dot(a, b, dims):
        return lax.dot_general(a, b, ((dims[:1], dims[1:]), ((), ())), preferred_element_type=jnp.float32)

    scale = jnp.exp(jnp.full((1, 1), temp_ref[0], jnp.float32))
    mains = [ref[...].reshape(chips * TALL, MAIN) for ref in image_refs]
    parts = []
    for i, image_main in enumerate(mains):
        span = slice(i * chips * TALL, (i + 1) * chips * TALL)
        logits = dot(image_main, texts[:, :MAIN], (1, 1))
        logits += dot(image_rest[span, :], texts[:, MAIN:], (1, 1))
        logits = scale * logits + bias_ref[0]
        row = lax.broadcasted_iota(jnp.int32, logits.shape, 0)
        col = lax.broadcasted_iota(jnp.int32, logits.shape, 1)
        real = (row % TALL < ROWS) & (col % TALL < ROWS)
        if i == 0:
            same = (row == col + place_ref[0] * TALL) & (col < TALL)
            sig = jax.nn.sigmoid(jnp.where(same, -logits, logits))
            sig = jnp.where(same, -sig, sig)
        else:
            sig = jax.nn.sigmoid(logits)
        coeff = rounded(jnp.where(real, sig * scale, 0.0))
        coeff_ref[span, :] = coeff
        parts.append(coeff)

    n = main.shape[0]
    total = sum(dot(coeff, image_main, (0, 0)) for coeff, image_main in zip(parts, mains))
    main[...] = total.reshape(n, TALL, MAIN)
    rest[:n] = dot(coeff_ref[...], image_rest[...], (0, 0)).reshape(n, TALL, REST)
    packed(main, rest, n)
    z = place_ref[1]
    for i, near in enumerate(near_moves(z)):
        for j, by in enumerate(FAR):
            source = (z - near - by + 32) % 16
            slot = source // 4 % 2 * 2 + source // 8
            outs[i][slot] = main[i * far + j].astype(outs[i].dtype)
            if i == 0:
                half_out[slot] = texts[j * TALL : (j + 1) * TALL, :]


def text_terms(log_temp, bias, place, images, texts):
    n_images, n_texts = 2 * images[0].shape[0], 4 * texts[0].shape[0]
    return pl.pallas_call(
        text_kernel,
        in_specs=[pl.BlockSpec(memory_space=pltpu.SMEM)] * 3
        + [pl.BlockSpec(memory_space=pltpu.VMEM)] * 6,
        out_shape=[
            jax.ShapeDtypeStruct((n_images * TALL, n_texts * TALL), jnp.bfloat16),
            jax.ShapeDtypeStruct((n_texts * TALL, WIDTH), jnp.bfloat16),
            jax.ShapeDtypeStruct((n_texts // 4, TALL, WIDTH), jnp.bfloat16),
            jax.ShapeDtypeStruct((n_texts // 4, TALL, MAIN), jnp.float32),
        ]
        + [jax.ShapeDtypeStruct((n_texts // 4, TALL, MAIN), jnp.bfloat16)] * 3,
        scratch_shapes=[
            pltpu.VMEM((n_images * TALL, REST), jnp.bfloat16),
            pltpu.VMEM((n_images // 2, TALL, REST), jnp.float32),
            pltpu.VMEM((n_texts, TALL, MAIN), jnp.float32),
        ],
        compiler_params=pltpu.CompilerParams(vmem_limit_bytes=VMEM),
        cost_estimate=pl.CostEstimate(
            flops=600_000_000, bytes_accessed=4_000_000, transcendentals=131_072
        ),
    )(log_temp, bias, place, *images, *texts)


def image_kernel(coeff_ref, texts_ref, out_ref, rest, main):
    n = main.shape[0]
    coeff = coeff_ref[...]
    main[...] = jnp.dot(
        coeff, texts_ref[:, :MAIN], preferred_element_type=jnp.float32
    ).reshape(n, TALL, MAIN)
    rest[...] = jnp.dot(
        coeff, texts_ref[:, MAIN:], preferred_element_type=jnp.float32
    ).reshape(n, TALL, REST)
    packed(main, rest, n)
    out_ref[:, 0] = rounded(main[: n // 2])
    out_ref[:, 1] = rounded(main[n // 2 :])


def image_terms(coeff, texts):
    n = coeff.shape[0] // TALL
    return pl.pallas_call(
        image_kernel,
        out_shape=jax.ShapeDtypeStruct((n // 2, 2, TALL, MAIN), jnp.bfloat16),
        scratch_shapes=[
            pltpu.VMEM((n, TALL, REST), jnp.float32),
            pltpu.VMEM((n, TALL, MAIN), jnp.float32),
        ],
        compiler_params=pltpu.CompilerParams(vmem_limit_bytes=VMEM),
        cost_estimate=pl.CostEstimate(
            flops=300_000_000, bytes_accessed=2_000_000, transcendentals=0
        ),
    )(coeff, texts)


def rounded(value):
    return value.astype(jnp.bfloat16)


def far_kernel(own_ref, near_a, near_b, near_c, half_ref, out_ref, block):
    n = own_ref.shape[0]
    part = own_ref[...] + sum(ref[...].astype(jnp.float32) for ref in (near_a, near_b, near_c))
    block[:, :ROWS, :MAIN] = part[:, :ROWS]
    block[:, ROWS:, :] = jnp.zeros((n, STEP, WIDTH), jnp.float32)
    for rows, cols, place in PIECES:
        block[:, rows, MAIN + cols.start : MAIN + cols.stop] = part[:, ROWS:, place]
    half = half_ref[...].astype(jnp.float32)

    along = jnp.sum(block[...] * half, axis=2, keepdims=True)
    lane = lax.broadcasted_iota(jnp.int32, (n, STEP, 128), 2)
    spare = slice(6 * 128, 7 * 128)

    def store(factor, first):
        held = out_ref[:, ROWS:, spare]
        for m in range(ROWS // STEP):
            piece = rounded(jnp.broadcast_to(factor[:, m * STEP : (m + 1) * STEP], lane.shape))
            held = jnp.where(lane == first + m, piece, held)
        out_ref[:, ROWS:, spare] = held

    def load(first):
        held = out_ref[:, ROWS:, spare].astype(jnp.float32)
        return [
            jnp.sum(jnp.where(lane == first + m, held, 0.0), axis=2, keepdims=True)
            for m in range(ROWS // STEP)
        ]

    out_ref[:, ROWS:, :] = jnp.zeros((n, STEP, WIDE), jnp.bfloat16)
    store(along, 0)
    for m, factor in enumerate(load(0)):
        rows = slice(m * STEP, (m + 1) * STEP)
        block[:, rows, :] = block[:, rows, :] - factor * half[:, rows]
    mean = jnp.sum(block[...], axis=1, keepdims=True) * (1.0 / ROWS)
    mean = rounded(mean).astype(jnp.float32)
    size = jnp.sum(mean * mean, axis=2, keepdims=True)
    along = jnp.sum(block[...] * mean, axis=2, keepdims=True)
    store(jnp.where(size > 0.0, along / jnp.where(size > 0.0, size, 1.0), 0.0), 4)
    for j in range(WIDTH // 128):
        row = ROWS + j % STEP
        cols = slice((3 + j // STEP) * 128, (4 + j // STEP) * 128)
        out_ref[:, row : row + 1, cols] = rounded(mean[:, :, j * 128 : (j + 1) * 128])
    for m, factor in enumerate(load(4)):
        rows = slice(m * STEP, (m + 1) * STEP)
        left = block[:, rows, :] - factor * mean
        block[:, rows, :] = left
    out_ref[:, :ROWS, :] = rounded(block[:, :ROWS, :WIDE])
    for m in range(ROWS // STEP):
        rows = slice(m * STEP, (m + 1) * STEP)
        out_ref[:, ROWS:, m * 128 : (m + 1) * 128] = rounded(block[:, rows, WIDE:])


def far_message(own, near, half):
    n = own.shape[0]
    return pl.pallas_call(
        far_kernel,
        out_shape=jax.ShapeDtypeStruct((n, TALL, WIDE), jnp.bfloat16),
        scratch_shapes=[pltpu.VMEM((n, TALL, WIDTH), jnp.float32)],
        compiler_params=pltpu.CompilerParams(vmem_limit_bytes=VMEM),
        cost_estimate=pl.CostEstimate(flops=500_000, bytes_accessed=1_000_000, transcendentals=0),
    )(own, *near, half)


def project(direction, unit, inverse):
    along = jnp.sum(unit * direction, axis=1, keepdims=True)
    return (direction - unit * along) * inverse


def finish_images_kernel(unit_ref, inverse_ref, back_ref, out_ref, block):
    total = jnp.sum(back_ref[...].astype(jnp.float32), axis=0)
    block[:, :MAIN] = total[:ROWS]
    for rows, cols, place in PIECES:
        block[rows, MAIN + cols.start : MAIN + cols.stop] = total[ROWS:, place]
    out_ref[...] = project(block[...], unit_ref[...], inverse_ref[...])


def finish_texts_kernel(unit_ref, inverse_ref, half_ref, back_ref, out_ref, block):
    back = back_ref[...].astype(jnp.float32)
    total = jnp.sum(back, axis=0)
    block[:, :WIDE] = total[:ROWS]
    spare = back[:, ROWS:, 6 * 128 : 7 * 128]
    lane = lax.broadcasted_iota(jnp.int32, spare.shape, 2)
    means = [
        back[:, ROWS + j % STEP : ROWS + j % STEP + 1, (3 + j // STEP) * 128 : (4 + j // STEP) * 128]
        for j in range(WIDTH // 128)
    ]
    for m in range(ROWS // STEP):
        rows = slice(m * STEP, (m + 1) * STEP)
        block[rows, WIDE:] = total[ROWS:, m * 128 : (m + 1) * 128]
        own = jnp.sum(jnp.where(lane == m, spare, 0.0), axis=2, keepdims=True)
        mean = jnp.sum(jnp.where(lane == 4 + m, spare, 0.0), axis=2, keepdims=True)
        block[rows, :] += jnp.sum(own, axis=0) * half_ref[rows, :].astype(jnp.float32)
        for j, piece in enumerate(means):
            block[rows, j * 128 : (j + 1) * 128] += jnp.sum(mean * piece, axis=0)
    out_ref[...] = project(block[...], unit_ref[...], inverse_ref[...])


def finish(kernel, unit, *operands):
    return pl.pallas_call(
        kernel,
        out_shape=jax.ShapeDtypeStruct(unit.shape, jnp.float32),
        scratch_shapes=[pltpu.VMEM((ROWS, WIDTH), jnp.float32)],
        compiler_params=pltpu.CompilerParams(vmem_limit_bytes=VMEM),
        cost_estimate=pl.CostEstimate(flops=500_000, bytes_accessed=1_000_000, transcendentals=0),
    )(unit, *operands)


def along_z(value, move):
    pairs = [(line_place(z), line_place((z + move(z)) % 16)) for z in range(16)]
    return lax.ppermute(value, LINE, pairs)


def across(value):
    return lax.ppermute(value, "core", [(0, 1), (1, 0)])


def on_device(image_embeds, text_embeds, log_temp, bias):
    z = lax.axis_index("zh") * 8 + lax.axis_index("zm") * 4 + lax.axis_index("zn")
    place = jnp.stack([lax.axis_index(PLANE), z]).astype(jnp.int32)
    sent, img_unit, img_inv, _ = spread(image_embeds, lax.axis_size(PLANE))
    own, txt_unit, txt_inv, txt_half = spread(text_embeds, 1)

    images = lax.all_to_all(sent, PLANE, 0, 0)
    images = [images, across(images)]
    own = jnp.concatenate([own] + [along_z(own, lambda z, by=by: by) for by in FAR[1:]], axis=0)
    texts = [own] + [along_z(own, lambda z, i=i: near_moves(z)[i]) for i in (1, 2, 3)]

    coeff, whole, half, part, *near = text_terms(log_temp, bias, place, images, texts)
    image_back = lax.all_to_all(image_terms(coeff, whole), PLANE, 0, 0)
    near = [along_z(value, lambda z, i=i: -near_moves(z)[i]) for i, value in enumerate(near, 1)]
    message, image_back = lax.optimization_barrier((far_message(part, near, half), image_back))
    text_back = lax.all_to_all(message, FAR_AXES, 0, 0)
    image_sum = jnp.sum(image_back.astype(jnp.float32), axis=0)
    image_sum = jnp.stack([image_sum[0], across(image_sum[1])], axis=0)
    return (
        finish(finish_images_kernel, img_unit, img_inv, image_sum),
        finish(finish_texts_kernel, txt_unit, txt_inv, txt_half, text_back),
    )


def solution(mesh):
    fine = Mesh(mesh.devices.reshape(SIZES), AXES)
    split = P(AXES, None)
    return jax.shard_map(
        on_device,
        mesh=fine,
        in_specs=(split, split, P(), P()),
        out_specs=(split, split),
        check_vma=False,
    )
```

```python
import jax
import jax.numpy as jnp
from jax import lax
from jax.experimental import pallas as pl
from jax.experimental.pallas import tpu as pltpu
from jax.sharding import Mesh, PartitionSpec as P

EPS = 1e-06
AXES = ("x", "zm", "zn", "core", "zh", "y")
SIZES = (4, 2, 4, 2, 2, 4)
PLANE = ("x", "y")
LINE = ("zm", "zn", "zh")
FAR_AXES = ("zm", "zh")
FAR = (0, 8, 12, 4)
VMEM = 48 * 1024 * 1024

ROWS = 12
WIDTH = 1152
TALL = 16
MAIN = 896
REST = WIDTH - MAIN
STEP = TALL - ROWS
PIECES = [
    (
        slice(m * STEP, (m + 1) * STEP),
        slice(g * 128, (g + 1) * 128),
        slice((3 * g + m) * 128, (3 * g + m + 1) * 128),
    )
    for g in range(REST // 128)
    for m in range(ROWS // STEP)
]

WIDE = 1024


def spread_kernel(emb_ref, out_ref, unit_ref, inverse_ref, half_ref, block):
    wide = emb_ref[...].astype(jnp.float32)
    inverse = lax.rsqrt(jnp.sum(wide * wide, axis=1, keepdims=True) + EPS)
    unit_ref[...] = wide * inverse
    inverse_ref[...] = inverse
    half_ref[...] = unit_ref[...].astype(jnp.bfloat16)
    block[:ROWS, :] = unit_ref[:, :MAIN]
    block[ROWS:, :] = jnp.zeros((STEP, MAIN), jnp.float32)
    for rows, cols, place in PIECES:
        block[ROWS:, place] = unit_ref[rows, MAIN + cols.start : MAIN + cols.stop]
    out_ref[...] = jnp.broadcast_to(block[...].astype(jnp.bfloat16)[None], out_ref.shape)


def spread(emb, peers):
    return pl.pallas_call(
        spread_kernel,
        out_shape=[
            jax.ShapeDtypeStruct((peers, TALL, MAIN), jnp.bfloat16),
            jax.ShapeDtypeStruct(emb.shape, jnp.float32),
            jax.ShapeDtypeStruct((ROWS, 1), jnp.float32),
            jax.ShapeDtypeStruct(emb.shape, jnp.bfloat16),
        ],
        scratch_shapes=[pltpu.VMEM((TALL, MAIN), jnp.float32)],
        compiler_params=pltpu.CompilerParams(vmem_limit_bytes=VMEM),
        cost_estimate=pl.CostEstimate(flops=100_000, bytes_accessed=1_000_000, transcendentals=0),
    )(emb)


def packed(main, rest, n):
    for rows, cols, place in PIECES:
        main[:n, ROWS:, place] = rest[:n, rows, cols]
    return main[:n]


def line_place(z):
    return (z // 4 % 2) * 8 + (z % 4) * 2 + z // 8


def near_moves(z):
    return (0, 1, -1, 2 - 4 * (z % 2))


def text_kernel(temp_ref, bias_ref, place_ref, *refs):
    image_refs, text_refs = refs[:2], refs[2:6]
    coeff_ref, texts, half_out = refs[6:9]
    outs = refs[9:13]
    image_rest, rest, main = refs[13:]
    chips, far = image_refs[0].shape[0], text_refs[0].shape[0]
    rest[:, ROWS:, :] = jnp.zeros((rest.shape[0], STEP, REST), jnp.float32)

    def gather_rest(ref, out, start):
        n = ref.shape[0]
        for rows, cols, place in PIECES:
            rest[:n, rows, cols] = ref[:, ROWS:, place].astype(jnp.float32)
        out[pl.ds(start * TALL, n * TALL), -REST:] = rounded(rest[:n].reshape(n * TALL, REST))

    for i, ref in enumerate(text_refs):
        texts[pl.ds(i * far * TALL, far * TALL), :MAIN] = ref[...].reshape(far * TALL, MAIN)
        gather_rest(ref, texts, i * far)
    for i, ref in enumerate(image_refs):
        gather_rest(ref, image_rest, i * chips)

    def dot(a, b, dims):
        return lax.dot_general(a, b, ((dims[:1], dims[1:]), ((), ())), preferred_element_type=jnp.float32)

    scale = jnp.exp(jnp.full((1, 1), temp_ref[0], jnp.float32))
    mains = [ref[...].reshape(chips * TALL, MAIN) for ref in image_refs]
    parts = []
    for i, image_main in enumerate(mains):
        span = slice(i * chips * TALL, (i + 1) * chips * TALL)
        logits = dot(image_main, texts[:, :MAIN], (1, 1))
        logits += dot(image_rest[span, :], texts[:, MAIN:], (1, 1))
        logits = scale * logits + bias_ref[0]
        row = lax.broadcasted_iota(jnp.int32, logits.shape, 0)
        col = lax.broadcasted_iota(jnp.int32, logits.shape, 1)
        real = (row % TALL < ROWS) & (col % TALL < ROWS)
        if i == 0:
            same = (row == col + place_ref[0] * TALL) & (col < TALL)
            sig = jax.nn.sigmoid(jnp.where(same, -logits, logits))
            sig = jnp.where(same, -sig, sig)
        else:
            sig = jax.nn.sigmoid(logits)
        coeff = rounded(jnp.where(real, sig * scale, 0.0))
        coeff_ref[span, :] = coeff
        parts.append(coeff)

    n = main.shape[0]
    total = sum(dot(coeff, image_main, (0, 0)) for coeff, image_main in zip(parts, mains))
    main[...] = total.reshape(n, TALL, MAIN)
    rest[:n] = dot(coeff_ref[...], image_rest[...], (0, 0)).reshape(n, TALL, REST)
    packed(main, rest, n)
    z = place_ref[1]
    for i, near in enumerate(near_moves(z)):
        for j, by in enumerate(FAR):
            source = (z - near - by + 32) % 16
            slot = source // 4 % 2 * 2 + source // 8
            outs[i][slot] = main[i * far + j].astype(outs[i].dtype)
            if i == 0:
                half_out[slot] = texts[j * TALL : (j + 1) * TALL, :]


def text_terms(log_temp, bias, place, images, texts):
    n_images, n_texts = 2 * images[0].shape[0], 4 * texts[0].shape[0]
    return pl.pallas_call(
        text_kernel,
        in_specs=[pl.BlockSpec(memory_space=pltpu.SMEM)] * 3
        + [pl.BlockSpec(memory_space=pltpu.VMEM)] * 6,
        out_shape=[
            jax.ShapeDtypeStruct((n_images * TALL, n_texts * TALL), jnp.bfloat16),
            jax.ShapeDtypeStruct((n_texts * TALL, WIDTH), jnp.bfloat16),
            jax.ShapeDtypeStruct((n_texts // 4, TALL, WIDTH), jnp.bfloat16),
            jax.ShapeDtypeStruct((n_texts // 4, TALL, MAIN), jnp.float32),
        ]
        + [jax.ShapeDtypeStruct((n_texts // 4, TALL, MAIN), jnp.bfloat16)] * 3,
        scratch_shapes=[
            pltpu.VMEM((n_images * TALL, REST), jnp.bfloat16),
            pltpu.VMEM((n_images // 2, TALL, REST), jnp.float32),
            pltpu.VMEM((n_texts, TALL, MAIN), jnp.float32),
        ],
        compiler_params=pltpu.CompilerParams(vmem_limit_bytes=VMEM),
        cost_estimate=pl.CostEstimate(
            flops=600_000_000, bytes_accessed=4_000_000, transcendentals=131_072
        ),
    )(log_temp, bias, place, *images, *texts)


def image_kernel(core_ref, coeff_ref, texts_ref, out_ref, rest, main):
    n = main.shape[0]
    coeff = coeff_ref[...]
    main[...] = jnp.dot(
        coeff, texts_ref[:, :MAIN], preferred_element_type=jnp.float32
    ).reshape(n, TALL, MAIN)
    rest[...] = jnp.dot(
        coeff, texts_ref[:, MAIN:], preferred_element_type=jnp.float32
    ).reshape(n, TALL, REST)
    packed(main, rest, n)
    for i in range(n):
        chip = i % (n // 2)
        core = core_ref[0] if i < n // 2 else 1 - core_ref[0]
        out_ref[chip // 4 * 8 + core * 4 + chip % 4] = rounded(main[i])


def image_terms(core, coeff, texts):
    n = coeff.shape[0] // TALL
    return pl.pallas_call(
        image_kernel,
        in_specs=[pl.BlockSpec(memory_space=pltpu.SMEM)]
        + [pl.BlockSpec(memory_space=pltpu.VMEM)] * 2,
        out_shape=jax.ShapeDtypeStruct((n, TALL, MAIN), jnp.bfloat16),
        scratch_shapes=[
            pltpu.VMEM((n, TALL, REST), jnp.float32),
            pltpu.VMEM((n, TALL, MAIN), jnp.float32),
        ],
        compiler_params=pltpu.CompilerParams(vmem_limit_bytes=VMEM),
        cost_estimate=pl.CostEstimate(
            flops=300_000_000, bytes_accessed=2_000_000, transcendentals=0
        ),
    )(core, coeff, texts)


def rounded(value):
    return value.astype(jnp.bfloat16)


def far_kernel(own_ref, near_a, near_b, near_c, half_ref, out_ref, block):
    n = own_ref.shape[0]
    part = own_ref[...] + sum(ref[...].astype(jnp.float32) for ref in (near_a, near_b, near_c))
    block[:, :ROWS, :MAIN] = part[:, :ROWS]
    block[:, ROWS:, :] = jnp.zeros((n, STEP, WIDTH), jnp.float32)
    for rows, cols, place in PIECES:
        block[:, rows, MAIN + cols.start : MAIN + cols.stop] = part[:, ROWS:, place]
    half = half_ref[...].astype(jnp.float32)

    along = jnp.sum(block[...] * half, axis=2, keepdims=True)
    lane = lax.broadcasted_iota(jnp.int32, (n, STEP, 128), 2)
    spare = slice(6 * 128, 7 * 128)

    def store(factor, first):
        held = out_ref[:, ROWS:, spare]
        for m in range(ROWS // STEP):
            piece = rounded(jnp.broadcast_to(factor[:, m * STEP : (m + 1) * STEP], lane.shape))
            held = jnp.where(lane == first + m, piece, held)
        out_ref[:, ROWS:, spare] = held

    def load(first):
        held = out_ref[:, ROWS:, spare].astype(jnp.float32)
        return [
            jnp.sum(jnp.where(lane == first + m, held, 0.0), axis=2, keepdims=True)
            for m in range(ROWS // STEP)
        ]

    out_ref[:, ROWS:, :] = jnp.zeros((n, STEP, WIDE), jnp.bfloat16)
    store(along, 0)
    for m, factor in enumerate(load(0)):
        rows = slice(m * STEP, (m + 1) * STEP)
        block[:, rows, :] = block[:, rows, :] - factor * half[:, rows]
    mean = jnp.sum(block[...], axis=1, keepdims=True) * (1.0 / ROWS)
    mean = rounded(mean).astype(jnp.float32)
    size = jnp.sum(mean * mean, axis=2, keepdims=True)
    along = jnp.sum(block[...] * mean, axis=2, keepdims=True)
    store(jnp.where(size > 0.0, along / jnp.where(size > 0.0, size, 1.0), 0.0), 4)
    for j in range(WIDTH // 128):
        row = ROWS + j % STEP
        cols = slice((3 + j // STEP) * 128, (4 + j // STEP) * 128)
        out_ref[:, row : row + 1, cols] = rounded(mean[:, :, j * 128 : (j + 1) * 128])
    for m, factor in enumerate(load(4)):
        rows = slice(m * STEP, (m + 1) * STEP)
        left = block[:, rows, :] - factor * mean
        block[:, rows, :] = left
    out_ref[:, :ROWS, :] = rounded(block[:, :ROWS, :WIDE])
    for m in range(ROWS // STEP):
        rows = slice(m * STEP, (m + 1) * STEP)
        out_ref[:, ROWS:, m * 128 : (m + 1) * 128] = rounded(block[:, rows, WIDE:])


def far_message(own, near, half):
    n = own.shape[0]
    return pl.pallas_call(
        far_kernel,
        out_shape=jax.ShapeDtypeStruct((n, TALL, WIDE), jnp.bfloat16),
        scratch_shapes=[pltpu.VMEM((n, TALL, WIDTH), jnp.float32)],
        compiler_params=pltpu.CompilerParams(vmem_limit_bytes=VMEM),
        cost_estimate=pl.CostEstimate(flops=500_000, bytes_accessed=1_000_000, transcendentals=0),
    )(own, *near, half)


def project(direction, unit, inverse):
    along = jnp.sum(unit * direction, axis=1, keepdims=True)
    return (direction - unit * along) * inverse


def finish_images_kernel(unit_ref, inverse_ref, back_ref, out_ref, block):
    total = jnp.sum(back_ref[...].astype(jnp.float32), axis=0)
    block[:, :MAIN] = total[:ROWS]
    for rows, cols, place in PIECES:
        block[rows, MAIN + cols.start : MAIN + cols.stop] = total[ROWS:, place]
    out_ref[...] = project(block[...], unit_ref[...], inverse_ref[...])


def finish_texts_kernel(unit_ref, inverse_ref, half_ref, back_ref, out_ref, block):
    back = back_ref[...].astype(jnp.float32)
    total = jnp.sum(back, axis=0)
    block[:, :WIDE] = total[:ROWS]
    spare = back[:, ROWS:, 6 * 128 : 7 * 128]
    lane = lax.broadcasted_iota(jnp.int32, spare.shape, 2)
    means = [
        back[:, ROWS + j % STEP : ROWS + j % STEP + 1, (3 + j // STEP) * 128 : (4 + j // STEP) * 128]
        for j in range(WIDTH // 128)
    ]
    for m in range(ROWS // STEP):
        rows = slice(m * STEP, (m + 1) * STEP)
        block[rows, WIDE:] = total[ROWS:, m * 128 : (m + 1) * 128]
        own = jnp.sum(jnp.where(lane == m, spare, 0.0), axis=2, keepdims=True)
        mean = jnp.sum(jnp.where(lane == 4 + m, spare, 0.0), axis=2, keepdims=True)
        block[rows, :] += jnp.sum(own, axis=0) * half_ref[rows, :].astype(jnp.float32)
        for j, piece in enumerate(means):
            block[rows, j * 128 : (j + 1) * 128] += jnp.sum(mean * piece, axis=0)
    out_ref[...] = project(block[...], unit_ref[...], inverse_ref[...])


def finish(kernel, unit, *operands):
    return pl.pallas_call(
        kernel,
        out_shape=jax.ShapeDtypeStruct(unit.shape, jnp.float32),
        scratch_shapes=[pltpu.VMEM((ROWS, WIDTH), jnp.float32)],
        compiler_params=pltpu.CompilerParams(vmem_limit_bytes=VMEM),
        cost_estimate=pl.CostEstimate(flops=500_000, bytes_accessed=1_000_000, transcendentals=0),
    )(unit, *operands)


def along_z(value, move):
    pairs = [(line_place(z), line_place((z + move(z)) % 16)) for z in range(16)]
    return lax.ppermute(value, LINE, pairs)


def across(value):
    return lax.ppermute(value, "core", [(0, 1), (1, 0)])


def on_device(image_embeds, text_embeds, log_temp, bias):
    z = lax.axis_index("zh") * 8 + lax.axis_index("zm") * 4 + lax.axis_index("zn")
    place = jnp.stack([lax.axis_index(PLANE), z]).astype(jnp.int32)
    sent, img_unit, img_inv, _ = spread(image_embeds, lax.axis_size(PLANE))
    own, txt_unit, txt_inv, txt_half = spread(text_embeds, 1)

    images = lax.all_to_all(sent, PLANE, 0, 0)
    images = [images, across(images)]
    own = jnp.concatenate([own] + [along_z(own, lambda z, by=by: by) for by in FAR[1:]], axis=0)
    texts = [own] + [along_z(own, lambda z, i=i: near_moves(z)[i]) for i in (1, 2, 3)]

    coeff, whole, half, part, *near = text_terms(log_temp, bias, place, images, texts)
    core = lax.axis_index("core").astype(jnp.int32).reshape(1)
    image_back = lax.all_to_all(image_terms(core, coeff, whole), ("x", "core", "y"), 0, 0)
    near = [along_z(value, lambda z, i=i: -near_moves(z)[i]) for i, value in enumerate(near, 1)]
    message, image_back = lax.optimization_barrier((far_message(part, near, half), image_back))
    text_back = lax.all_to_all(message, FAR_AXES, 0, 0)
    return (
        finish(finish_images_kernel, img_unit, img_inv, image_back),
        finish(finish_texts_kernel, txt_unit, txt_inv, txt_half, text_back),
    )


def solution(mesh):
    fine = Mesh(mesh.devices.reshape(SIZES), AXES)
    split = P(AXES, None)
    return jax.shard_map(
        on_device,
        mesh=fine,
        in_specs=(split, split, P(), P()),
        out_specs=(split, split),
        check_vma=False,
    )
```

```python
import jax
import jax.numpy as jnp
from jax import lax
from jax.experimental import pallas as pl
from jax.experimental.pallas import tpu as pltpu
from jax.sharding import Mesh, PartitionSpec as P

EPS = 1e-06
AXES = ("x", "zm", "zn", "core", "zh", "y")
SIZES = (4, 2, 4, 2, 2, 4)
PLANE = ("x", "y")
LINE = ("zm", "zn", "zh")
FAR_AXES = ("zm", "zh")
FAR = (0, 4, 12, 8)
VMEM = 48 * 1024 * 1024

ROWS = 12
WIDTH = 1152
TALL = 16
MAIN = 896
REST = WIDTH - MAIN
STEP = TALL - ROWS
PIECES = [
    (
        slice(m * STEP, (m + 1) * STEP),
        slice(g * 128, (g + 1) * 128),
        slice((3 * g + m) * 128, (3 * g + m + 1) * 128),
    )
    for g in range(REST // 128)
    for m in range(ROWS // STEP)
]

WIDE = 1024


def spread_kernel(emb_ref, out_ref, unit_ref, inverse_ref, half_ref, block):
    wide = emb_ref[...].astype(jnp.float32)
    inverse = lax.rsqrt(jnp.sum(wide * wide, axis=1, keepdims=True) + EPS)
    unit_ref[...] = wide * inverse
    inverse_ref[...] = inverse
    half_ref[...] = unit_ref[...].astype(jnp.bfloat16)
    block[:ROWS, :] = unit_ref[:, :MAIN]
    block[ROWS:, :] = jnp.zeros((STEP, MAIN), jnp.float32)
    for rows, cols, place in PIECES:
        block[ROWS:, place] = unit_ref[rows, MAIN + cols.start : MAIN + cols.stop]
    out_ref[...] = jnp.broadcast_to(block[...].astype(jnp.bfloat16)[None], out_ref.shape)


def spread(emb, peers):
    return pl.pallas_call(
        spread_kernel,
        out_shape=[
            jax.ShapeDtypeStruct((peers, TALL, MAIN), jnp.bfloat16),
            jax.ShapeDtypeStruct(emb.shape, jnp.float32),
            jax.ShapeDtypeStruct((ROWS, 1), jnp.float32),
            jax.ShapeDtypeStruct(emb.shape, jnp.bfloat16),
        ],
        scratch_shapes=[pltpu.VMEM((TALL, MAIN), jnp.float32)],
        compiler_params=pltpu.CompilerParams(vmem_limit_bytes=VMEM),
        cost_estimate=pl.CostEstimate(flops=100_000, bytes_accessed=1_000_000, transcendentals=0),
    )(emb)


def packed(main, rest, n):
    for rows, cols, place in PIECES:
        main[:n, ROWS:, place] = rest[:n, rows, cols]
    return main[:n]


def line_place(z):
    return (z // 4 % 2) * 8 + (z % 4) * 2 + z // 8


def near_moves(z):
    return (0, 1, -1, 2 - 4 * (z % 2))


def text_kernel(temp_ref, bias_ref, place_ref, *refs):
    image_refs, text_refs = refs[:2], refs[2:6]
    coeff_ref, texts, half_out = refs[6:9]
    outs = refs[9:13]
    image_rest, rest, main = refs[13:]
    chips, far = image_refs[0].shape[0], text_refs[0].shape[0]
    rest[:, ROWS:, :] = jnp.zeros((rest.shape[0], STEP, REST), jnp.float32)

    def gather_rest(ref, out, start):
        n = ref.shape[0]
        for rows, cols, place in PIECES:
            rest[:n, rows, cols] = ref[:, ROWS:, place].astype(jnp.float32)
        out[pl.ds(start * TALL, n * TALL), -REST:] = rounded(rest[:n].reshape(n * TALL, REST))

    for i, ref in enumerate(text_refs):
        texts[pl.ds(i * far * TALL, far * TALL), :MAIN] = ref[...].reshape(far * TALL, MAIN)
        gather_rest(ref, texts, i * far)
    for i, ref in enumerate(image_refs):
        gather_rest(ref, image_rest, i * chips)

    def dot(a, b, dims):
        return lax.dot_general(a, b, ((dims[:1], dims[1:]), ((), ())), preferred_element_type=jnp.float32)

    scale = jnp.exp(jnp.full((1, 1), temp_ref[0], jnp.float32))
    mains = [ref[...].reshape(chips * TALL, MAIN) for ref in image_refs]
    parts = []
    for i, image_main in enumerate(mains):
        span = slice(i * chips * TALL, (i + 1) * chips * TALL)
        logits = dot(image_main, texts[:, :MAIN], (1, 1))
        logits += dot(image_rest[span, :], texts[:, MAIN:], (1, 1))
        logits = scale * logits + bias_ref[0]
        row = lax.broadcasted_iota(jnp.int32, logits.shape, 0)
        col = lax.broadcasted_iota(jnp.int32, logits.shape, 1)
        real = (row % TALL < ROWS) & (col % TALL < ROWS)
        if i == 0:
            same = (row == col + place_ref[0] * TALL) & (col < TALL)
            sig = jax.nn.sigmoid(jnp.where(same, -logits, logits))
            sig = jnp.where(same, -sig, sig)
        else:
            sig = jax.nn.sigmoid(logits)
        coeff = rounded(jnp.where(real, sig * scale, 0.0))
        coeff_ref[span, :] = coeff
        parts.append(coeff)

    n = main.shape[0]
    total = sum(dot(coeff, image_main, (0, 0)) for coeff, image_main in zip(parts, mains))
    main[...] = total.reshape(n, TALL, MAIN)
    rest[:n] = dot(coeff_ref[...], image_rest[...], (0, 0)).reshape(n, TALL, REST)
    packed(main, rest, n)
    z = place_ref[1]
    for i, near in enumerate(near_moves(z)):
        for j, by in enumerate(FAR):
            source = (z - near - by + 32) % 16
            slot = source // 4 % 2 * 2 + source // 8
            outs[i][slot] = main[i * far + j].astype(outs[i].dtype)
            if i == 0:
                half_out[slot] = texts[j * TALL : (j + 1) * TALL, :]


def text_terms(log_temp, bias, place, images, texts):
    n_images, n_texts = 2 * images[0].shape[0], 4 * texts[0].shape[0]
    return pl.pallas_call(
        text_kernel,
        in_specs=[pl.BlockSpec(memory_space=pltpu.SMEM)] * 3
        + [pl.BlockSpec(memory_space=pltpu.VMEM)] * 6,
        out_shape=[
            jax.ShapeDtypeStruct((n_images * TALL, n_texts * TALL), jnp.bfloat16),
            jax.ShapeDtypeStruct((n_texts * TALL, WIDTH), jnp.bfloat16),
            jax.ShapeDtypeStruct((n_texts // 4, TALL, WIDTH), jnp.bfloat16),
            jax.ShapeDtypeStruct((n_texts // 4, TALL, MAIN), jnp.float32),
        ]
        + [jax.ShapeDtypeStruct((n_texts // 4, TALL, MAIN), jnp.bfloat16)] * 3,
        scratch_shapes=[
            pltpu.VMEM((n_images * TALL, REST), jnp.bfloat16),
            pltpu.VMEM((n_images // 2, TALL, REST), jnp.float32),
            pltpu.VMEM((n_texts, TALL, MAIN), jnp.float32),
        ],
        compiler_params=pltpu.CompilerParams(vmem_limit_bytes=VMEM),
        cost_estimate=pl.CostEstimate(
            flops=600_000_000, bytes_accessed=4_000_000, transcendentals=131_072
        ),
    )(log_temp, bias, place, *images, *texts)


def image_kernel(core_ref, coeff_ref, texts_ref, out_ref, rest, main):
    n = main.shape[0]
    coeff = coeff_ref[...]
    main[...] = jnp.dot(
        coeff, texts_ref[:, :MAIN], preferred_element_type=jnp.float32
    ).reshape(n, TALL, MAIN)
    rest[...] = jnp.dot(
        coeff, texts_ref[:, MAIN:], preferred_element_type=jnp.float32
    ).reshape(n, TALL, REST)
    packed(main, rest, n)
    for i in range(n):
        chip = i % (n // 2)
        core = core_ref[0] if i < n // 2 else 1 - core_ref[0]
        out_ref[chip // 4 * 8 + core * 4 + chip % 4] = rounded(main[i])


def image_terms(core, coeff, texts):
    n = coeff.shape[0] // TALL
    return pl.pallas_call(
        image_kernel,
        in_specs=[pl.BlockSpec(memory_space=pltpu.SMEM)]
        + [pl.BlockSpec(memory_space=pltpu.VMEM)] * 2,
        out_shape=jax.ShapeDtypeStruct((n, TALL, MAIN), jnp.bfloat16),
        scratch_shapes=[
            pltpu.VMEM((n, TALL, REST), jnp.float32),
            pltpu.VMEM((n, TALL, MAIN), jnp.float32),
        ],
        compiler_params=pltpu.CompilerParams(vmem_limit_bytes=VMEM),
        cost_estimate=pl.CostEstimate(
            flops=300_000_000, bytes_accessed=2_000_000, transcendentals=0
        ),
    )(core, coeff, texts)


def rounded(value):
    return value.astype(jnp.bfloat16)


def far_kernel(own_ref, near_a, near_b, near_c, half_ref, out_ref, block):
    n = own_ref.shape[0]
    part = own_ref[...] + sum(ref[...].astype(jnp.float32) for ref in (near_a, near_b, near_c))
    block[:, :ROWS, :MAIN] = part[:, :ROWS]
    block[:, ROWS:, :] = jnp.zeros((n, STEP, WIDTH), jnp.float32)
    for rows, cols, place in PIECES:
        block[:, rows, MAIN + cols.start : MAIN + cols.stop] = part[:, ROWS:, place]
    half = half_ref[...].astype(jnp.float32)

    along = jnp.sum(block[...] * half, axis=2, keepdims=True)
    lane = lax.broadcasted_iota(jnp.int32, (n, STEP, 128), 2)
    spare = slice(6 * 128, 7 * 128)

    def store(factor, first):
        held = out_ref[:, ROWS:, spare]
        for m in range(ROWS // STEP):
            piece = rounded(jnp.broadcast_to(factor[:, m * STEP : (m + 1) * STEP], lane.shape))
            held = jnp.where(lane == first + m, piece, held)
        out_ref[:, ROWS:, spare] = held

    def load(first):
        held = out_ref[:, ROWS:, spare].astype(jnp.float32)
        return [
            jnp.sum(jnp.where(lane == first + m, held, 0.0), axis=2, keepdims=True)
            for m in range(ROWS // STEP)
        ]

    out_ref[:, ROWS:, :] = jnp.zeros((n, STEP, WIDE), jnp.bfloat16)
    store(along, 0)
    for m, factor in enumerate(load(0)):
        rows = slice(m * STEP, (m + 1) * STEP)
        block[:, rows, :] = block[:, rows, :] - factor * half[:, rows]
    mean = jnp.sum(block[...], axis=1, keepdims=True) * (1.0 / ROWS)
    mean = rounded(mean).astype(jnp.float32)
    size = jnp.sum(mean * mean, axis=2, keepdims=True)
    along = jnp.sum(block[...] * mean, axis=2, keepdims=True)
    store(jnp.where(size > 0.0, along / jnp.where(size > 0.0, size, 1.0), 0.0), 4)
    for j in range(WIDTH // 128):
        row = ROWS + j % STEP
        cols = slice((3 + j // STEP) * 128, (4 + j // STEP) * 128)
        out_ref[:, row : row + 1, cols] = rounded(mean[:, :, j * 128 : (j + 1) * 128])
    for m, factor in enumerate(load(4)):
        rows = slice(m * STEP, (m + 1) * STEP)
        left = block[:, rows, :] - factor * mean
        block[:, rows, :] = left
    out_ref[:, :ROWS, :] = rounded(block[:, :ROWS, :WIDE])
    for m in range(ROWS // STEP):
        rows = slice(m * STEP, (m + 1) * STEP)
        out_ref[:, ROWS:, m * 128 : (m + 1) * 128] = rounded(block[:, rows, WIDE:])


def far_message(own, near, half):
    n = own.shape[0]
    return pl.pallas_call(
        far_kernel,
        out_shape=jax.ShapeDtypeStruct((n, TALL, WIDE), jnp.bfloat16),
        scratch_shapes=[pltpu.VMEM((n, TALL, WIDTH), jnp.float32)],
        compiler_params=pltpu.CompilerParams(vmem_limit_bytes=VMEM),
        cost_estimate=pl.CostEstimate(flops=500_000, bytes_accessed=1_000_000, transcendentals=0),
    )(own, *near, half)


def project(direction, unit, inverse):
    along = jnp.sum(unit * direction, axis=1, keepdims=True)
    return (direction - unit * along) * inverse


def finish_images_kernel(unit_ref, inverse_ref, back_ref, out_ref, block):
    total = jnp.sum(back_ref[...].astype(jnp.float32), axis=0)
    block[:, :MAIN] = total[:ROWS]
    for rows, cols, place in PIECES:
        block[rows, MAIN + cols.start : MAIN + cols.stop] = total[ROWS:, place]
    out_ref[...] = project(block[...], unit_ref[...], inverse_ref[...])


def finish_texts_kernel(unit_ref, inverse_ref, half_ref, back_ref, out_ref, block):
    back = back_ref[...].astype(jnp.float32)
    total = jnp.sum(back, axis=0)
    block[:, :WIDE] = total[:ROWS]
    spare = back[:, ROWS:, 6 * 128 : 7 * 128]
    lane = lax.broadcasted_iota(jnp.int32, spare.shape, 2)
    means = [
        back[:, ROWS + j % STEP : ROWS + j % STEP + 1, (3 + j // STEP) * 128 : (4 + j // STEP) * 128]
        for j in range(WIDTH // 128)
    ]
    for m in range(ROWS // STEP):
        rows = slice(m * STEP, (m + 1) * STEP)
        block[rows, WIDE:] = total[ROWS:, m * 128 : (m + 1) * 128]
        own = jnp.sum(jnp.where(lane == m, spare, 0.0), axis=2, keepdims=True)
        mean = jnp.sum(jnp.where(lane == 4 + m, spare, 0.0), axis=2, keepdims=True)
        block[rows, :] += jnp.sum(own, axis=0) * half_ref[rows, :].astype(jnp.float32)
        for j, piece in enumerate(means):
            block[rows, j * 128 : (j + 1) * 128] += jnp.sum(mean * piece, axis=0)
    out_ref[...] = project(block[...], unit_ref[...], inverse_ref[...])


def finish(kernel, unit, *operands):
    return pl.pallas_call(
        kernel,
        out_shape=jax.ShapeDtypeStruct(unit.shape, jnp.float32),
        scratch_shapes=[pltpu.VMEM((ROWS, WIDTH), jnp.float32)],
        compiler_params=pltpu.CompilerParams(vmem_limit_bytes=VMEM),
        cost_estimate=pl.CostEstimate(flops=500_000, bytes_accessed=1_000_000, transcendentals=0),
    )(unit, *operands)


def along_z(value, move):
    pairs = [(line_place(z), line_place((z + move(z)) % 16)) for z in range(16)]
    return lax.ppermute(value, LINE, pairs)


def across(value):
    return lax.ppermute(value, "core", [(0, 1), (1, 0)])


def on_device(image_embeds, text_embeds, log_temp, bias):
    z = lax.axis_index("zh") * 8 + lax.axis_index("zm") * 4 + lax.axis_index("zn")
    place = jnp.stack([lax.axis_index(PLANE), z]).astype(jnp.int32)
    sent, img_unit, img_inv, _ = spread(image_embeds, lax.axis_size(PLANE))
    own, txt_unit, txt_inv, txt_half = spread(text_embeds, 1)

    images = lax.all_to_all(sent, PLANE, 0, 0)
    images = [images, across(images)]
    own = jnp.concatenate([own] + [along_z(own, lambda z, by=by: by) for by in FAR[1:]], axis=0)
    texts = [own] + [along_z(own, lambda z, i=i: near_moves(z)[i]) for i in (1, 2, 3)]

    coeff, whole, half, part, *near = text_terms(log_temp, bias, place, images, texts)
    core = lax.axis_index("core").astype(jnp.int32).reshape(1)
    image_back = lax.all_to_all(image_terms(core, coeff, whole), ("x", "core", "y"), 0, 0)
    near = [along_z(near[i - 1], lambda z, i=i: -near_moves(z)[i]) for i in (3, 2, 1)]
    message, image_back = lax.optimization_barrier((far_message(part, near, half), image_back))
    text_back = lax.all_to_all(message, FAR_AXES, 0, 0)
    return (
        finish(finish_images_kernel, img_unit, img_inv, image_back),
        finish(finish_texts_kernel, txt_unit, txt_inv, txt_half, text_back),
    )


def solution(mesh):
    fine = Mesh(mesh.devices.reshape(SIZES), AXES)
    split = P(AXES, None)
    return jax.shard_map(
        on_device,
        mesh=fine,
        in_specs=(split, split, P(), P()),
        out_specs=(split, split),
        check_vma=False,
    )
```

```python
import jax
import jax.numpy as jnp
from jax import lax
from jax.experimental import pallas as pl
from jax.experimental.pallas import tpu as pltpu
from jax.sharding import Mesh, PartitionSpec as P

EPS = 1e-06
AXES = ("x", "zm", "zn", "core", "zh", "y")
SIZES = (4, 2, 4, 2, 2, 4)
PLANE = ("x", "y")
LINE = ("zm", "zn", "zh")
FAR_AXES = ("zm", "zh")
FAR = (0, 4, 12, 8)
VMEM = 48 * 1024 * 1024

ROWS = 12
WIDTH = 1152
TALL = 16
MAIN = 896
REST = WIDTH - MAIN
STEP = TALL - ROWS
PIECES = [
    (
        slice(m * STEP, (m + 1) * STEP),
        slice(g * 128, (g + 1) * 128),
        slice((3 * g + m) * 128, (3 * g + m + 1) * 128),
    )
    for g in range(REST // 128)
    for m in range(ROWS // STEP)
]

WIDE = 1024


def spread_kernel(emb_ref, out_ref, unit_ref, inverse_ref, half_ref, block):
    wide = emb_ref[...].astype(jnp.float32)
    inverse = lax.rsqrt(jnp.sum(wide * wide, axis=1, keepdims=True) + EPS)
    unit_ref[...] = wide * inverse
    inverse_ref[...] = inverse
    half_ref[...] = unit_ref[...].astype(jnp.bfloat16)
    block[:ROWS, :] = unit_ref[:, :MAIN]
    block[ROWS:, :] = jnp.zeros((STEP, MAIN), jnp.float32)
    for rows, cols, place in PIECES:
        block[ROWS:, place] = unit_ref[rows, MAIN + cols.start : MAIN + cols.stop]
    out_ref[...] = jnp.broadcast_to(block[...].astype(jnp.bfloat16)[None], out_ref.shape)


def spread(emb, peers):
    return pl.pallas_call(
        spread_kernel,
        out_shape=[
            jax.ShapeDtypeStruct((peers, TALL, MAIN), jnp.bfloat16),
            jax.ShapeDtypeStruct(emb.shape, jnp.float32),
            jax.ShapeDtypeStruct((ROWS, 1), jnp.float32),
            jax.ShapeDtypeStruct(emb.shape, jnp.bfloat16),
        ],
        scratch_shapes=[pltpu.VMEM((TALL, MAIN), jnp.float32)],
        compiler_params=pltpu.CompilerParams(vmem_limit_bytes=VMEM),
        cost_estimate=pl.CostEstimate(flops=100_000, bytes_accessed=1_000_000, transcendentals=0),
    )(emb)


def packed(main, rest, n):
    for rows, cols, place in PIECES:
        main[:n, ROWS:, place] = rest[:n, rows, cols]
    return main[:n]


def line_place(z):
    return (z // 4 % 2) * 8 + (z % 4) * 2 + z // 8


def near_moves(z):
    return (0, 1, -1, 2 - 4 * (z % 2))


def text_kernel(temp_ref, bias_ref, place_ref, *refs):
    image_refs, text_refs = refs[:2], refs[2:6]
    coeff_ref, texts, half_out = refs[6:9]
    outs = refs[9:13]
    image_rest, rest, main = refs[13:]
    chips, far = image_refs[0].shape[0], text_refs[0].shape[0]
    rest[:, ROWS:, :] = jnp.zeros((rest.shape[0], STEP, REST), jnp.float32)

    def gather_rest(ref, out, start):
        n = ref.shape[0]
        for rows, cols, place in PIECES:
            rest[:n, rows, cols] = ref[:, ROWS:, place].astype(jnp.float32)
        out[pl.ds(start * TALL, n * TALL), -REST:] = rounded(rest[:n].reshape(n * TALL, REST))

    for i, ref in enumerate(text_refs):
        texts[pl.ds(i * far * TALL, far * TALL), :MAIN] = ref[...].reshape(far * TALL, MAIN)
        gather_rest(ref, texts, i * far)
    for i, ref in enumerate(image_refs):
        gather_rest(ref, image_rest, i * chips)

    def dot(a, b, dims):
        return lax.dot_general(a, b, ((dims[:1], dims[1:]), ((), ())), preferred_element_type=jnp.float32)

    scale = jnp.exp(jnp.full((1, 1), temp_ref[0], jnp.float32))
    mains = [ref[...].reshape(chips * TALL, MAIN) for ref in image_refs]
    parts = []
    for i, image_main in enumerate(mains):
        span = slice(i * chips * TALL, (i + 1) * chips * TALL)
        logits = dot(image_main, texts[:, :MAIN], (1, 1))
        logits += dot(image_rest[span, :], texts[:, MAIN:], (1, 1))
        logits = scale * logits + bias_ref[0]
        row = lax.broadcasted_iota(jnp.int32, logits.shape, 0)
        col = lax.broadcasted_iota(jnp.int32, logits.shape, 1)
        real = (row % TALL < ROWS) & (col % TALL < ROWS)
        if i == 0:
            same = (row == col + place_ref[0] * TALL) & (col < TALL)
            sig = jax.nn.sigmoid(jnp.where(same, -logits, logits))
            sig = jnp.where(same, -sig, sig)
        else:
            sig = jax.nn.sigmoid(logits)
        coeff = rounded(jnp.where(real, sig * scale, 0.0))
        coeff_ref[span, :] = coeff
        parts.append(coeff)

    n = main.shape[0]
    total = sum(dot(coeff, image_main, (0, 0)) for coeff, image_main in zip(parts, mains))
    main[...] = total.reshape(n, TALL, MAIN)
    rest[:n] = dot(coeff_ref[...], image_rest[...], (0, 0)).reshape(n, TALL, REST)
    packed(main, rest, n)
    z = place_ref[1]
    for i, near in enumerate(near_moves(z)):
        for j, by in enumerate(FAR):
            source = (z - near - by + 32) % 16
            slot = source // 4 % 2 * 2 + source // 8
            outs[i][slot] = main[i * far + j].astype(outs[i].dtype)
            if i == 0:
                half_out[slot] = texts[j * TALL : (j + 1) * TALL, :]


def text_terms(log_temp, bias, place, images, texts):
    n_images, n_texts = 2 * images[0].shape[0], 4 * texts[0].shape[0]
    return pl.pallas_call(
        text_kernel,
        in_specs=[pl.BlockSpec(memory_space=pltpu.SMEM)] * 3
        + [pl.BlockSpec(memory_space=pltpu.VMEM)] * 6,
        out_shape=[
            jax.ShapeDtypeStruct((n_images * TALL, n_texts * TALL), jnp.bfloat16),
            jax.ShapeDtypeStruct((n_texts * TALL, WIDTH), jnp.bfloat16),
            jax.ShapeDtypeStruct((n_texts // 4, TALL, WIDTH), jnp.bfloat16),
            jax.ShapeDtypeStruct((n_texts // 4, TALL, MAIN), jnp.float32),
        ]
        + [jax.ShapeDtypeStruct((n_texts // 4, TALL, MAIN), jnp.bfloat16)] * 3,
        scratch_shapes=[
            pltpu.VMEM((n_images * TALL, REST), jnp.bfloat16),
            pltpu.VMEM((n_images // 2, TALL, REST), jnp.float32),
            pltpu.VMEM((n_texts, TALL, MAIN), jnp.float32),
        ],
        compiler_params=pltpu.CompilerParams(vmem_limit_bytes=VMEM),
        cost_estimate=pl.CostEstimate(
            flops=600_000_000, bytes_accessed=4_000_000, transcendentals=131_072
        ),
    )(log_temp, bias, place, *images, *texts)


def image_kernel(core_ref, coeff_ref, texts_ref, out_ref, rest, main):
    n = main.shape[0]
    coeff = coeff_ref[...]
    main[...] = jnp.dot(
        coeff, texts_ref[:, :MAIN], preferred_element_type=jnp.float32
    ).reshape(n, TALL, MAIN)
    rest[...] = jnp.dot(
        coeff, texts_ref[:, MAIN:], preferred_element_type=jnp.float32
    ).reshape(n, TALL, REST)
    packed(main, rest, n)
    for i in range(n):
        chip = i % (n // 2)
        core = core_ref[0] if i < n // 2 else 1 - core_ref[0]
        out_ref[chip // 4 * 8 + core * 4 + chip % 4] = rounded(main[i])


def image_terms(core, coeff, texts):
    n = coeff.shape[0] // TALL
    return pl.pallas_call(
        image_kernel,
        in_specs=[pl.BlockSpec(memory_space=pltpu.SMEM)]
        + [pl.BlockSpec(memory_space=pltpu.VMEM)] * 2,
        out_shape=jax.ShapeDtypeStruct((n, TALL, MAIN), jnp.bfloat16),
        scratch_shapes=[
            pltpu.VMEM((n, TALL, REST), jnp.float32),
            pltpu.VMEM((n, TALL, MAIN), jnp.float32),
        ],
        compiler_params=pltpu.CompilerParams(vmem_limit_bytes=VMEM),
        cost_estimate=pl.CostEstimate(
            flops=300_000_000, bytes_accessed=2_000_000, transcendentals=0
        ),
    )(core, coeff, texts)


def rounded(value):
    return value.astype(jnp.bfloat16)


def far_kernel(own_ref, near_a, near_b, near_c, half_ref, out_ref, block):
    n = own_ref.shape[0]
    part = own_ref[...] + sum(ref[...].astype(jnp.float32) for ref in (near_a, near_b, near_c))
    block[:, :ROWS, :MAIN] = part[:, :ROWS]
    block[:, ROWS:, :] = jnp.zeros((n, STEP, WIDTH), jnp.float32)
    for rows, cols, place in PIECES:
        block[:, rows, MAIN + cols.start : MAIN + cols.stop] = part[:, ROWS:, place]
    half = half_ref[...].astype(jnp.float32)

    along = jnp.sum(block[...] * half, axis=2, keepdims=True)
    lane = lax.broadcasted_iota(jnp.int32, (n, STEP, 128), 2)
    spare = slice(6 * 128, 7 * 128)

    def store(factor, first):
        held = out_ref[:, ROWS:, spare]
        for m in range(ROWS // STEP):
            piece = rounded(jnp.broadcast_to(factor[:, m * STEP : (m + 1) * STEP], lane.shape))
            held = jnp.where(lane == first + m, piece, held)
        out_ref[:, ROWS:, spare] = held

    def load(first):
        held = out_ref[:, ROWS:, spare].astype(jnp.float32)
        return [
            jnp.sum(jnp.where(lane == first + m, held, 0.0), axis=2, keepdims=True)
            for m in range(ROWS // STEP)
        ]

    out_ref[:, ROWS:, :] = jnp.zeros((n, STEP, WIDE), jnp.bfloat16)
    store(along, 0)
    for m, factor in enumerate(load(0)):
        rows = slice(m * STEP, (m + 1) * STEP)
        block[:, rows, :] = block[:, rows, :] - factor * half[:, rows]
    mean = jnp.sum(block[...], axis=1, keepdims=True) * (1.0 / ROWS)
    mean = rounded(mean).astype(jnp.float32)
    size = jnp.sum(mean * mean, axis=2, keepdims=True)
    along = jnp.sum(block[...] * mean, axis=2, keepdims=True)
    store(jnp.where(size > 0.0, along / jnp.where(size > 0.0, size, 1.0), 0.0), 4)
    for j in range(WIDTH // 128):
        row = ROWS + j % STEP
        cols = slice((3 + j // STEP) * 128, (4 + j // STEP) * 128)
        out_ref[:, row : row + 1, cols] = rounded(mean[:, :, j * 128 : (j + 1) * 128])
    for m, factor in enumerate(load(4)):
        rows = slice(m * STEP, (m + 1) * STEP)
        left = block[:, rows, :] - factor * mean
        block[:, rows, :] = left
    out_ref[:, :ROWS, :] = rounded(block[:, :ROWS, :WIDE])
    for m in range(ROWS // STEP):
        rows = slice(m * STEP, (m + 1) * STEP)
        out_ref[:, ROWS:, m * 128 : (m + 1) * 128] = rounded(block[:, rows, WIDE:])


def far_message(own, near, half):
    n = own.shape[0]
    return pl.pallas_call(
        far_kernel,
        out_shape=jax.ShapeDtypeStruct((n, TALL, WIDE), jnp.bfloat16),
        scratch_shapes=[pltpu.VMEM((n, TALL, WIDTH), jnp.float32)],
        compiler_params=pltpu.CompilerParams(vmem_limit_bytes=VMEM),
        cost_estimate=pl.CostEstimate(flops=500_000, bytes_accessed=1_000_000, transcendentals=0),
    )(own, *near, half)


def project(direction, unit, inverse):
    along = jnp.sum(unit * direction, axis=1, keepdims=True)
    return (direction - unit * along) * inverse


def finish_images_kernel(unit_ref, inverse_ref, back_ref, out_ref, block):
    total = jnp.sum(back_ref[...].astype(jnp.float32), axis=0)
    block[:, :MAIN] = total[:ROWS]
    for rows, cols, place in PIECES:
        block[rows, MAIN + cols.start : MAIN + cols.stop] = total[ROWS:, place]
    out_ref[...] = project(block[...], unit_ref[...], inverse_ref[...])


def finish_texts_kernel(unit_ref, inverse_ref, half_ref, back_ref, out_ref, block):
    back = back_ref[...].astype(jnp.float32)
    total = jnp.sum(back, axis=0)
    block[:, :WIDE] = total[:ROWS]
    spare = back[:, ROWS:, 6 * 128 : 7 * 128]
    lane = lax.broadcasted_iota(jnp.int32, spare.shape, 2)
    means = [
        back[:, ROWS + j % STEP : ROWS + j % STEP + 1, (3 + j // STEP) * 128 : (4 + j // STEP) * 128]
        for j in range(WIDTH // 128)
    ]
    for m in range(ROWS // STEP):
        rows = slice(m * STEP, (m + 1) * STEP)
        block[rows, WIDE:] = total[ROWS:, m * 128 : (m + 1) * 128]
        own = jnp.sum(jnp.where(lane == m, spare, 0.0), axis=2, keepdims=True)
        mean = jnp.sum(jnp.where(lane == 4 + m, spare, 0.0), axis=2, keepdims=True)
        block[rows, :] += jnp.sum(own, axis=0) * half_ref[rows, :].astype(jnp.float32)
        for j, piece in enumerate(means):
            block[rows, j * 128 : (j + 1) * 128] += jnp.sum(mean * piece, axis=0)
    out_ref[...] = project(block[...], unit_ref[...], inverse_ref[...])


def finish(kernel, unit, *operands):
    return pl.pallas_call(
        kernel,
        out_shape=jax.ShapeDtypeStruct(unit.shape, jnp.float32),
        scratch_shapes=[pltpu.VMEM((ROWS, WIDTH), jnp.float32)],
        compiler_params=pltpu.CompilerParams(vmem_limit_bytes=VMEM),
        cost_estimate=pl.CostEstimate(flops=500_000, bytes_accessed=1_000_000, transcendentals=0),
    )(unit, *operands)


def along_z(value, move):
    pairs = [(line_place(z), line_place((z + move(z)) % 16)) for z in range(16)]
    return lax.ppermute(value, LINE, pairs)


def across(value):
    return lax.ppermute(value, "core", [(0, 1), (1, 0)])


def on_device(image_embeds, text_embeds, log_temp, bias):
    z = lax.axis_index("zh") * 8 + lax.axis_index("zm") * 4 + lax.axis_index("zn")
    place = jnp.stack([lax.axis_index(PLANE), z]).astype(jnp.int32)
    sent, img_unit, img_inv, _ = spread(image_embeds, lax.axis_size(PLANE))
    own, txt_unit, txt_inv, txt_half = spread(text_embeds, 1)

    images = lax.all_to_all(sent, PLANE, 0, 0)
    images = [images, across(images)]
    own = jnp.concatenate([own] + [along_z(own, lambda z, by=by: by) for by in FAR[1:]], axis=0)
    texts = [own] + [along_z(own, lambda z, i=i: near_moves(z)[i]) for i in (1, 2, 3)]

    coeff, whole, half, part, *near = text_terms(log_temp, bias, place, images, texts)
    core = lax.axis_index("core").astype(jnp.int32).reshape(1)
    image_back = lax.all_to_all(image_terms(core, coeff, whole), ("x", "core", "y"), 0, 0)
    near = [along_z(near[i - 1], lambda z, i=i: -near_moves(z)[i]) for i in (1, 2, 3)]
    message, image_back = lax.optimization_barrier((far_message(part, near, half), image_back))
    text_back = lax.all_to_all(message, FAR_AXES, 0, 0)
    return (
        finish(finish_images_kernel, img_unit, img_inv, image_back),
        finish(finish_texts_kernel, txt_unit, txt_inv, txt_half, text_back),
    )


def solution(mesh):
    fine = Mesh(mesh.devices.reshape(SIZES), AXES)
    split = P(AXES, None)
    return jax.shard_map(
        on_device,
        mesh=fine,
        in_specs=(split, split, P(), P()),
        out_specs=(split, split),
        check_vma=False,
    )
```

```python
import jax
import jax.numpy as jnp
from jax import lax
from jax.experimental import pallas as pl
from jax.experimental.pallas import tpu as pltpu
from jax.sharding import Mesh, PartitionSpec as P

EPS = 1e-06
AXES = ("x", "zm", "zn", "core", "zh", "y")
SIZES = (4, 2, 4, 2, 2, 4)
PLANE = ("x", "core", "y")
LINE = ("zm", "zn", "zh")
FAR = (0, 4, 12, 8)
VMEM = 48 * 1024 * 1024

ROWS = 12
WIDTH = 1152
TALL = 16
MAIN = 896
REST = WIDTH - MAIN
STEP = TALL - ROWS
PIECES = [
    (
        slice(m * STEP, (m + 1) * STEP),
        slice(g * 128, (g + 1) * 128),
        slice((3 * g + m) * 128, (3 * g + m + 1) * 128),
    )
    for g in range(REST // 128)
    for m in range(ROWS // STEP)
]


def spread_kernel(emb_ref, out_ref, unit_ref, inverse_ref, block):
    wide = emb_ref[...].astype(jnp.float32)
    inverse = lax.rsqrt(jnp.sum(wide * wide, axis=1, keepdims=True) + EPS)
    unit_ref[...] = wide * inverse
    inverse_ref[...] = inverse
    block[:ROWS, :] = unit_ref[:, :MAIN]
    block[ROWS:, :] = jnp.zeros((STEP, MAIN), jnp.float32)
    for rows, cols, place in PIECES:
        block[ROWS:, place] = unit_ref[rows, MAIN + cols.start : MAIN + cols.stop]
    out_ref[...] = jnp.broadcast_to(block[...].astype(jnp.bfloat16)[None], out_ref.shape)


def spread(emb, peers):
    return pl.pallas_call(
        spread_kernel,
        out_shape=[
            jax.ShapeDtypeStruct((peers, TALL, MAIN), jnp.bfloat16),
            jax.ShapeDtypeStruct(emb.shape, jnp.float32),
            jax.ShapeDtypeStruct((ROWS, 1), jnp.float32),
        ],
        scratch_shapes=[pltpu.VMEM((TALL, MAIN), jnp.float32)],
        compiler_params=pltpu.CompilerParams(vmem_limit_bytes=VMEM),
        cost_estimate=pl.CostEstimate(flops=100_000, bytes_accessed=1_000_000, transcendentals=0),
    )(emb)


def packed(main, rest, n):
    for rows, cols, place in PIECES:
        main[:n, ROWS:, place] = rest[:n, rows, cols]
    return main[:n]


def pair_kernel(temp_ref, bias_ref, place_ref, images_ref, *refs):
    text_refs = refs[:4]
    core_out, image_out, text_out = refs[4:7]
    texts, image_rest, coeff_ref, rest, main = refs[7:]
    n_images, far = images_ref.shape[0], text_refs[0].shape[0]
    rest[:, ROWS:, :] = jnp.zeros((n_images, STEP, REST), jnp.float32)

    def gather_rest(ref):
        n = ref.shape[0]
        for rows, cols, place in PIECES:
            rest[:n, rows, cols] = ref[:, ROWS:, place].astype(jnp.float32)
        return rest[:n].reshape(n * TALL, REST).astype(jnp.bfloat16)

    for i, ref in enumerate(text_refs):
        span = pl.ds(i * far * TALL, far * TALL)
        texts[span, :MAIN] = ref[...].reshape(far * TALL, MAIN)
        texts[span, MAIN:] = gather_rest(ref)
    image_rest[...] = gather_rest(images_ref)
    image_main = images_ref[...].reshape(n_images * TALL, MAIN)

    def dot(a, b, dims):
        return lax.dot_general(
            a, b, ((dims[:1], dims[1:]), ((), ())), preferred_element_type=jnp.float32
        )

    scale = jnp.exp(jnp.full((1, 1), temp_ref[0], jnp.float32))
    logits = dot(image_main, texts[:, :MAIN], (1, 1)) + dot(image_rest[...], texts[:, MAIN:], (1, 1))
    logits = scale * logits + bias_ref[0]
    x, core, y = place_ref[0] // 8, place_ref[0] // 4 % 2, place_ref[0] % 4
    z = place_ref[1]
    row = lax.broadcasted_iota(jnp.int32, logits.shape, 0)
    col = lax.broadcasted_iota(jnp.int32, logits.shape, 1)
    real = (row % TALL < ROWS) & (col % TALL < ROWS)
    same = (row == col + place_ref[0] * TALL) & (col < TALL)
    sig = jax.nn.sigmoid(jnp.where(same, -logits, logits))
    coeff_ref[...] = jnp.where(real, jnp.where(same, -sig, sig) * scale, 0.0).astype(jnp.bfloat16)
    coeff = coeff_ref[...]

    main[...] = dot(coeff, texts[:, :MAIN], (1, 0)).reshape(n_images, TALL, MAIN)
    rest[...] = dot(coeff, texts[:, MAIN:], (1, 0)).reshape(n_images, TALL, REST)
    packed(main, rest, n_images)
    for dy in range(4):
        for dx in range(4):
            spot = (x + dx) % 4 * 8 + (y + dy) % 4
            core_out[dy * 4 + dx] = main[spot + (1 - core) * 4].astype(jnp.bfloat16)
            image_out[dy * 4 + dx] = main[spot + core * 4]

    n = 4 * far
    main[:n] = dot(coeff, image_main, (0, 0)).reshape(n, TALL, MAIN)
    rest[:n] = dot(coeff, image_rest[...], (0, 0)).reshape(n, TALL, REST)
    packed(main, rest, n)
    for i, near in enumerate(near_moves(z)):
        for j, by in enumerate(FAR):
            source = (z - near - by + 32) % 16
            text_out[line_place(source)] = main[i * far + j].astype(jnp.bfloat16)


def pair_terms(log_temp, bias, place, images, texts):
    n_images, n_texts = images.shape[0], 4 * texts[0].shape[0]
    return pl.pallas_call(
        pair_kernel,
        in_specs=[pl.BlockSpec(memory_space=pltpu.SMEM)] * 3
        + [pl.BlockSpec(memory_space=pltpu.VMEM)] * 5,
        out_shape=[
            jax.ShapeDtypeStruct((n_images // 2, TALL, MAIN), jnp.bfloat16),
            jax.ShapeDtypeStruct((n_images // 2, TALL, MAIN), jnp.float32),
            jax.ShapeDtypeStruct((n_texts, TALL, MAIN), jnp.bfloat16),
        ],
        scratch_shapes=[
            pltpu.VMEM((n_texts * TALL, WIDTH), jnp.bfloat16),
            pltpu.VMEM((n_images * TALL, REST), jnp.bfloat16),
            pltpu.VMEM((n_images * TALL, n_texts * TALL), jnp.bfloat16),
            pltpu.VMEM((n_images, TALL, REST), jnp.float32),
            pltpu.VMEM((n_images, TALL, MAIN), jnp.float32),
        ],
        compiler_params=pltpu.CompilerParams(vmem_limit_bytes=VMEM),
        cost_estimate=pl.CostEstimate(
            flops=900_000_000, bytes_accessed=4_000_000, transcendentals=131_072
        ),
    )(log_temp, bias, place, images, *texts)


def finish_kernel(unit_ref, inverse_ref, *refs):
    back_refs, (out_ref, block) = refs[:-2], refs[-2:]
    total = sum(jnp.sum(ref[...].astype(jnp.float32), axis=0) for ref in back_refs)
    block[:, :MAIN] = total[:ROWS]
    for rows, cols, place in PIECES:
        block[rows, MAIN + cols.start : MAIN + cols.stop] = total[ROWS:, place]
    unit = unit_ref[...]
    direction = block[...]
    along = jnp.sum(unit * direction, axis=1, keepdims=True)
    out_ref[...] = (direction - unit * along) * inverse_ref[...]


def finish(unit, inverse, *back):
    return pl.pallas_call(
        finish_kernel,
        out_shape=jax.ShapeDtypeStruct(unit.shape, jnp.float32),
        scratch_shapes=[pltpu.VMEM((ROWS, WIDTH), jnp.float32)],
        compiler_params=pltpu.CompilerParams(vmem_limit_bytes=VMEM),
        cost_estimate=pl.CostEstimate(flops=500_000, bytes_accessed=1_000_000, transcendentals=0),
    )(unit, inverse, *back)


def line_place(z):
    return (z // 4 % 2) * 8 + (z % 4) * 2 + z // 8


def near_moves(z):
    return (0, 1, -1, 2 - 4 * (z % 2))


def along_z(value, move):
    pairs = [(line_place(z), line_place((z + move(z)) % 16)) for z in range(16)]
    return lax.ppermute(value, LINE, pairs)


def around(value, axis, by):
    n = lax.axis_size(axis)
    return lax.ppermute(value, axis, [(i, (i + by) % n) for i in range(n)])


def on_device(image_embeds, text_embeds, log_temp, bias):
    z = lax.axis_index("zh") * 8 + lax.axis_index("zm") * 4 + lax.axis_index("zn")
    place = jnp.stack([lax.axis_index(PLANE), z]).astype(jnp.int32)
    sent, img_unit, img_inv = spread(image_embeds, lax.axis_size(PLANE))
    own, txt_unit, txt_inv = spread(text_embeds, 1)

    images = lax.all_to_all(sent, PLANE, 0, 0)
    own = jnp.concatenate([own] + [along_z(own, lambda z, by=by: by) for by in FAR[1:]], axis=0)
    texts = [own] + [along_z(own, lambda z, i=i: near_moves(z)[i]) for i in (1, 2, 3)]

    core_part, part, text_part = pair_terms(log_temp, bias, place, images, texts)
    text_back = lax.all_to_all(text_part, LINE, 0, 0)
    part = part + around(core_part, "core", 1).astype(jnp.float32)
    part = part.reshape((4, 4) + part.shape[1:])
    part = part[0] + sum(
        around(part[by].astype(jnp.bfloat16), "y", by).astype(jnp.float32) for by in (1, 3, 2)
    )
    image_back = [part[:1]] + [around(part[by : by + 1], "x", by) for by in (1, 3, 2)]
    return (
        finish(img_unit, img_inv, *image_back),
        finish(txt_unit, txt_inv, text_back),
    )


def solution(mesh):
    fine = Mesh(mesh.devices.reshape(SIZES), AXES)
    split = P(AXES, None)
    return jax.shard_map(
        on_device,
        mesh=fine,
        in_specs=(split, split, P(), P()),
        out_specs=(split, split),
        check_vma=False,
    )
```

```python
import jax
import jax.numpy as jnp
from jax import lax
from jax.experimental import pallas as pl
from jax.experimental.pallas import tpu as pltpu
from jax.sharding import Mesh, PartitionSpec as P

EPS = 1e-06
AXES = ("x", "zm", "zn", "core", "zh", "y")
SIZES = (4, 2, 4, 2, 2, 4)
PLANE = ("x", "core", "y")
LINE = ("zm", "zn", "zh")
FAR = (0, 4, 12, 8)
VMEM = 48 * 1024 * 1024

ROWS = 12
WIDTH = 1152
TALL = 16
MAIN = 896
REST = WIDTH - MAIN
STEP = TALL - ROWS
PIECES = [
    (
        slice(m * STEP, (m + 1) * STEP),
        slice(g * 128, (g + 1) * 128),
        slice((3 * g + m) * 128, (3 * g + m + 1) * 128),
    )
    for g in range(REST // 128)
    for m in range(ROWS // STEP)
]


def spread_kernel(emb_ref, out_ref, unit_ref, inverse_ref, block):
    wide = emb_ref[...].astype(jnp.float32)
    inverse = lax.rsqrt(jnp.sum(wide * wide, axis=1, keepdims=True) + EPS)
    unit_ref[...] = wide * inverse
    inverse_ref[...] = inverse
    block[:ROWS, :] = unit_ref[:, :MAIN]
    block[ROWS:, :] = jnp.zeros((STEP, MAIN), jnp.float32)
    for rows, cols, place in PIECES:
        block[ROWS:, place] = unit_ref[rows, MAIN + cols.start : MAIN + cols.stop]
    out_ref[...] = jnp.broadcast_to(block[...].astype(jnp.bfloat16)[None], out_ref.shape)


def spread(emb, peers):
    return pl.pallas_call(
        spread_kernel,
        out_shape=[
            jax.ShapeDtypeStruct((peers, TALL, MAIN), jnp.bfloat16),
            jax.ShapeDtypeStruct(emb.shape, jnp.float32),
            jax.ShapeDtypeStruct((ROWS, 1), jnp.float32),
        ],
        scratch_shapes=[pltpu.VMEM((TALL, MAIN), jnp.float32)],
        compiler_params=pltpu.CompilerParams(vmem_limit_bytes=VMEM),
        cost_estimate=pl.CostEstimate(flops=100_000, bytes_accessed=1_000_000, transcendentals=0),
    )(emb)


def packed(main, rest, n):
    for rows, cols, place in PIECES:
        main[:n, ROWS:, place] = rest[:n, rows, cols]
    return main[:n]


def pair_kernel(temp_ref, bias_ref, place_ref, images_ref, *refs):
    text_refs = refs[:4]
    core_out, image_out, text_out = refs[4:7]
    texts, image_rest, coeff_ref, rest, main = refs[7:]
    n_images, far = images_ref.shape[0], text_refs[0].shape[0]
    rest[:, ROWS:, :] = jnp.zeros((n_images, STEP, REST), jnp.float32)

    def gather_rest(ref):
        n = ref.shape[0]
        for rows, cols, place in PIECES:
            rest[:n, rows, cols] = ref[:, ROWS:, place].astype(jnp.float32)
        return rest[:n].reshape(n * TALL, REST).astype(jnp.bfloat16)

    for i, ref in enumerate(text_refs):
        span = pl.ds(i * far * TALL, far * TALL)
        texts[span, :MAIN] = ref[...].reshape(far * TALL, MAIN)
        texts[span, MAIN:] = gather_rest(ref)
    image_rest[...] = gather_rest(images_ref)
    image_main = images_ref[...].reshape(n_images * TALL, MAIN)

    def dot(a, b, dims):
        return lax.dot_general(
            a, b, ((dims[:1], dims[1:]), ((), ())), preferred_element_type=jnp.float32
        )

    scale = jnp.exp(jnp.full((1, 1), temp_ref[0], jnp.float32))
    logits = dot(image_main, texts[:, :MAIN], (1, 1)) + dot(image_rest[...], texts[:, MAIN:], (1, 1))
    logits = scale * logits + bias_ref[0]
    x, core, y = place_ref[0] // 8, place_ref[0] // 4 % 2, place_ref[0] % 4
    z = place_ref[1]
    row = lax.broadcasted_iota(jnp.int32, logits.shape, 0)
    col = lax.broadcasted_iota(jnp.int32, logits.shape, 1)
    real = (row % TALL < ROWS) & (col % TALL < ROWS)
    same = (row == col + place_ref[0] * TALL) & (col < TALL)
    sig = jax.nn.sigmoid(jnp.where(same, -logits, logits))
    coeff_ref[...] = jnp.where(real, jnp.where(same, -sig, sig) * scale, 0.0).astype(jnp.bfloat16)
    coeff = coeff_ref[...]

    main[...] = dot(coeff, texts[:, :MAIN], (1, 0)).reshape(n_images, TALL, MAIN)
    rest[...] = dot(coeff, texts[:, MAIN:], (1, 0)).reshape(n_images, TALL, REST)
    packed(main, rest, n_images)
    for dy in range(4):
        for dx in range(4):
            spot = (x + dx) % 4 * 8 + (y + dy) % 4
            core_out[dy * 4 + dx] = main[spot + (1 - core) * 4].astype(jnp.bfloat16)
            image_out[dy * 4 + dx] = main[spot + core * 4]

    n = 4 * far
    main[:n] = dot(coeff, image_main, (0, 0)).reshape(n, TALL, MAIN)
    rest[:n] = dot(coeff, image_rest[...], (0, 0)).reshape(n, TALL, REST)
    packed(main, rest, n)
    for i, near in enumerate(near_moves(z)):
        for j, by in enumerate(FAR):
            source = (z - near - by + 32) % 16
            text_out[line_place(source)] = main[i * far + j].astype(jnp.bfloat16)


def pair_terms(log_temp, bias, place, images, texts):
    n_images, n_texts = images.shape[0], 4 * texts[0].shape[0]
    return pl.pallas_call(
        pair_kernel,
        in_specs=[pl.BlockSpec(memory_space=pltpu.SMEM)] * 3
        + [pl.BlockSpec(memory_space=pltpu.VMEM)] * 5,
        out_shape=[
            jax.ShapeDtypeStruct((n_images // 2, TALL, MAIN), jnp.bfloat16),
            jax.ShapeDtypeStruct((n_images // 2, TALL, MAIN), jnp.float32),
            jax.ShapeDtypeStruct((n_texts, TALL, MAIN), jnp.bfloat16),
        ],
        scratch_shapes=[
            pltpu.VMEM((n_texts * TALL, WIDTH), jnp.bfloat16),
            pltpu.VMEM((n_images * TALL, REST), jnp.bfloat16),
            pltpu.VMEM((n_images * TALL, n_texts * TALL), jnp.bfloat16),
            pltpu.VMEM((n_images, TALL, REST), jnp.float32),
            pltpu.VMEM((n_images, TALL, MAIN), jnp.float32),
        ],
        compiler_params=pltpu.CompilerParams(vmem_limit_bytes=VMEM),
        cost_estimate=pl.CostEstimate(
            flops=900_000_000, bytes_accessed=4_000_000, transcendentals=131_072
        ),
    )(log_temp, bias, place, images, *texts)


def finish_kernel(unit_ref, inverse_ref, *refs):
    back_refs, (out_ref, block) = refs[:-2], refs[-2:]
    total = sum(jnp.sum(ref[...].astype(jnp.float32), axis=0) for ref in back_refs)
    block[:, :MAIN] = total[:ROWS]
    for rows, cols, place in PIECES:
        block[rows, MAIN + cols.start : MAIN + cols.stop] = total[ROWS:, place]
    unit = unit_ref[...]
    direction = block[...]
    along = jnp.sum(unit * direction, axis=1, keepdims=True)
    out_ref[...] = (direction - unit * along) * inverse_ref[...]


def finish(unit, inverse, *back):
    return pl.pallas_call(
        finish_kernel,
        out_shape=jax.ShapeDtypeStruct(unit.shape, jnp.float32),
        scratch_shapes=[pltpu.VMEM((ROWS, WIDTH), jnp.float32)],
        compiler_params=pltpu.CompilerParams(vmem_limit_bytes=VMEM),
        cost_estimate=pl.CostEstimate(flops=500_000, bytes_accessed=1_000_000, transcendentals=0),
    )(unit, inverse, *back)


def line_place(z):
    return (z // 4 % 2) * 8 + (z % 4) * 2 + z // 8


def near_moves(z):
    return (0, 1, -1, 2 - 4 * (z % 2))


def along_z(value, move):
    pairs = [(line_place(z), line_place((z + move(z)) % 16)) for z in range(16)]
    return lax.ppermute(value, LINE, pairs)


def around(value, axis, by):
    n = lax.axis_size(axis)
    return lax.ppermute(value, axis, [(i, (i + by) % n) for i in range(n)])


def on_device(image_embeds, text_embeds, log_temp, bias):
    z = lax.axis_index("zh") * 8 + lax.axis_index("zm") * 4 + lax.axis_index("zn")
    place = jnp.stack([lax.axis_index(PLANE), z]).astype(jnp.int32)
    sent, img_unit, img_inv = spread(image_embeds, lax.axis_size(PLANE))
    own, txt_unit, txt_inv = spread(text_embeds, 1)

    images = lax.all_to_all(sent, PLANE, 0, 0)
    own = jnp.concatenate([own] + [along_z(own, lambda z, by=by: by) for by in FAR[1:]], axis=0)
    texts = [own] + [along_z(own, lambda z, i=i: near_moves(z)[i]) for i in (1, 2, 3)]

    core_part, part, text_part = pair_terms(log_temp, bias, place, images, texts)
    text_back = lax.all_to_all(text_part, LINE, 0, 0)
    part = part + around(core_part, "core", 1).astype(jnp.float32)
    part = part.reshape((4, 4) + part.shape[1:])
    part = part[0] + sum(
        around(part[by].astype(jnp.bfloat16), "y", by).astype(jnp.float32) for by in (1, 3, 2)
    )
    image_back = jnp.stack([part[0]] + [around(part[by], "x", by) for by in (1, 3, 2)], axis=0)
    return (
        finish(img_unit, img_inv, image_back),
        finish(txt_unit, txt_inv, text_back),
    )


def solution(mesh):
    fine = Mesh(mesh.devices.reshape(SIZES), AXES)
    split = P(AXES, None)
    return jax.shard_map(
        on_device,
        mesh=fine,
        in_specs=(split, split, P(), P()),
        out_specs=(split, split),
        check_vma=False,
    )
```

```python
import jax
import jax.numpy as jnp
from jax import lax
from jax.experimental import pallas as pl
from jax.experimental.pallas import tpu as pltpu
from jax.sharding import Mesh, PartitionSpec as P

EPS = 1e-06
AXES = ("x", "zm", "zn", "core", "zh", "y")
SIZES = (4, 2, 4, 2, 2, 4)
PLANE = ("x", "core", "y")
LINE = ("zm", "zn", "zh")
FAR = (0, 4, 12, 8)
VMEM = 48 * 1024 * 1024

ROWS = 12
WIDTH = 1152
TALL = 16
MAIN = 896
REST = WIDTH - MAIN
STEP = TALL - ROWS
PIECES = [
    (
        slice(m * STEP, (m + 1) * STEP),
        slice(g * 128, (g + 1) * 128),
        slice((3 * g + m) * 128, (3 * g + m + 1) * 128),
    )
    for g in range(REST // 128)
    for m in range(ROWS // STEP)
]


def spread_kernel(emb_ref, out_ref, unit_ref, inverse_ref, block):
    wide = emb_ref[...].astype(jnp.float32)
    inverse = lax.rsqrt(jnp.sum(wide * wide, axis=1, keepdims=True) + EPS)
    unit_ref[...] = wide * inverse
    inverse_ref[...] = inverse
    block[:ROWS, :] = unit_ref[:, :MAIN]
    block[ROWS:, :] = jnp.zeros((STEP, MAIN), jnp.float32)
    for rows, cols, place in PIECES:
        block[ROWS:, place] = unit_ref[rows, MAIN + cols.start : MAIN + cols.stop]
    out_ref[...] = jnp.broadcast_to(block[...].astype(jnp.bfloat16)[None], out_ref.shape)


def spread(emb, peers):
    return pl.pallas_call(
        spread_kernel,
        out_shape=[
            jax.ShapeDtypeStruct((peers, TALL, MAIN), jnp.bfloat16),
            jax.ShapeDtypeStruct(emb.shape, jnp.float32),
            jax.ShapeDtypeStruct((ROWS, 1), jnp.float32),
        ],
        scratch_shapes=[pltpu.VMEM((TALL, MAIN), jnp.float32)],
        compiler_params=pltpu.CompilerParams(vmem_limit_bytes=VMEM),
        cost_estimate=pl.CostEstimate(flops=100_000, bytes_accessed=1_000_000, transcendentals=0),
    )(emb)


def packed(main, rest, n):
    for rows, cols, place in PIECES:
        main[:n, ROWS:, place] = rest[:n, rows, cols]
    return main[:n]


def pair_kernel(temp_ref, bias_ref, place_ref, images_ref, *refs):
    text_refs = refs[:4]
    core_out, image_out, text_out = refs[4:7]
    texts, image_rest, coeff_ref, rest, main = refs[7:]
    n_images, far = images_ref.shape[0], text_refs[0].shape[0]
    rest[:, ROWS:, :] = jnp.zeros((n_images, STEP, REST), jnp.float32)

    def gather_rest(ref):
        n = ref.shape[0]
        for rows, cols, place in PIECES:
            rest[:n, rows, cols] = ref[:, ROWS:, place].astype(jnp.float32)
        return rest[:n].reshape(n * TALL, REST).astype(jnp.bfloat16)

    for i, ref in enumerate(text_refs):
        span = pl.ds(i * far * TALL, far * TALL)
        texts[span, :MAIN] = ref[...].reshape(far * TALL, MAIN)
        texts[span, MAIN:] = gather_rest(ref)
    image_rest[...] = gather_rest(images_ref)
    image_main = images_ref[...].reshape(n_images * TALL, MAIN)

    def dot(a, b, dims):
        return lax.dot_general(
            a, b, ((dims[:1], dims[1:]), ((), ())), preferred_element_type=jnp.float32
        )

    scale = jnp.exp(jnp.full((1, 1), temp_ref[0], jnp.float32))
    logits = dot(image_main, texts[:, :MAIN], (1, 1)) + dot(image_rest[...], texts[:, MAIN:], (1, 1))
    logits = scale * logits + bias_ref[0]
    x, core, y = place_ref[0] // 8, place_ref[0] // 4 % 2, place_ref[0] % 4
    z = place_ref[1]
    row = lax.broadcasted_iota(jnp.int32, logits.shape, 0)
    col = lax.broadcasted_iota(jnp.int32, logits.shape, 1)
    real = (row % TALL < ROWS) & (col % TALL < ROWS)
    same = (row == col + place_ref[0] * TALL) & (col < TALL)
    sig = jax.nn.sigmoid(jnp.where(same, -logits, logits))
    coeff_ref[...] = jnp.where(real, jnp.where(same, -sig, sig) * scale, 0.0).astype(jnp.bfloat16)
    coeff = coeff_ref[...]

    main[...] = dot(coeff, texts[:, :MAIN], (1, 0)).reshape(n_images, TALL, MAIN)
    rest[...] = dot(coeff, texts[:, MAIN:], (1, 0)).reshape(n_images, TALL, REST)
    packed(main, rest, n_images)
    for dy in range(4):
        for dx in range(4):
            spot = (x + dx) % 4 * 8 + (y + dy) % 4
            core_out[dy * 4 + dx] = main[spot + (1 - core) * 4].astype(jnp.bfloat16)
            image_out[dy * 4 + dx] = main[spot + core * 4]

    n = 4 * far
    main[:n] = dot(coeff, image_main, (0, 0)).reshape(n, TALL, MAIN)
    rest[:n] = dot(coeff, image_rest[...], (0, 0)).reshape(n, TALL, REST)
    packed(main, rest, n)
    for i, near in enumerate(near_moves(z)):
        for j, by in enumerate(FAR):
            source = (z - near - by + 32) % 16
            text_out[line_place(source)] = main[i * far + j].astype(jnp.bfloat16)


def pair_terms(log_temp, bias, place, images, texts):
    n_images, n_texts = images.shape[0], 4 * texts[0].shape[0]
    return pl.pallas_call(
        pair_kernel,
        in_specs=[pl.BlockSpec(memory_space=pltpu.SMEM)] * 3
        + [pl.BlockSpec(memory_space=pltpu.VMEM)] * 5,
        out_shape=[
            jax.ShapeDtypeStruct((n_images // 2, TALL, MAIN), jnp.bfloat16),
            jax.ShapeDtypeStruct((n_images // 2, TALL, MAIN), jnp.float32),
            jax.ShapeDtypeStruct((n_texts, TALL, MAIN), jnp.bfloat16),
        ],
        scratch_shapes=[
            pltpu.VMEM((n_texts * TALL, WIDTH), jnp.bfloat16),
            pltpu.VMEM((n_images * TALL, REST), jnp.bfloat16),
            pltpu.VMEM((n_images * TALL, n_texts * TALL), jnp.bfloat16),
            pltpu.VMEM((n_images, TALL, REST), jnp.float32),
            pltpu.VMEM((n_images, TALL, MAIN), jnp.float32),
        ],
        compiler_params=pltpu.CompilerParams(vmem_limit_bytes=VMEM),
        cost_estimate=pl.CostEstimate(
            flops=900_000_000, bytes_accessed=4_000_000, transcendentals=131_072
        ),
    )(log_temp, bias, place, images, *texts)


def finish_kernel(unit_ref, inverse_ref, *refs):
    back_refs, (out_ref, block) = refs[:-2], refs[-2:]
    total = sum(jnp.sum(ref[...].astype(jnp.float32), axis=0) for ref in back_refs)
    block[:, :MAIN] = total[:ROWS]
    for rows, cols, place in PIECES:
        block[rows, MAIN + cols.start : MAIN + cols.stop] = total[ROWS:, place]
    unit = unit_ref[...]
    direction = block[...]
    along = jnp.sum(unit * direction, axis=1, keepdims=True)
    out_ref[...] = (direction - unit * along) * inverse_ref[...]


def finish(unit, inverse, *back):
    return pl.pallas_call(
        finish_kernel,
        out_shape=jax.ShapeDtypeStruct(unit.shape, jnp.float32),
        scratch_shapes=[pltpu.VMEM((ROWS, WIDTH), jnp.float32)],
        compiler_params=pltpu.CompilerParams(vmem_limit_bytes=VMEM),
        cost_estimate=pl.CostEstimate(flops=500_000, bytes_accessed=1_000_000, transcendentals=0),
    )(unit, inverse, *back)


def line_place(z):
    return (z // 4 % 2) * 8 + (z % 4) * 2 + z // 8


def near_moves(z):
    return (0, 1, -1, 2 - 4 * (z % 2))


def along_z(value, move):
    pairs = [(line_place(z), line_place((z + move(z)) % 16)) for z in range(16)]
    return lax.ppermute(value, LINE, pairs)


def around(value, axis, by):
    n = lax.axis_size(axis)
    return lax.ppermute(value, axis, [(i, (i + by) % n) for i in range(n)])


def on_device(image_embeds, text_embeds, log_temp, bias):
    z = lax.axis_index("zh") * 8 + lax.axis_index("zm") * 4 + lax.axis_index("zn")
    place = jnp.stack([lax.axis_index(PLANE), z]).astype(jnp.int32)
    sent, img_unit, img_inv = spread(image_embeds, lax.axis_size(PLANE))
    own, txt_unit, txt_inv = spread(text_embeds, 1)

    images = lax.all_to_all(sent, PLANE, 0, 0)
    own = jnp.concatenate([own] + [along_z(own, lambda z, by=by: by) for by in FAR[1:]], axis=0)
    texts = [own] + [along_z(own, lambda z, i=i: near_moves(z)[i]) for i in (1, 2, 3)]

    core_part, part, text_part = pair_terms(log_temp, bias, place, images, texts)
    text_back = lax.all_to_all(text_part, LINE, 0, 0)
    part = part + around(core_part, "core", 1).astype(jnp.float32)
    part = part.reshape((4, 4) + part.shape[1:])
    part = part[0] + sum(
        around(part[by].astype(jnp.bfloat16), "y", by).astype(jnp.float32) for by in (2, 1, 3)
    )
    image_back = jnp.stack([part[0]] + [around(part[by], "x", by) for by in (1, 3, 2)], axis=0)
    return (
        finish(img_unit, img_inv, image_back),
        finish(txt_unit, txt_inv, text_back),
    )


def solution(mesh):
    fine = Mesh(mesh.devices.reshape(SIZES), AXES)
    split = P(AXES, None)
    return jax.shard_map(
        on_device,
        mesh=fine,
        in_specs=(split, split, P(), P()),
        out_specs=(split, split),
        check_vma=False,
    )
```
